32 devices in a mesh: fsdp: 4 (over y, core), ctx: 4 (over z), tp: 2 (over x).
Axes of the slice: x: 2, y: 2, z: 4, core: 2. Of those that a mesh axis runs over, the one named last changes fastest.
Arguments:
- inputs: bfloat16 [4, 1024, 1536], P('fsdp', 'ctx'), may hold values from -6 to 6
- cotangent: bfloat16 [4, 1024, 1536], P('fsdp', 'ctx'), may hold values from -6 to 6
- doc_bounds: int32 [4, 2], P('fsdp'), may hold values from 1 to 1023, as said below
- attn_gain: bfloat16 [1536], P(('fsdp', 'ctx')), may hold values from 0.5 to 1.5
- w_query: bfloat16 [1536, 1536], P(('fsdp', 'ctx'), 'tp'), may hold values from -0.15625 to 0.15625
- w_key: bfloat16 [1536, 512], P(('fsdp', 'ctx'), 'tp'), may hold values from -0.15625 to 0.15625
- w_value: bfloat16 [1536, 512], P(('fsdp', 'ctx'), 'tp'), may hold values from -0.15625 to 0.15625
- w_output: bfloat16 [1536, 1536], P('tp', ('fsdp', 'ctx')), may hold values from -2.5 to 2.5
- query_gain: bfloat16 [64], P(('fsdp', 'ctx')), may hold values from 0.099609375 to 1.8984375
- key_gain: bfloat16 [64], P(('fsdp', 'ctx')), may hold values from 0.099609375 to 1.8984375
- ffn_gain: bfloat16 [1536], P(('fsdp', 'ctx')), may hold values from 0.5 to 1.5
- w_gate: bfloat16 [1536, 6912], P(('fsdp', 'ctx'), 'tp'), may hold values from -0.15625 to 0.15625
- w_up: bfloat16 [1536, 6912], P(('fsdp', 'ctx'), 'tp'), may hold values from -0.15625 to 0.15625
- w_down: bfloat16 [6912, 1536], P('tp', ('fsdp', 'ctx')), may hold values from -0.078125 to 0.078125
Outputs:
- result: bfloat16 [4, 1024, 1536], P('fsdp', 'ctx')
- grad_inputs: float32 [4, 1024, 1536], P('fsdp', 'ctx')
- grad_attn_gain: float32 [1536], P(('fsdp', 'ctx'))
- grad_query: float32 [1536, 1536], P(('fsdp', 'ctx'), 'tp')
- grad_key: float32 [1536, 512], P(('fsdp', 'ctx'), 'tp')
- grad_value: float32 [1536, 512], P(('fsdp', 'ctx'), 'tp')
- grad_output: float32 [1536, 1536], P('tp', ('fsdp', 'ctx'))
- grad_query_gain: float32 [64], P(('fsdp', 'ctx'))
- grad_key_gain: float32 [64], P(('fsdp', 'ctx'))
- grad_ffn_gain: float32 [1536], P(('fsdp', 'ctx'))
- grad_gate: float32 [1536, 6912], P(('fsdp', 'ctx'), 'tp')
- grad_up: float32 [1536, 6912], P(('fsdp', 'ctx'), 'tp')
- grad_down: float32 [6912, 1536], P('tp', ('fsdp', 'ctx'))
The draws below stay inside these ranges and needn't reach their ends.
Inputs may be any that keep to these rules, and one draw needn't show every extreme that they name: Each sequence holds three documents: the second begins at doc_bounds[s,0], one of the indices 1 to 255, the third at doc_bounds[s,1], one of the indices 1024 - 255 to 1023.
All inputs are finite; a program needn't handle non-finite values.
Results may differ from the reference program's by a relative error of at most 0.02.
Values may be sent and summed in bfloat16 or wider, within the bound.
No kernel may reach another device: no remote copies, remote signals or barrier semaphores. Data moves between devices by JAX's collectives and lax.ppermute only.
A program may use at most 192 MiB of HBM per device.

```python
import jax
import jax.numpy as jnp
from jax import lax

D = 1536
HQ = 24
HK = 8
HEAD = 64
FF = 6912
TOK_DEV = 256
SEQS = 4
LENGTH = 1024
N_CTX = 4


def draw_doc_bounds(key, part):
    first_key = jax.random.fold_in(key, 11)
    second_key = jax.random.fold_in(key, 23)
    pick_first = jax.random.randint(jax.random.fold_in(key, 31), (), 0, SEQS)
    pick_second = jax.random.randint(jax.random.fold_in(key, 37), (), 0, SEQS)
    first = jax.random.randint(first_key, (SEQS,), 1, TOK_DEV)
    second = jax.random.randint(second_key, (SEQS,), LENGTH - TOK_DEV + 1, LENGTH)
    which = jnp.arange(SEQS, dtype=jnp.int32)
    first = jnp.where(which == pick_first, 1, first)
    second = jnp.where(which == pick_second, LENGTH - 1, second)
    return jnp.stack([first, second], axis=1).astype(jnp.int32)


def block_scale(key, extent, shards, least, largest):
    level, own = 1.0, jax.random.fold_in(key, 6)
    for position, parts in shards:
        steps = jnp.exp(jax.random.uniform(jax.random.fold_in(own, position), (parts,), jnp.float32, least / len(shards), largest / len(shards)))
        level = level * jnp.repeat(steps, extent[position] // parts).reshape([-1 if axis == position else 1 for axis in range(len(extent))])
    return level


def normal_values(stream_key, extent, spread, limit, shards=(), held_as=jnp.bfloat16):
    level = block_scale(stream_key, extent, shards, -0.22, 0.18) if shards else 1.0
    drawn = jax.random.normal(stream_key, extent, jnp.float32) * spread * level
    return jnp.minimum(jnp.maximum(drawn, -limit), limit).astype(held_as)


def setup_inputs(seed: int = 0) -> dict:
    splits = jax.random.split(jax.random.key(seed), 15)
    return {
        "inputs": normal_values(splits[0], (SEQS, LENGTH, D), 1.0, 6.0, ((0, 4), (1, 4))),
        "cotangent": normal_values(splits[1], (SEQS, LENGTH, D), 1.0, 6.0, ((0, 4), (1, 4))),
        "doc_bounds": draw_doc_bounds(jax.random.fold_in(splits[14], 71), 0),
        "attn_gain": jnp.clip(1.0 + 0.1 * jax.random.normal(splits[3], (D,), jnp.float32), 0.5, 1.5).astype(jnp.bfloat16),
        "w_query": normal_values(splits[4], (D, HQ * HEAD), D ** -0.5, 0.15625, ((0, 16), (1, 2))),
        "w_key": normal_values(splits[5], (D, HK * HEAD), D ** -0.5, 0.15625, ((0, 16), (1, 2))),
        "w_value": normal_values(splits[6], (D, HK * HEAD), D ** -0.5, 0.15625, ((0, 16), (1, 2))),
        "w_output": normal_values(splits[7], (HQ * HEAD, D), (((TOK_DEV * N_CTX) / 4) ** 0.5 / (HQ * HEAD) ** 0.5), 2.5, ((0, 2), (1, 16))),
        "query_gain": jnp.clip(1.0 + 0.18 * jax.random.normal(splits[8], (HEAD,), jnp.float32), 0.099609375, 1.8984375).astype(jnp.bfloat16),
        "key_gain": jnp.clip(1.0 + 0.18 * jax.random.normal(splits[9], (HEAD,), jnp.float32), 0.099609375, 1.8984375).astype(jnp.bfloat16),
        "ffn_gain": jnp.clip(1.0 + 0.1 * jax.random.normal(splits[10], (D,), jnp.float32), 0.5, 1.5).astype(jnp.bfloat16),
        "w_gate": normal_values(splits[11], (D, FF), D ** -0.5, 0.15625, ((0, 16), (1, 2))),
        "w_up": normal_values(splits[12], (D, FF), D ** -0.5, 0.15625, ((0, 16), (1, 2))),
        "w_down": normal_values(splits[13], (FF, D), FF ** -0.5, 0.078125, ((0, 2), (1, 16))),
    }


EPS = 1e-05
THETA = 1000000.0
NEG = -1e+30
HIGH = lax.Precision.HIGHEST

@jax.custom_vjp
def low(v):
    return lax.optimization_barrier(v.astype(jnp.bfloat16)).astype(jnp.float32)

@jax.custom_vjp
def low_back(v):
    return v

def low_keep(v):
    return (low(v), None)

def low_pass(kept, grad):
    return (grad,)

def back_keep(v):
    return (v, None)

def back_low(kept, grad):
    return (low(grad),)
low.defvjp(low_keep, low_pass)
low_back.defvjp(back_keep, back_low)

def matmul(left, right):
    return jnp.dot(left, right, precision=HIGH, preferred_element_type=jnp.float32)

def inverse_rms(values):
    return lax.rsqrt(lax.optimization_barrier(jnp.mean(values * values, axis=-1, keepdims=True)) + EPS)

def rotate(values, cosine, sine):
    half = values.shape[-1] // 2
    front = values[..., :half]
    back = values[..., half:]
    return jnp.concatenate([front * cosine - back * sine, back * cosine + front * sine], axis=-1)

def positions(bounds, count):
    index = jnp.arange(count, dtype=jnp.int32)
    docs = (index >= bounds[0]).astype(jnp.int32) + (index >= bounds[1]).astype(jnp.int32)
    begin = jnp.where(index >= bounds[1], bounds[1], jnp.where(index >= bounds[0], bounds[0], 0))
    return (index, docs, index - begin)

def tables(where_in):
    freq = THETA ** (-(jnp.arange(HEAD // 2, dtype=jnp.float32) * 2.0 / HEAD))
    angle = where_in.astype(jnp.float32)[:, None] * freq[None, :]
    return (jnp.cos(angle)[:, None, :], jnp.sin(angle)[:, None, :])

def attend(queries, keys, values, index, docs):
    count = queries.shape[0]
    block = min(512, count)
    starts = jnp.arange(count // block, dtype=jnp.int32) * block

    def one_block(start):
        rows = lax.dynamic_slice_in_dim(queries, start, block, 0)
        row_index = lax.dynamic_slice_in_dim(index, start, block, 0)
        row_docs = lax.dynamic_slice_in_dim(docs, start, block, 0)
        scores = low_back(jnp.einsum('qkge,tke->kgqt', rows, keys, precision=HIGH) * HEAD ** (-0.5))
        allowed = (index[None, :] <= row_index[:, None]) & (docs[None, :] == row_docs[:, None])
        scores = jnp.where(allowed, scores, NEG)
        scores = scores - lax.optimization_barrier(jnp.max(scores, axis=-1, keepdims=True))
        weights = jnp.exp(scores)
        probs = weights / lax.optimization_barrier(jnp.sum(weights, axis=-1, keepdims=True))
        return jnp.einsum('kgqt,tke->qkge', low(probs), values, precision=HIGH)
    mixed = lax.map(jax.checkpoint(one_block), starts)
    return mixed.reshape(count, HQ * HEAD)

def forward(params, tokens, bounds):
    gain_attn, w_query, w_key, w_value, w_output, gain_query, gain_key, gain_ffn, w_gate, w_up, w_down = params
    count = tokens.shape[0]
    groups = HQ // HK
    index, docs, where_in = positions(bounds, count)
    cosine, sine = tables(where_in)
    first_inv = inverse_rms(tokens)
    normed = low(tokens * first_inv * gain_attn)
    queries = low_back(matmul(normed, w_query)).reshape(count, HQ, HEAD)
    keys = low_back(matmul(normed, w_key)).reshape(count, HK, HEAD)
    values = low(low_back(matmul(normed, w_value))).reshape(count, HK, HEAD)
    queries = queries * inverse_rms(queries) * gain_query
    keys = keys * inverse_rms(keys) * gain_key
    queries = low(rotate(queries, cosine, sine)).reshape(count, HK, groups, HEAD)
    keys = low(rotate(keys, cosine, sine))
    mixed = low(low_back(attend(queries, keys, values, index, docs)))
    branch = low_back(matmul(mixed, w_output))
    hidden = tokens + branch
    second_inv = inverse_rms(hidden)
    hidden_normed = low(hidden * second_inv * gain_ffn)
    gate = low_back(matmul(hidden_normed, w_gate))
    upward = low_back(matmul(hidden_normed, w_up))
    middle = low(jax.nn.silu(gate) * upward)
    return hidden + matmul(middle, w_down)

def reference(inputs, cotangent, doc_bounds, attn_gain, w_query, w_key, w_value, w_output, query_gain, key_gain, ffn_gain, w_gate, w_up, w_down):
    params = tuple((weight.astype(jnp.float32) for weight in (attn_gain, w_query, w_key, w_value, w_output, query_gain, key_gain, ffn_gain, w_gate, w_up, w_down)))

    def one_sequence(totals, item):
        tokens, pulled, bounds = item

        def apply(weights, sequence):
            return forward(weights, sequence, bounds)
        output, backward = jax.vjp(apply, params, tokens)
        grad_params, grad_tokens = backward(pulled)
        totals = jax.tree.map(lambda left, right: left + right, totals, grad_params)
        return (totals, (output.astype(jnp.bfloat16), grad_tokens))
    zeros = jax.tree.map(jnp.zeros_like, params)
    totals, (result, grad_inputs) = lax.scan(one_sequence, zeros, (inputs.astype(jnp.float32), cotangent.astype(jnp.float32), doc_bounds))
    return (result, grad_inputs, totals[0], totals[1], totals[2], totals[3], totals[4], totals[5], totals[6], totals[7], totals[8], totals[9], totals[10])
```

```python
import jax
import jax.numpy as jnp
from jax import lax
from jax.sharding import PartitionSpec as P

HQ = 24
HK = 8
HEAD = 64


EPS = 1e-05
THETA = 1000000.0
NEG = -1e30
LINE = 4


def inverse_rms(values):
    return lax.rsqrt(jnp.mean(values * values, axis=-1, keepdims=True) + EPS)


def rotate(values, cosine, sine):
    half = values.shape[-1] // 2
    front = values[..., :half]
    back = values[..., half:]
    return jnp.concatenate([front * cosine - back * sine, back * cosine + front * sine], axis=-1)


def unrotate(grads, cosine, sine):
    half = grads.shape[-1] // 2
    front = grads[..., :half]
    back = grads[..., half:]
    return jnp.concatenate([front * cosine + back * sine, back * cosine - front * sine], axis=-1)


def norm_back(values, inverse, gain, grads):
    scaled = grads * gain
    return inverse * scaled - values * (inverse * inverse * inverse) * jnp.mean(
        scaled * values, axis=-1, keepdims=True
    )


def contract_rows(left, right):
    return lax.dot_general(
        left, right, (((0,), (0,)), ((), ())), preferred_element_type=jnp.float32
    )


def contract_cols(left, right):
    return lax.dot_general(
        left, right, (((1,), (1,)), ((), ())), preferred_element_type=jnp.float32
    )


def document(index, bounds):
    return (index >= bounds[0]).astype(jnp.int32) + (index >= bounds[1]).astype(jnp.int32)


def doc_position(index, bounds):
    begin = jnp.where(index >= bounds[1], bounds[1], jnp.where(index >= bounds[0], bounds[0], 0))
    return index - begin


def tables(where_in):
    freq = THETA ** (-(jnp.arange(HEAD // 2, dtype=jnp.float32) * 2.0 / HEAD))
    angle = where_in.astype(jnp.float32)[:, None] * freq[None, :]
    return (jnp.cos(angle)[:, None, :], jnp.sin(angle)[:, None, :])


def keep_state(current):
    return current


def pick(stack, index, axis=0):
    return lax.dynamic_index_in_dim(stack, index, axis, keepdims=False)


def place(stack, part, index, axis=0):
    return lax.dynamic_update_index_in_dim(stack, part, index, axis)


def flip(part, bit):
    size = lax.axis_size("fsdp")
    return lax.ppermute(part, "fsdp", [(i, i ^ bit) for i in range(size)])


def swap(part):
    return lax.ppermute(part, "tp", [(0, 1), (1, 0)])


def line_gather(part, both=True, axis=0):
    size = lax.axis_size("ctx")
    if size > LINE:
        return lax.all_gather(part, "ctx", axis=axis)
    me = lax.axis_index("ctx")
    rights = [part]
    lefts = [part]
    for step in range(1, size):
        rights.append(
            lax.ppermute(rights[-1], "ctx", [(i, i + 1) for i in range(step - 1, size - 1)])
        )
        if both:
            lefts.append(
                lax.ppermute(lefts[-1], "ctx", [(i, i - 1) for i in range(1, size - step + 1)])
            )
    shape = part.shape[:axis] + (size,) + part.shape[axis:]
    whole = place(jnp.zeros(shape, part.dtype), part, me, axis)
    for step in range(1, size):
        other = lefts[size - step] if both else jnp.zeros_like(part)
        block = jnp.where(me >= step, rights[step], other)
        whole = place(whole, block, lax.rem(me - step + size, size), axis)
    return whole


def line_scatter(take, both=True):
    size = lax.axis_size("ctx")
    me = lax.axis_index("ctx")
    low = jnp.bfloat16

    def term(index):
        return take(jnp.clip(index, 0, size - 1)).astype(jnp.float32)

    from_left = None
    from_right = None
    for step in range(1, size):
        ahead = size - step
        if both:
            send = term(me + ahead)
            if from_left is not None:
                send = send + from_left.astype(jnp.float32)
            from_left = lax.ppermute(
                send.astype(low), "ctx", [(i, i + 1) for i in range(0, size - ahead)]
            )
        send = term(me - ahead)
        if from_right is not None:
            send = send + from_right.astype(jnp.float32)
        from_right = lax.ppermute(
            send.astype(low), "ctx", [(i, i - 1) for i in range(ahead, size)]
        )
    total = term(me) + from_right.astype(jnp.float32)
    if both:
        total = total + from_left.astype(jnp.float32)
    return total


def group_gather(part):
    me = lax.axis_index("fsdp")
    across = flip(part, 2)
    beside = flip(part, 1)
    corner = flip(across, 1)
    whole = jnp.zeros((lax.axis_size("fsdp"),) + part.shape, part.dtype)
    whole = place(whole, part, me)
    whole = place(whole, across, me ^ 2)
    whole = place(whole, beside, me ^ 1)
    return place(whole, corner, me ^ 3)


def group_scatter(terms):
    me = lax.axis_index("fsdp")
    far = pick(terms, me ^ 2).astype(jnp.float32) + flip(pick(terms, me ^ 3), 1).astype(
        jnp.float32
    )
    near = pick(terms, me).astype(jnp.float32) + flip(pick(terms, me ^ 1), 1).astype(jnp.float32)
    return near + flip(far.astype(jnp.bfloat16), 2).astype(jnp.float32)


def group_trade(parts):
    me = lax.axis_index("fsdp")
    whole = place(jnp.zeros_like(parts), pick(parts, me), me)
    for bit in (1, 2, 3):
        whole = place(whole, flip(pick(parts, me ^ bit), bit), me ^ bit)
    return whole


def gather_all(part):
    return group_gather(line_gather(part))


def scatter_all(terms):
    size = lax.axis_size("ctx")
    parts = lax.axis_size("fsdp")
    low = jnp.bfloat16
    own = group_scatter(terms.reshape(parts, size, -1, terms.shape[-1])).astype(low)
    if size > LINE:
        return lax.psum_scatter(own, "ctx", scatter_dimension=0, tiled=False).astype(jnp.float32)
    return line_scatter(lambda index: pick(own, index))


def scatter_hidden(terms):
    size = lax.axis_size("ctx")
    parts = lax.axis_size("fsdp")
    width = terms.shape[-1]
    blocks = terms.reshape(parts, size, -1, width)
    if size > LINE:
        own = lax.psum_scatter(blocks, "ctx", scatter_dimension=1, tiled=False)
    else:
        own = line_scatter(lambda index: pick(blocks, index, 1)).astype(jnp.bfloat16)
    traded = group_trade(own)
    return jnp.concatenate([traded[i] for i in range(parts)], axis=-1).astype(jnp.float32)


def body(
    inputs,
    cotangent,
    doc_bounds,
    attn_gain,
    w_query,
    w_key,
    w_value,
    w_output,
    query_gain,
    key_gain,
    ffn_gain,
    w_gate,
    w_up,
    w_down,
):
    parts = lax.axis_size("fsdp")
    size = lax.axis_size("ctx")
    tensor = lax.axis_size("tp")
    me = lax.axis_index("ctx")
    low = jnp.bfloat16
    share = w_query.shape[0]
    model = share * parts * size
    query_heads = HQ // tensor
    key_heads = HK // tensor
    groups = HQ // HK
    kv_width = key_heads * HEAD
    small = query_gain.shape[0]

    gains = jnp.concatenate([attn_gain, ffn_gain, query_gain, key_gain])
    pad = 16
    gain_rows = jnp.zeros((pad, 2 * kv_width), low).at[0, : gains.shape[0]].set(gains)
    kv_block = jnp.concatenate(
        [jnp.concatenate([w_key, w_value], axis=1), gain_rows], axis=0
    )
    whole_kv = gather_all(kv_block)
    full_kv = whole_kv[:, :, :share].reshape(model, 2 * kv_width)
    all_gains = whole_kv[:, :, share].reshape(parts * size, 2 * kv_width).astype(jnp.float32)
    gain_attn = all_gains[:, :share].reshape(model)
    gain_ffn = all_gains[:, share : 2 * share].reshape(model)
    gain_query = all_gains[:, 2 * share : 2 * share + small].reshape(HEAD)
    gain_key = all_gains[:, 2 * share + small : 2 * share + 2 * small].reshape(HEAD)
    full_query = gather_all(w_query).reshape(model, query_heads * HEAD)
    full_output = gather_all(w_output.T).reshape(model, query_heads * HEAD)

    hidden_part = w_gate.shape[1] // parts
    stacked = jnp.stack([w_gate, w_up, w_down.T]).reshape(3, share, parts, hidden_part)
    traded = group_trade(stacked.transpose(2, 0, 1, 3))
    full_gate, full_up, full_down = (
        line_gather(traded[:, i], axis=1).reshape(model, hidden_part) for i in range(3)
    )
    pulled = cotangent[0]

    tokens = inputs[0].astype(jnp.float32)
    rows = tokens.shape[0]
    pulled_all = group_gather(pulled).reshape(parts * rows, model)
    length = rows * size
    first = me * rows
    last_row = first + rows - 1
    bounds = doc_bounds[0]
    row_index = first + jnp.arange(rows, dtype=jnp.int32)
    row_docs = document(row_index, bounds)
    cosine, sine = tables(doc_position(row_index, bounds))
    scale = HEAD ** (-0.5)
    first_inv = inverse_rms(tokens)
    normed = (tokens * first_inv * gain_attn).astype(low)
    keys_values = jnp.dot(normed, full_kv, preferred_element_type=jnp.float32)
    keys = keys_values[:, :kv_width].reshape(rows, key_heads, HEAD)
    values = keys_values[:, kv_width:].astype(low)
    key_inv = inverse_rms(keys)
    key_rot = rotate(keys * key_inv * gain_key, cosine, sine).astype(low).reshape(rows, kv_width)
    gathered = line_gather(jnp.concatenate([key_rot, values], axis=1), both=False)
    gathered = gathered.reshape(length, 2 * kv_width)
    all_keys = gathered[:, :kv_width]
    all_values = gathered[:, kv_width:]
    queries = jnp.dot(normed, full_query, preferred_element_type=jnp.float32).reshape(
        rows, query_heads, HEAD
    )
    query_inv = inverse_rms(queries)
    query_rot = (
        rotate(queries * query_inv * gain_query, cosine, sine)
        .astype(low)
        .reshape(rows, key_heads, groups, HEAD)
    )
    block = 512
    block_count = length // block
    block_ids = jnp.arange(block_count, dtype=jnp.int32)

    def block_scores(block_id):
        start = block_id * block
        key_block = lax.dynamic_slice_in_dim(all_keys, start, block, 0).reshape(
            block, key_heads, HEAD
        )
        value_block = lax.dynamic_slice_in_dim(all_values, start, block, 0).reshape(
            block, key_heads, HEAD
        )
        key_index = start + jnp.arange(block, dtype=jnp.int32)
        allowed = (key_index[None, :] <= row_index[:, None]) & (
            document(key_index, bounds)[None, :] == row_docs[:, None]
        )
        scores = (
            jnp.einsum("qkge,tke->kgqt", query_rot, key_block, preferred_element_type=jnp.float32)
            * scale
        )
        return (key_block, value_block, allowed, scores)

    def stats_step(state, block_id):

        def stats_work(current):
            top, total = current
            scores_all = block_scores(block_id)
            allowed = scores_all[2]
            scores = scores_all[3]
            new_top = jnp.maximum(top, jnp.max(jnp.where(allowed, scores, NEG), axis=-1))
            weights = jnp.where(allowed, jnp.exp(scores - new_top[..., None]), 0.0)
            return (new_top, total * jnp.exp(top - new_top) + jnp.sum(weights, axis=-1))

        return (lax.cond(block_id * block <= last_row, stats_work, keep_state, state), None)

    top_start = jnp.full((key_heads, groups, rows), NEG, jnp.float32)
    total_start = jnp.zeros((key_heads, groups, rows), jnp.float32)
    (top, total), _ = lax.scan(stats_step, (top_start, total_start), block_ids)
    log_total = top + jnp.log(total)

    def value_step(accum, block_id):

        def value_work(current):
            _, value_block, allowed, scores = block_scores(block_id)
            probs = jnp.where(allowed, jnp.exp(scores - log_total[..., None]), 0.0).astype(low)
            return current + jnp.einsum(
                "kgqt,tke->qkge", probs, value_block, preferred_element_type=jnp.float32
            )

        return (lax.cond(block_id * block <= last_row, value_work, keep_state, accum), None)

    mixed, _ = lax.scan(
        value_step, jnp.zeros((rows, key_heads, groups, HEAD), jnp.float32), block_ids
    )
    mixed_low = mixed.reshape(rows, query_heads * HEAD).astype(low)
    branch_part = contract_cols(mixed_low, full_output).astype(low)
    branch = branch_part.astype(jnp.float32) + swap(branch_part).astype(jnp.float32)
    hidden = tokens + branch
    second_inv = inverse_rms(hidden)
    hidden_normed = (hidden * second_inv * gain_ffn).astype(low)

    hidden_all = group_gather(hidden_normed).reshape(parts * rows, model)
    gate = jnp.dot(hidden_all, full_gate, preferred_element_type=jnp.float32)
    upward = jnp.dot(hidden_all, full_up, preferred_element_type=jnp.float32)
    sigma = jax.nn.sigmoid(gate)
    active = gate * sigma
    middle = (active * upward).astype(low)
    grad_down = scatter_hidden(contract_rows(pulled_all, middle).astype(low)).T
    grad_middle = jnp.dot(pulled_all, full_down, preferred_element_type=jnp.float32)
    grad_gate_low = (grad_middle * upward * sigma * (1.0 + gate * (1.0 - sigma))).astype(low)
    grad_up_low = (grad_middle * active).astype(low)
    normed_part = group_scatter(
        (contract_cols(grad_gate_low, full_gate) + contract_cols(grad_up_low, full_up))
        .astype(low)
        .reshape(parts, rows, model)
    ).astype(low)
    grad_normed_ffn = normed_part.astype(jnp.float32) + swap(normed_part).astype(jnp.float32)
    grad_gate = scatter_hidden(contract_rows(hidden_all, grad_gate_low).astype(low))
    grad_up = scatter_hidden(contract_rows(hidden_all, grad_up_low).astype(low))
    feed_part = group_scatter(
        contract_cols(middle, full_down).astype(low).reshape(parts, rows, model)
    ).astype(low)
    feed = feed_part.astype(jnp.float32) + swap(feed_part).astype(jnp.float32)
    result = (hidden + feed).astype(low)[None]

    ffn_gain_part = jnp.sum(grad_normed_ffn * hidden * second_inv, axis=0) * 0.5
    grad_hidden = pulled.astype(jnp.float32) + norm_back(
        hidden, second_inv, gain_ffn, grad_normed_ffn
    )
    grad_hidden_low = grad_hidden.astype(low)
    grad_output = scatter_all(contract_rows(grad_hidden_low, mixed_low).astype(low)).T
    grad_mixed = (
        jnp.dot(grad_hidden_low, full_output, preferred_element_type=jnp.float32)
        .astype(low)
        .reshape(rows, key_heads, groups, HEAD)
    )
    delta = jnp.einsum("qkge,qkge->kgq", grad_mixed.astype(jnp.float32), mixed)

    def grad_step(accum, block_id):

        def grad_work(current):
            key_block, value_block, allowed, scores = block_scores(block_id)
            probs = jnp.where(allowed, jnp.exp(scores - log_total[..., None]), 0.0)
            grad_value_block = jnp.einsum(
                "kgqt,qkge->tke",
                probs.astype(low),
                grad_mixed,
                preferred_element_type=jnp.float32,
            )
            grad_probs = jnp.einsum(
                "qkge,tke->kgqt", grad_mixed, value_block, preferred_element_type=jnp.float32
            )
            grad_scores = (probs * (grad_probs - delta[..., None])).astype(low)
            updated = (
                current
                + jnp.einsum(
                    "kgqt,tke->qkge", grad_scores, key_block, preferred_element_type=jnp.float32
                )
                * scale
            )
            grad_key_block = (
                jnp.einsum(
                    "kgqt,qkge->tke", grad_scores, query_rot, preferred_element_type=jnp.float32
                )
                * scale
            )
            terms = jnp.concatenate(
                [
                    grad_key_block.reshape(block, kv_width),
                    grad_value_block.reshape(block, kv_width),
                ],
                axis=1,
            )
            return (updated, terms)

        def skipped(current):
            return (current, jnp.zeros((block, 2 * kv_width), jnp.float32))

        return lax.cond(block_id * block <= last_row, grad_work, skipped, accum)

    grad_query_rot, key_terms = lax.scan(
        grad_step, jnp.zeros((rows, key_heads, groups, HEAD), jnp.float32), block_ids
    )
    key_terms = key_terms.reshape(size, rows, 2 * kv_width).astype(low)
    if size > LINE:
        own_terms = lax.psum_scatter(key_terms, "ctx", scatter_dimension=0, tiled=False).astype(
            jnp.float32
        )
    else:
        own_terms = line_scatter(lambda index: pick(key_terms, index), both=False)
    grad_query_norm = unrotate(grad_query_rot.reshape(rows, query_heads, HEAD), cosine, sine)
    query_gain_part = jnp.sum(grad_query_norm * queries * query_inv, axis=(0, 1))
    grad_query_low = (
        norm_back(queries, query_inv, gain_query, grad_query_norm)
        .astype(low)
        .reshape(rows, query_heads * HEAD)
    )
    grad_query = scatter_all(contract_rows(normed, grad_query_low).astype(low))

    grad_key_rot = own_terms[:, :kv_width].reshape(rows, key_heads, HEAD)
    grad_value_low = own_terms[:, kv_width:].astype(low)
    grad_key_norm = unrotate(grad_key_rot, cosine, sine)
    key_gain_part = jnp.sum(grad_key_norm * keys * key_inv, axis=(0, 1))
    grad_key_low = (
        norm_back(keys, key_inv, gain_key, grad_key_norm).astype(low).reshape(rows, kv_width)
    )
    grad_kv_low = jnp.concatenate([grad_key_low, grad_value_low], axis=1)
    normed_terms = contract_cols(grad_query_low, full_query) + contract_cols(grad_kv_low, full_kv)
    normed_low = normed_terms.astype(low)
    grad_normed = normed_low.astype(jnp.float32) + swap(normed_low).astype(jnp.float32)
    attn_gain_part = jnp.sum(normed_terms * tokens * first_inv, axis=0)
    shards = parts * size
    gain_parts = jnp.concatenate(
        [
            attn_gain_part.reshape(shards, share),
            ffn_gain_part.reshape(shards, share),
            query_gain_part.reshape(shards, small),
            key_gain_part.reshape(shards, small),
        ],
        axis=1,
    ).astype(low)
    width = gain_parts.shape[1]
    gain_block = jnp.zeros((shards, pad, 2 * kv_width), low).at[:, 0, :width].set(gain_parts)
    kv_terms = contract_rows(normed, grad_kv_low).astype(low).reshape(shards, share, 2 * kv_width)
    own_kv = scatter_all(
        jnp.concatenate([kv_terms, gain_block], axis=1).reshape(
            shards * (share + pad), 2 * kv_width
        )
    )
    grad_key = own_kv[:share, :kv_width]
    grad_value = own_kv[:share, kv_width:]
    own_gains = own_kv[share, :width].astype(low)
    grad_gains = own_gains.astype(jnp.float32) + swap(own_gains).astype(jnp.float32)
    grad_inputs = grad_hidden + norm_back(tokens, first_inv, gain_attn, grad_normed)
    return (
        result,
        grad_inputs[None],
        grad_gains[:share],
        grad_query,
        grad_key,
        grad_value,
        grad_output,
        grad_gains[2 * share : 2 * share + small],
        grad_gains[2 * share + small :],
        grad_gains[share : 2 * share],
        grad_gate,
        grad_up,
        grad_down,
    )


def solution(mesh):
    vector = P(("fsdp", "ctx"))
    columns = P(("fsdp", "ctx"), "tp")
    tall = P("tp", ("fsdp", "ctx"))
    act = P("fsdp", "ctx", None)
    return jax.shard_map(
        body,
        mesh=mesh,
        in_specs=(
            act,
            act,
            P("fsdp", None),
            vector,
            columns,
            columns,
            columns,
            tall,
            vector,
            vector,
            vector,
            columns,
            columns,
            tall,
        ),
        out_specs=(
            act,
            act,
            vector,
            columns,
            columns,
            columns,
            tall,
            vector,
            vector,
            vector,
            columns,
            columns,
            tall,
        ),
        check_vma=False,
    )
```

```python
import jax
import jax.numpy as jnp
from jax import lax
from jax.sharding import PartitionSpec as P

HQ = 24
HK = 8
HEAD = 64


EPS = 1e-05
THETA = 1000000.0
NEG = -1e30
LINE = 4


def inverse_rms(values):
    return lax.rsqrt(jnp.mean(values * values, axis=-1, keepdims=True) + EPS)


def rotate(values, cosine, sine):
    half = values.shape[-1] // 2
    front = values[..., :half]
    back = values[..., half:]
    return jnp.concatenate([front * cosine - back * sine, back * cosine + front * sine], axis=-1)


def unrotate(grads, cosine, sine):
    half = grads.shape[-1] // 2
    front = grads[..., :half]
    back = grads[..., half:]
    return jnp.concatenate([front * cosine + back * sine, back * cosine - front * sine], axis=-1)


def norm_back(values, inverse, gain, grads):
    scaled = grads * gain
    return inverse * scaled - values * (inverse * inverse * inverse) * jnp.mean(
        scaled * values, axis=-1, keepdims=True
    )


def contract_rows(left, right):
    return lax.dot_general(
        left, right, (((0,), (0,)), ((), ())), preferred_element_type=jnp.float32
    )


def contract_cols(left, right):
    return lax.dot_general(
        left, right, (((1,), (1,)), ((), ())), preferred_element_type=jnp.float32
    )


def document(index, bounds):
    return (index >= bounds[0]).astype(jnp.int32) + (index >= bounds[1]).astype(jnp.int32)


def doc_position(index, bounds):
    begin = jnp.where(index >= bounds[1], bounds[1], jnp.where(index >= bounds[0], bounds[0], 0))
    return index - begin


def tables(where_in):
    freq = THETA ** (-(jnp.arange(HEAD // 2, dtype=jnp.float32) * 2.0 / HEAD))
    angle = where_in.astype(jnp.float32)[:, None] * freq[None, :]
    return (jnp.cos(angle)[:, None, :], jnp.sin(angle)[:, None, :])


def keep_state(current):
    return current


def pick(stack, index, axis=0):
    return lax.dynamic_index_in_dim(stack, index, axis, keepdims=False)


def place(stack, part, index, axis=0):
    return lax.dynamic_update_index_in_dim(stack, part, index, axis)


def after(value, *others):
    return lax.optimization_barrier((value,) + others)[0]


def flip(part, bit):
    size = lax.axis_size("fsdp")
    return lax.ppermute(part, "fsdp", [(i, i ^ bit) for i in range(size)])


def swap(part):
    return lax.ppermute(part, "tp", [(0, 1), (1, 0)])


def turn(part):
    size = lax.axis_size("ctx")
    return lax.ppermute(part, "ctx", [(i, (i + 1) % size) for i in range(size)])


def ring_slots(part):
    slots = [part]
    for _ in range(1, lax.axis_size("ctx")):
        slots.append(turn(slots[-1]))
    return slots


def in_order(slots, axis=0):
    size = len(slots)
    me = lax.axis_index("ctx")
    first = slots[0]
    whole = jnp.zeros(first.shape[:axis] + (size,) + first.shape[axis:], first.dtype)
    for step, part in enumerate(slots):
        whole = place(whole, part, lax.rem(me - step + size, size), axis)
    return whole


def ring_gather(part, axis=0):
    if lax.axis_size("ctx") > LINE:
        return lax.all_gather(part, "ctx", axis=axis)
    return in_order(ring_slots(part), axis)


def ring_scatter(terms):
    size = lax.axis_size("ctx")
    if size > LINE:
        return lax.psum_scatter(terms, "ctx", scatter_dimension=0, tiled=False).astype(jnp.float32)
    me = lax.axis_index("ctx")

    def term(step):
        return pick(terms, lax.rem(me - step + size, size))

    moving = term(1)
    for step in range(1, size):
        total = turn(moving).astype(jnp.float32) + term((step + 1) % size).astype(jnp.float32)
        moving = total.astype(jnp.bfloat16)
    return total


def back_gather(part):
    size = lax.axis_size("ctx")
    if size > LINE:
        return lax.all_gather(part, "ctx", axis=0)
    slots = [part]
    for step in range(1, size):
        slots.append(lax.ppermute(part, "ctx", [(i, i + step) for i in range(size - step)]))
    return in_order(slots)


def back_scatter(terms):
    size = lax.axis_size("ctx")
    if size > LINE:
        return lax.psum_scatter(terms, "ctx", scatter_dimension=0, tiled=False).astype(jnp.float32)
    me = lax.axis_index("ctx")
    total = pick(terms, me).astype(jnp.float32)
    for step in range(1, size):
        part = pick(terms, jnp.maximum(me - step, 0))
        part = lax.ppermute(part, "ctx", [(i, i - step) for i in range(step, size)])
        total = total + part.astype(jnp.float32)
    return total


def group_slots(part):
    across = flip(part, 2)
    both = flip(jnp.stack([part, across]), 1)
    return [part, both[0], across, both[1]]


def group_order(slots):
    me = lax.axis_index("fsdp")
    whole = jnp.zeros((len(slots),) + slots[0].shape, slots[0].dtype)
    for bit, part in enumerate(slots):
        whole = place(whole, part, me ^ bit)
    return whole


def group_sum(terms):
    beside = flip(terms[1::2], 1).astype(jnp.float32)
    far = terms[2].astype(jnp.float32) + beside[1]
    near = terms[0].astype(jnp.float32) + beside[0]
    return near + flip(far.astype(jnp.bfloat16), 2).astype(jnp.float32)


def gather_all(part):
    return group_order(group_slots(ring_gather(part)))


def scatter_all(terms):
    size = lax.axis_size("ctx")
    parts = lax.axis_size("fsdp")
    me = lax.axis_index("fsdp")
    terms = terms.reshape(parts, size, -1, terms.shape[-1])
    terms = jnp.stack([pick(terms, me ^ bit) for bit in range(parts)])
    return ring_scatter(group_sum(terms).astype(jnp.bfloat16))


def scatter_hidden(terms):
    size = lax.axis_size("ctx")
    parts = lax.axis_size("fsdp")
    me = lax.axis_index("fsdp")
    count, _, width = terms.shape
    blocks = terms.reshape(count, parts, size, -1, width)
    blocks = blocks.transpose(2, 0, 1, 3, 4).reshape(-1, width)
    own = lax.psum_scatter(blocks, "ctx", scatter_dimension=0, tiled=True)
    own = own.reshape(count, parts, -1, width)
    slots = [pick(own, me, 1)] + [flip(pick(own, me ^ bit, 1), bit) for bit in range(1, parts)]
    whole = group_order(slots)
    return jnp.concatenate([whole[i] for i in range(parts)], axis=-1).astype(jnp.float32)


def body(
    inputs,
    cotangent,
    doc_bounds,
    attn_gain,
    w_query,
    w_key,
    w_value,
    w_output,
    query_gain,
    key_gain,
    ffn_gain,
    w_gate,
    w_up,
    w_down,
):
    parts = lax.axis_size("fsdp")
    size = lax.axis_size("ctx")
    tensor = lax.axis_size("tp")
    me = lax.axis_index("ctx")
    low = jnp.bfloat16
    share = w_query.shape[0]
    model = share * parts * size
    query_heads = HQ // tensor
    key_heads = HK // tensor
    groups = HQ // HK
    kv_width = key_heads * HEAD
    small = query_gain.shape[0]

    gains = jnp.concatenate([attn_gain, ffn_gain, query_gain, key_gain])
    pad = 16
    gain_rows = jnp.zeros((pad, 2 * kv_width), low).at[0, : gains.shape[0]].set(gains)
    kv_block = jnp.concatenate(
        [jnp.concatenate([w_key, w_value], axis=1), gain_rows], axis=0
    )
    whole_kv = gather_all(kv_block)
    full_kv = whole_kv[:, :, :share].reshape(model, 2 * kv_width)
    all_gains = whole_kv[:, :, share].reshape(parts * size, 2 * kv_width).astype(jnp.float32)
    gain_attn = all_gains[:, :share].reshape(model)
    gain_ffn = all_gains[:, share : 2 * share].reshape(model)
    gain_query = all_gains[:, 2 * share : 2 * share + small].reshape(HEAD)
    gain_key = all_gains[:, 2 * share + small : 2 * share + 2 * small].reshape(HEAD)
    full_query = gather_all(w_query).reshape(model, query_heads * HEAD)
    full_output = gather_all(w_output.T).reshape(model, query_heads * HEAD)

    place_in_group = lax.axis_index("fsdp")
    hidden_part = w_gate.shape[1] // parts
    stacked = jnp.stack([w_gate, w_up, w_down.T]).reshape(3, share, parts, hidden_part)
    stacked = stacked.transpose(2, 0, 1, 3)
    traded = group_order(
        [pick(stacked, place_in_group)]
        + [flip(pick(stacked, place_in_group ^ bit), bit) for bit in range(1, parts)]
    )
    gate_up = ring_gather(traded[:, :2].transpose(1, 0, 2, 3), 2).reshape(2, model, hidden_part)
    full_gate = gate_up[0]
    full_up = gate_up[1]
    full_down = ring_gather(traded[:, 2], 1).reshape(model, hidden_part)
    pulled = cotangent[0]

    tokens = inputs[0].astype(jnp.float32)
    rows = tokens.shape[0]
    pulled_all = jnp.concatenate(group_slots(pulled))
    length = rows * size
    first = me * rows
    last_row = first + rows - 1
    bounds = doc_bounds[0]
    row_index = first + jnp.arange(rows, dtype=jnp.int32)
    row_docs = document(row_index, bounds)
    cosine, sine = tables(doc_position(row_index, bounds))
    scale = HEAD ** (-0.5)
    first_inv = inverse_rms(tokens)
    normed = (tokens * first_inv * gain_attn).astype(low)
    keys_values = jnp.dot(normed, full_kv, preferred_element_type=jnp.float32)
    keys = keys_values[:, :kv_width].reshape(rows, key_heads, HEAD)
    values = keys_values[:, kv_width:].astype(low)
    key_inv = inverse_rms(keys)
    key_rot = rotate(keys * key_inv * gain_key, cosine, sine).astype(low).reshape(rows, kv_width)
    gathered = back_gather(jnp.concatenate([key_rot, values], axis=1))
    gathered = gathered.reshape(length, 2 * kv_width)
    all_keys = gathered[:, :kv_width]
    all_values = gathered[:, kv_width:]
    queries = jnp.dot(normed, full_query, preferred_element_type=jnp.float32).reshape(
        rows, query_heads, HEAD
    )
    query_inv = inverse_rms(queries)
    query_rot = (
        rotate(queries * query_inv * gain_query, cosine, sine)
        .astype(low)
        .reshape(rows, key_heads, groups, HEAD)
    )
    block = 512
    block_count = length // block
    block_ids = jnp.arange(block_count, dtype=jnp.int32)

    def block_scores(block_id):
        start = block_id * block
        key_block = lax.dynamic_slice_in_dim(all_keys, start, block, 0).reshape(
            block, key_heads, HEAD
        )
        value_block = lax.dynamic_slice_in_dim(all_values, start, block, 0).reshape(
            block, key_heads, HEAD
        )
        key_index = start + jnp.arange(block, dtype=jnp.int32)
        allowed = (key_index[None, :] <= row_index[:, None]) & (
            document(key_index, bounds)[None, :] == row_docs[:, None]
        )
        scores = (
            jnp.einsum("qkge,tke->kgqt", query_rot, key_block, preferred_element_type=jnp.float32)
            * scale
        )
        return (key_block, value_block, allowed, scores)

    def stats_step(state, block_id):

        def stats_work(current):
            top, total = current
            scores_all = block_scores(block_id)
            allowed = scores_all[2]
            scores = scores_all[3]
            new_top = jnp.maximum(top, jnp.max(jnp.where(allowed, scores, NEG), axis=-1))
            weights = jnp.where(allowed, jnp.exp(scores - new_top[..., None]), 0.0)
            return (new_top, total * jnp.exp(top - new_top) + jnp.sum(weights, axis=-1))

        return (lax.cond(block_id * block <= last_row, stats_work, keep_state, state), None)

    top_start = jnp.full((key_heads, groups, rows), NEG, jnp.float32)
    total_start = jnp.zeros((key_heads, groups, rows), jnp.float32)
    (top, total), _ = lax.scan(stats_step, (top_start, total_start), block_ids)
    log_total = top + jnp.log(total)

    def value_step(accum, block_id):

        def value_work(current):
            _, value_block, allowed, scores = block_scores(block_id)
            probs = jnp.where(allowed, jnp.exp(scores - log_total[..., None]), 0.0).astype(low)
            return current + jnp.einsum(
                "kgqt,tke->qkge", probs, value_block, preferred_element_type=jnp.float32
            )

        return (lax.cond(block_id * block <= last_row, value_work, keep_state, accum), None)

    mixed, _ = lax.scan(
        value_step, jnp.zeros((rows, key_heads, groups, HEAD), jnp.float32), block_ids
    )
    mixed_low = mixed.reshape(rows, query_heads * HEAD).astype(low)
    branch_part = contract_cols(mixed_low, full_output).astype(low)
    branch = branch_part.astype(jnp.float32) + swap(branch_part).astype(jnp.float32)
    hidden = tokens + branch
    second_inv = inverse_rms(hidden)
    hidden_normed = (hidden * second_inv * gain_ffn).astype(low)

    hidden_all = jnp.concatenate(group_slots(hidden_normed))
    gate = jnp.dot(hidden_all, full_gate, preferred_element_type=jnp.float32)
    upward = jnp.dot(hidden_all, full_up, preferred_element_type=jnp.float32)
    sigma = jax.nn.sigmoid(gate)
    active = gate * sigma
    middle = (active * upward).astype(low)
    grad_down = scatter_hidden(contract_rows(pulled_all, middle).astype(low)[None])[0].T
    grad_middle = jnp.dot(pulled_all, full_down, preferred_element_type=jnp.float32)
    grad_gate_low = (grad_middle * upward * sigma * (1.0 + gate * (1.0 - sigma))).astype(low)
    grad_up_low = (grad_middle * active).astype(low)
    normed_part = group_sum(
        (contract_cols(grad_gate_low, full_gate) + contract_cols(grad_up_low, full_up))
        .astype(low)
        .reshape(parts, rows, model)
    ).astype(low)
    grad_normed_ffn = normed_part.astype(jnp.float32) + swap(normed_part).astype(jnp.float32)
    grad_gate, grad_up = scatter_hidden(
        jnp.stack(
            [
                contract_rows(hidden_all, grad_gate_low).astype(low),
                contract_rows(hidden_all, grad_up_low).astype(low),
            ]
        )
    )
    feed_part = group_sum(
        contract_cols(middle, full_down).astype(low).reshape(parts, rows, model)
    ).astype(low)
    feed = feed_part.astype(jnp.float32) + swap(feed_part).astype(jnp.float32)
    result = (hidden + feed).astype(low)[None]

    ffn_gain_part = jnp.sum(grad_normed_ffn * hidden * second_inv, axis=0) * 0.5
    grad_hidden = pulled.astype(jnp.float32) + norm_back(
        hidden, second_inv, gain_ffn, grad_normed_ffn
    )
    grad_hidden_low = grad_hidden.astype(low)
    grad_output = scatter_all(contract_rows(grad_hidden_low, mixed_low).astype(low)).T
    grad_mixed = (
        jnp.dot(grad_hidden_low, full_output, preferred_element_type=jnp.float32)
        .astype(low)
        .reshape(rows, key_heads, groups, HEAD)
    )
    delta = jnp.einsum("qkge,qkge->kgq", grad_mixed.astype(jnp.float32), mixed)

    def grad_step(accum, block_id):

        def grad_work(current):
            key_block, value_block, allowed, scores = block_scores(block_id)
            probs = jnp.where(allowed, jnp.exp(scores - log_total[..., None]), 0.0)
            grad_value_block = jnp.einsum(
                "kgqt,qkge->tke",
                probs.astype(low),
                grad_mixed,
                preferred_element_type=jnp.float32,
            )
            grad_probs = jnp.einsum(
                "qkge,tke->kgqt", grad_mixed, value_block, preferred_element_type=jnp.float32
            )
            grad_scores = (probs * (grad_probs - delta[..., None])).astype(low)
            updated = (
                current
                + jnp.einsum(
                    "kgqt,tke->qkge", grad_scores, key_block, preferred_element_type=jnp.float32
                )
                * scale
            )
            grad_key_block = (
                jnp.einsum(
                    "kgqt,qkge->tke", grad_scores, query_rot, preferred_element_type=jnp.float32
                )
                * scale
            )
            terms = jnp.concatenate(
                [
                    grad_key_block.reshape(block, kv_width),
                    grad_value_block.reshape(block, kv_width),
                ],
                axis=1,
            )
            return (updated, terms)

        def skipped(current):
            return (current, jnp.zeros((block, 2 * kv_width), jnp.float32))

        return lax.cond(block_id * block <= last_row, grad_work, skipped, accum)

    grad_query_rot, key_terms = lax.scan(
        grad_step, jnp.zeros((rows, key_heads, groups, HEAD), jnp.float32), block_ids
    )
    key_terms = key_terms.reshape(size, rows, 2 * kv_width).astype(low)
    own_terms = back_scatter(key_terms)
    grad_query_norm = unrotate(grad_query_rot.reshape(rows, query_heads, HEAD), cosine, sine)
    query_gain_part = jnp.sum(grad_query_norm * queries * query_inv, axis=(0, 1))
    grad_query_low = (
        norm_back(queries, query_inv, gain_query, grad_query_norm)
        .astype(low)
        .reshape(rows, query_heads * HEAD)
    )
    grad_query = scatter_all(contract_rows(normed, grad_query_low).astype(low))

    grad_key_rot = own_terms[:, :kv_width].reshape(rows, key_heads, HEAD)
    grad_value_low = own_terms[:, kv_width:].astype(low)
    grad_key_norm = unrotate(grad_key_rot, cosine, sine)
    key_gain_part = jnp.sum(grad_key_norm * keys * key_inv, axis=(0, 1))
    grad_key_low = (
        norm_back(keys, key_inv, gain_key, grad_key_norm).astype(low).reshape(rows, kv_width)
    )
    grad_kv_low = jnp.concatenate([grad_key_low, grad_value_low], axis=1)
    normed_terms = contract_cols(grad_query_low, full_query) + contract_cols(grad_kv_low, full_kv)
    normed_low = normed_terms.astype(low)
    grad_normed = normed_low.astype(jnp.float32) + swap(normed_low).astype(jnp.float32)
    attn_gain_part = jnp.sum(normed_terms * tokens * first_inv, axis=0)
    shards = parts * size
    gain_parts = jnp.concatenate(
        [
            attn_gain_part.reshape(shards, share),
            ffn_gain_part.reshape(shards, share),
            query_gain_part.reshape(shards, small),
            key_gain_part.reshape(shards, small),
        ],
        axis=1,
    ).astype(low)
    width = gain_parts.shape[1]
    gain_block = jnp.zeros((shards, pad, 2 * kv_width), low).at[:, 0, :width].set(gain_parts)
    kv_terms = contract_rows(normed, grad_kv_low).astype(low).reshape(shards, share, 2 * kv_width)
    own_kv = scatter_all(
        jnp.concatenate([kv_terms, gain_block], axis=1).reshape(
            shards * (share + pad), 2 * kv_width
        )
    )
    grad_key = own_kv[:share, :kv_width]
    grad_value = own_kv[:share, kv_width:]
    own_gains = own_kv[share, :width].astype(low)
    grad_gains = own_gains.astype(jnp.float32) + swap(own_gains).astype(jnp.float32)
    grad_inputs = grad_hidden + norm_back(tokens, first_inv, gain_attn, grad_normed)
    return (
        result,
        grad_inputs[None],
        grad_gains[:share],
        grad_query,
        grad_key,
        grad_value,
        grad_output,
        grad_gains[2 * share : 2 * share + small],
        grad_gains[2 * share + small :],
        grad_gains[share : 2 * share],
        grad_gate,
        grad_up,
        grad_down,
    )


def solution(mesh):
    vector = P(("fsdp", "ctx"))
    columns = P(("fsdp", "ctx"), "tp")
    tall = P("tp", ("fsdp", "ctx"))
    act = P("fsdp", "ctx", None)
    return jax.shard_map(
        body,
        mesh=mesh,
        in_specs=(
            act,
            act,
            P("fsdp", None),
            vector,
            columns,
            columns,
            columns,
            tall,
            vector,
            vector,
            vector,
            columns,
            columns,
            tall,
        ),
        out_specs=(
            act,
            act,
            vector,
            columns,
            columns,
            columns,
            tall,
            vector,
            vector,
            vector,
            columns,
            columns,
            tall,
        ),
        check_vma=False,
    )
```

```python
import functools
import math

import jax
import jax.numpy as jnp
from jax import lax
from jax.experimental import pallas as pl
from jax.experimental.pallas import tpu as pltpu
from jax.sharding import PartitionSpec as P

HQ = 24
HK = 8
HEAD = 64
GROUP = HQ // HK


EPS = 1e-05
THETA = 1000000.0
LINE = 4
LOG2E = math.log2(math.e)
LOW = jnp.bfloat16
VMEM = pl.BlockSpec(memory_space=pltpu.VMEM)
SMEM = pl.BlockSpec(memory_space=pltpu.SMEM)
ANY = pl.BlockSpec(memory_space=pl.ANY)
PARAMS = pltpu.CompilerParams(vmem_limit_bytes=52 * 1024 * 1024)


def inverse_rms(values):
    return lax.rsqrt(jnp.mean(values * values, axis=-1, keepdims=True) + EPS)


def norm_back(values, inverse, gain, grads):
    scaled = grads * gain
    return inverse * scaled - values * (inverse * inverse * inverse) * jnp.mean(
        scaled * values, axis=-1, keepdims=True
    )


def contract_rows(left, right):
    return lax.dot_general(
        left, right, (((0,), (0,)), ((), ())), preferred_element_type=jnp.float32
    )


def contract_cols(left, right):
    return lax.dot_general(
        left, right, (((1,), (1,)), ((), ())), preferred_element_type=jnp.float32
    )


def tables(first, rows, bounds):
    index = first + jnp.arange(rows, dtype=jnp.int32)
    begin = jnp.where(index >= bounds[1], bounds[1], jnp.where(index >= bounds[0], bounds[0], 0))
    freq = THETA ** (-(jnp.arange(HEAD // 2, dtype=jnp.float32) * 2.0 / HEAD))
    angle = (index - begin).astype(jnp.float32)[:, None] * freq[None, :]
    cosine = jnp.cos(angle)
    sine = jnp.sin(angle)
    return (
        jnp.concatenate([cosine, cosine, cosine, cosine], axis=1),
        jnp.concatenate([-sine, sine, -sine, sine], axis=1),
    )


def shaped(shape, dtype=LOW):
    return jax.ShapeDtypeStruct(shape, dtype)


def cost(micros):
    return pl.CostEstimate(
        flops=int(micros * 9e8), bytes_accessed=int(micros * 1e6), transcendentals=0
    )


def pair_inverse(x):
    lane=lax.broadcasted_iota(jnp.int32,x.shape,1)
    left=lane<HEAD
    sq=x*x
    a=jnp.sum(jnp.where(left,sq,0.0),axis=-1,keepdims=True)
    b=jnp.sum(jnp.where(left,0.0,sq),axis=-1,keepdims=True)
    return lax.rsqrt(jnp.where(left,a,b)*(1.0/HEAD)+EPS)

def pair_mean(x):
    lane=lax.broadcasted_iota(jnp.int32,x.shape,1)
    left=lane<HEAD
    a=jnp.sum(jnp.where(left,x,0.0),axis=-1,keepdims=True)
    b=jnp.sum(jnp.where(left,0.0,x),axis=-1,keepdims=True)
    return jnp.where(left,a,b)*(1.0/HEAD)

def partner(x):
    lane=lax.broadcasted_iota(jnp.int32,x.shape,1)
    front=lax.rem(lane,HEAD)<HEAD//2
    return jnp.where(front,pltpu.roll(x,2*HEAD-HEAD//2,1),pltpu.roll(x,HEAD//2,1))

def kprep_kernel(kv_ref,gain_ref,cos_ref,sin_ref,out_ref):
    width=kv_ref.shape[1]//2
    for i in range(width//128):
        x=kv_ref[:,128*i:128*(i+1)]
        xn=x*pair_inverse(x)*gain_ref[...]
        out_ref[:,128*i:128*(i+1)]=(xn*cos_ref[...]+partner(xn)*sin_ref[...]).astype(jnp.bfloat16)
    out_ref[:,width:]=kv_ref[:,width:].astype(jnp.bfloat16)

def bias_of(first_key,first_row,bounds_ref,keys,rows):
    key=first_key+lax.broadcasted_iota(jnp.int32,(keys,rows),0)
    row=first_row+lax.broadcasted_iota(jnp.int32,(keys,rows),1)
    b0=bounds_ref[0]; b1=bounds_ref[1]
    begin=jnp.where(row>=b1,b1,jnp.where(row>=b0,b0,0))
    return jnp.where((key<=row)&(key>=begin),0.0,-1e30)

def fwd_kernel(slots, where_ref, bounds_ref, q_ref, *refs):
    kv_refs = refs[:slots]
    gain_ref, cos_ref, sin_ref, qr_ref, ob_ref, oT_ref, qs, ks, vs, bias = refs[slots:]
    rows, width = kv_refs[0].shape
    width //= 2
    heads = q_ref.shape[1] // HEAD
    kvh = width // HEAD
    me = where_ref[slots]
    for i in range(heads // 2):
        at = slice(2 * HEAD * i, 2 * HEAD * (i + 1))
        x = q_ref[:, at]
        xn = x * pair_inverse(x) * gain_ref[...]
        qr_ref[:, at] = (xn * cos_ref[...] + partner(xn) * sin_ref[...]).astype(LOW)
    for h in range(heads):
        qs[h] = qr_ref[:, HEAD * h : HEAD * (h + 1)]
    for j in range(slots):
        for k in range(kvh):
            ks[j * kvh + k] = kv_refs[j][:, HEAD * k : HEAD * (k + 1)]
            vT = kv_refs[j][:, width + HEAD * k : width + HEAD * (k + 1)].astype(jnp.float32).T
            vs[j * kvh + k] = jnp.concatenate([vT, jnp.ones_like(vT)], axis=0).astype(LOW)
    oT_ref[...] = jnp.zeros_like(oT_ref)

    def step(t, carry):
        c = where_ref[t // kvh]
        k = lax.rem(t, kvh)

        @pl.when((c <= me) & (c >= 0))
        def _():
            @pl.when(k == 0)
            def _():
                bias[...] = bias_of(c * rows, me * rows, bounds_ref, rows, rows)

            kb = ks[t]
            vaug = vs[t]
            for g in range(GROUP):
                s = contract_cols(kb, qs[k * GROUP + g])
                p = jnp.exp2(s * (0.125 * LOG2E) + bias[...]).astype(LOW)
                oT_ref[k, :, g * rows : (g + 1) * rows] += jnp.dot(
                    vaug, p, preferred_element_type=jnp.float32
                )

        return carry

    lax.fori_loop(0, slots * kvh, step, 0)
    for k in range(kvh):
        oT = oT_ref[k, :HEAD, :] * (1.0 / oT_ref[k, HEAD : HEAD + 1, :])
        oT_ref[k, :HEAD, :] = oT
        for g in range(GROUP):
            h = k * GROUP + g
            ob_ref[:, HEAD * h : HEAD * (h + 1)] = oT[:, g * rows : (g + 1) * rows].T.astype(LOW)


def bwd_kernel(slots, where_ref, bounds_ref, q_ref, qr_ref, dob_ref, oT_ref, *refs):
    kv_refs = refs[:slots]
    gain_ref, cos_ref, sin_ref, _, _, dqb_ref = refs[slots : slots + 6]
    dkv_refs = refs[slots + 6 : 2 * slots + 6]
    gg_ref, qs, ds_, ks, vs, kTs, dks, dvs, logl, delta, dqT, bias = refs[2 * slots + 6 :]
    rows, width = kv_refs[0].shape
    width //= 2
    heads = q_ref.shape[1] // HEAD
    kvh = width // HEAD
    me = where_ref[slots]
    for h in range(heads):
        k, g = h // GROUP, h % GROUP
        at = slice(g * rows, (g + 1) * rows)
        qs[h] = qr_ref[:, HEAD * h : HEAD * (h + 1)]
        d = dob_ref[:, HEAD * h : HEAD * (h + 1)]
        ds_[h] = d
        dT = d.astype(jnp.float32).T
        delta[k, :, at] = jnp.broadcast_to(
            jnp.sum(dT * oT_ref[k, :HEAD, at], axis=0, keepdims=True), (8, rows)
        )
    for k in range(kvh):
        logl[k] = jnp.broadcast_to(jnp.log2(oT_ref[k, HEAD : HEAD + 1, :]), logl.shape[1:])
    for j in range(slots):
        for k in range(kvh):
            t = j * kvh + k
            kb = kv_refs[j][:, HEAD * k : HEAD * (k + 1)]
            ks[t] = kb
            vs[t] = kv_refs[j][:, width + HEAD * k : width + HEAD * (k + 1)]
            kTs[t] = kb.astype(jnp.float32).T.astype(LOW)
    dqT[...] = jnp.zeros_like(dqT)

    def step(t, carry):
        c = where_ref[t // kvh]
        k = lax.rem(t, kvh)
        seen = (c <= me) & (c >= 0)

        @pl.when(seen)
        def _():
            @pl.when(k == 0)
            def _():
                bias[...] = bias_of(c * rows, me * rows, bounds_ref, rows, rows)

            kb = ks[t]
            vb = vs[t]
            kT = kTs[t]
            dk = jnp.zeros((rows, HEAD), jnp.float32)
            dv = jnp.zeros((rows, HEAD), jnp.float32)
            for g in range(GROUP):
                at = slice(g * rows, (g + 1) * rows)
                qh = qs[k * GROUP + g]
                dh = ds_[k * GROUP + g]
                s = contract_cols(kb, qh)
                p = jnp.exp2(s * (0.125 * LOG2E) + (bias[...] - logl[k, 0:1, at]))
                dp = contract_cols(vb, dh)
                ds = (p * (dp - delta[k, 0:1, at])).astype(LOW)
                dv += jnp.dot(p.astype(LOW), dh, preferred_element_type=jnp.float32)
                dk += jnp.dot(ds, qh, preferred_element_type=jnp.float32)
                dqT[k, :, at] += jnp.dot(kT, ds, preferred_element_type=jnp.float32)
            dks[t] = (dk * 0.125).astype(LOW)
            dvs[t] = dv.astype(LOW)

        @pl.when(jnp.logical_not(seen))
        def _():
            dks[t] = jnp.zeros((rows, HEAD), LOW)
            dvs[t] = jnp.zeros((rows, HEAD), LOW)

        return carry

    lax.fori_loop(0, slots * kvh, step, 0)
    for j in range(slots):
        for k in range(kvh):
            t = j * kvh + k
            dkv_refs[j][:, HEAD * k : HEAD * (k + 1)] = dks[t]
            dkv_refs[j][:, width + HEAD * k : width + HEAD * (k + 1)] = dvs[t]
    gg = jnp.zeros((1, 2 * HEAD), jnp.float32)
    for i in range(heads // 2):
        at = slice(2 * HEAD * i, 2 * HEAD * (i + 1))
        pair = []
        for h in (2 * i, 2 * i + 1):
            k, g = h // GROUP, h % GROUP
            pair.append(dqT[k, :, g * rows : (g + 1) * rows].T * 0.125)
        d = jnp.concatenate(pair, axis=1)
        x = q_ref[:, at]
        inv = pair_inverse(x)
        dn = d * cos_ref[...] - partner(d) * sin_ref[...]
        gg += jnp.sum(dn * x * inv, axis=0, keepdims=True)
        sc = dn * gain_ref[...]
        dqb_ref[:, at] = (inv * sc - x * (inv * inv * inv) * pair_mean(sc * x)).astype(LOW)
    gg_ref[...] = gg


def kback_kernel(kv_ref, d_ref, gain_ref, cos_ref, sin_ref, *refs):
    out_ref, gg_ref = refs[-2:]
    width = kv_ref.shape[1] // 2
    gg = jnp.zeros((1, 2 * HEAD), jnp.float32)
    for i in range(width // (2 * HEAD)):
        at = slice(2 * HEAD * i, 2 * HEAD * (i + 1))
        x = kv_ref[:, at]
        d = d_ref[:, at]
        inv = pair_inverse(x)
        dn = d * cos_ref[...] - partner(d) * sin_ref[...]
        gg += jnp.sum(dn * x * inv, axis=0, keepdims=True)
        sc = dn * gain_ref[...]
        out_ref[:, at] = (inv * sc - x * (inv * inv * inv) * pair_mean(sc * x)).astype(LOW)
    out_ref[:, width:] = d_ref[:, width:].astype(LOW)
    gg_ref[...] = gg


def prepare_keys(kv, gain, cosine, sine):
    return pl.pallas_call(
        kprep_kernel,
        out_shape=shaped(kv.shape),
        in_specs=[VMEM] * 4,
        out_specs=VMEM,
        compiler_params=PARAMS,
        name="keys",
        cost_estimate=cost(1),
    )(kv, gain, cosine, sine)


def attend(where, bounds, q, kv, gain, cosine, sine):
    slots = len(kv)
    rows, width = kv[0].shape
    heads = width // 2 // HEAD
    return pl.pallas_call(
        functools.partial(fwd_kernel, slots),
        out_shape=(
            shaped(q.shape),
            shaped(q.shape),
            shaped((heads, 2 * HEAD, GROUP * rows), jnp.float32),
        ),
        in_specs=[SMEM, SMEM] + [VMEM] * (4 + slots),
        out_specs=(VMEM,) * 3,
        scratch_shapes=[
            pltpu.VMEM((heads * GROUP, rows, HEAD), LOW),
            pltpu.VMEM((slots * heads, rows, HEAD), LOW),
            pltpu.VMEM((slots * heads, 2 * HEAD, rows), LOW),
            pltpu.VMEM((rows, rows), jnp.float32),
        ],
        compiler_params=PARAMS,
        name="attend",
        cost_estimate=cost(14),
    )(where, bounds, q, *kv, gain, cosine, sine)


def attend_back(where, bounds, q, qr, dob, mixed, kv, gain, cosine, sine, later):
    slots = len(kv)
    rows, width = kv[0].shape
    heads = width // 2 // HEAD
    return pl.pallas_call(
        functools.partial(bwd_kernel, slots),
        out_shape=(shaped(q.shape),)
        + (shaped(kv[0].shape),) * slots
        + (shaped((1, 2 * HEAD), jnp.float32),),
        in_specs=[SMEM, SMEM] + [VMEM] * (7 + slots) + [ANY] * 2,
        out_specs=(VMEM,) * (2 + slots),
        scratch_shapes=[
            pltpu.VMEM((heads * GROUP, rows, HEAD), LOW),
            pltpu.VMEM((heads * GROUP, rows, HEAD), LOW),
            pltpu.VMEM((slots * heads, rows, HEAD), LOW),
            pltpu.VMEM((slots * heads, rows, HEAD), LOW),
            pltpu.VMEM((slots * heads, HEAD, rows), LOW),
            pltpu.VMEM((slots * heads, rows, HEAD), LOW),
            pltpu.VMEM((slots * heads, rows, HEAD), LOW),
            pltpu.VMEM((heads, 8, GROUP * rows), jnp.float32),
            pltpu.VMEM((heads, 8, GROUP * rows), jnp.float32),
            pltpu.VMEM((heads, HEAD, GROUP * rows), jnp.float32),
            pltpu.VMEM((rows, rows), jnp.float32),
        ],
        compiler_params=PARAMS,
        name="attend_back",
        cost_estimate=cost(17),
    )(where, bounds, q, qr, dob, mixed, *kv, gain, cosine, sine, *later)


def keys_back(kv, grads, gain, cosine, sine, later=()):
    return pl.pallas_call(
        kback_kernel,
        out_shape=(shaped(kv.shape), shaped((1, 2 * HEAD), jnp.float32)),
        in_specs=[VMEM] * 5 + [ANY] * len(later),
        out_specs=(VMEM,) * 2,
        compiler_params=PARAMS,
        name="keys_back",
        cost_estimate=cost(1),
    )(kv, grads, gain, cosine, sine, *later)


def normed_back(grad_query, grad_kv, query, kv, tokens, inverse):
    def kernel(dq, dkv, wq, wkv, x, inv, out, gain):
        terms = contract_cols(dq[...], wq[...]) + contract_cols(dkv[...], wkv[...])
        out[...] = terms.astype(LOW)
        gain[...] = jnp.sum(
            terms * (x[...].astype(jnp.float32) * inv[...]), axis=0, keepdims=True
        )

    rows, model = tokens.shape
    return pl.pallas_call(
        kernel,
        out_shape=(shaped((rows, model)), shaped((1, model), jnp.float32)),
        in_specs=[VMEM] * 6,
        out_specs=(VMEM,) * 2,
        compiler_params=PARAMS,
        name="normed_back",
        cost_estimate=cost(4),
    )(grad_query, grad_kv, query, kv, tokens, inverse)


def begin(copies):
    for copy in copies:
        copy.start()


def finish(copies):
    for copy in copies:
        copy.wait()


def collect(parts, later=()):
    count = len(parts)

    def kernel(*refs):
        out, sems = refs[-2:]
        copies = [pltpu.make_async_copy(refs[i], out.at[i], sems.at[i]) for i in range(count)]
        begin(copies)
        finish(copies)

    return pl.pallas_call(
        kernel,
        out_shape=shaped((count,) + parts[0].shape, parts[0].dtype),
        in_specs=[ANY] * (count + len(later)),
        out_specs=VMEM,
        scratch_shapes=[pltpu.SemaphoreType.DMA((count,))],
        compiler_params=PARAMS,
        name="collect",
        cost_estimate=cost(1),
    )(*parts, *later)


def chunks_of(width):
    return ((0, width),)


def split_columns(where, weights):
    count = len(weights)
    share, width = weights[0].shape
    parts = 4
    width //= parts
    chunks = chunks_of(width)

    def kernel(where_ref, *refs):
        me = where_ref[where.shape[0] - 1]
        ins, outs = refs[:count], refs[count:]
        for column in range(parts):
            for bit in range(parts):

                @pl.when(column ^ bit == me)
                def _():
                    for j, (begin, end) in enumerate(chunks):
                        at = slice(column * width + begin, column * width + end)
                        for i in range(count):
                            outs[j * parts + bit][i] = ins[i][:, at]

    outs = pl.pallas_call(
        kernel,
        out_shape=tuple(
            shaped((count, share, end - begin)) for begin, end in chunks for _ in range(parts)
        ),
        in_specs=[SMEM] + [VMEM] * count,
        out_specs=(VMEM,) * (parts * len(chunks)),
        compiler_params=PARAMS,
        name="split_columns",
        cost_estimate=cost(3),
    )(where, *weights)
    return [outs[j * parts : (j + 1) * parts] for j in range(len(chunks))]


def join_columns(where, slots):
    parts = len(slots[0])
    count, share, _ = slots[0][0].shape
    width = sum(chunk[0].shape[-1] for chunk in slots)
    chunks = chunks_of(width)

    def kernel(where_ref, *refs):
        me = where_ref[where.shape[0] - 1]
        ins, outs = refs[: parts * len(chunks)], refs[parts * len(chunks) :]
        for column in range(parts):
            for bit in range(parts):

                @pl.when(column ^ bit == me)
                def _():
                    for j, (begin, end) in enumerate(chunks):
                        at = slice(column * width + begin, column * width + end)
                        for i in range(count):
                            outs[i][:, at] = ins[j * parts + bit][i].astype(jnp.float32)

    return pl.pallas_call(
        kernel,
        out_shape=(shaped((share, width * parts), jnp.float32),) * count,
        in_specs=[SMEM] + [VMEM] * (parts * len(chunks)),
        out_specs=(VMEM,) * count,
        compiler_params=PARAMS,
        name="join_columns",
        cost_estimate=cost(4),
    )(where, *[part for chunk in slots for part in chunk])


def arrange(where, slots, share, pieces):
    own, both, across = slots
    size, rows, width = own.shape
    parts = 4
    more = rows - share
    piece = width // pieces

    def kernel(where_ref, *refs):
        me = where_ref[size + 1]
        own, both, across = refs[:3]
        outs, sems = refs[3:-1], refs[-1]
        ins = [own, both.at[0], across, both.at[1]]
        copies = []
        for bit in range(parts):
            for step in range(size):
                index = (me ^ bit) * size + where_ref[step]
                row = pl.multiple_of(index * share, share)
                for i in range(pieces):
                    copies.append(
                        pltpu.make_async_copy(
                            ins[bit].at[step, pl.ds(0, share), pl.ds(i * piece, piece)],
                            outs[i].at[pl.ds(row, share)],
                            sems.at[i, bit, step],
                        )
                    )
                if more:
                    copies.append(
                        pltpu.make_async_copy(
                            ins[bit].at[step, pl.ds(share, more)],
                            outs[pieces].at[index],
                            sems.at[pieces, bit, step],
                        )
                    )
        begin(copies)
        finish(copies)

    shapes = [shaped((parts * size * share, piece))] * pieces
    if more:
        shapes.append(shaped((parts * size, more, width)))
    return pl.pallas_call(
        kernel,
        out_shape=tuple(shapes),
        in_specs=[SMEM] + [ANY] * 3,
        out_specs=(VMEM,) * len(shapes),
        scratch_shapes=[pltpu.SemaphoreType.DMA((pieces + 1, parts, size))],
        compiler_params=PARAMS,
        name="arrange",
        cost_estimate=cost(2),
    )(where, *slots)


def token_copies(refs, whole, sems):
    own, both, across = refs
    rows = own.shape[0]
    pairs = ((own, 0), (both.at[0], 1), (across, 2), (both.at[1], 3))
    return [
        pltpu.make_async_copy(ref, whole.at[pl.ds(i * rows, rows)], sems.at[i]) for ref, i in pairs
    ]


def weight_copies(where_ref, ref, m, whole, sems):
    size, parts, _, share, _ = ref.shape
    me = where_ref[size + 1]
    copies = []
    for c in range(size):
        for bit in range(parts):
            row = pl.multiple_of(((me ^ bit) * size + c) * share, share)
            copies.append(
                pltpu.make_async_copy(
                    ref.at[c, bit, m], whole.at[pl.ds(row, share)], sems.at[c * parts + bit]
                )
            )
    return copies


def ffn(where, tokens, pulled, weights, before=(), later=()):
    rows, model = tokens[0].shape
    size, parts, _, _, width = weights.shape
    total = rows * parts

    def kernel(where_ref, *refs):
        weights_ref = refs[6]
        more = len(before)
        sums = refs[7 : 7 + more]
        refs = refs[: 7 + more] + refs[7 + more + len(later) :]
        keep, send, middle, d_gate, d_up = refs[7 + more : 12 + more]
        hn, cot, w_gate, w_up, w_down, sem_h, sem_c, sem_g, sem_u, sem_d = refs[12 + more :]
        gates = weight_copies(where_ref, weights_ref, 0, w_gate, sem_g)
        reads = token_copies(refs[:3], hn, sem_h)
        ups = weight_copies(where_ref, weights_ref, 1, w_up, sem_u)
        pulls = token_copies(refs[3:6], cot, sem_c)
        downs = weight_copies(where_ref, weights_ref, 2, w_down, sem_d)
        for copies in (gates, reads, ups, pulls, downs):
            begin(copies)

        def token_part(i, carry):
            at = pl.ds(pl.multiple_of(i * rows, rows), rows)

            @pl.when(i == 0)
            def _():
                finish(gates)
                finish(reads)

            g = jnp.dot(hn[at], w_gate[...], preferred_element_type=jnp.float32)

            @pl.when(i == 0)
            def _():
                finish(ups)

            u = jnp.dot(hn[at], w_up[...], preferred_element_type=jnp.float32)
            sigma = jax.nn.sigmoid(g)
            active = g * sigma
            middle[at] = (active * u).astype(LOW)

            @pl.when(i == 0)
            def _():
                finish(pulls)
                finish(downs)

            d = jnp.dot(cot[at], w_down[...], preferred_element_type=jnp.float32)
            d_gate[at] = (d * u * sigma * (1.0 + g * (1.0 - sigma))).astype(LOW)
            d_up[at] = (d * active).astype(LOW)
            back = contract_cols(d_gate[at], w_gate[...]) + contract_cols(d_up[at], w_up[...])
            index = i // 2
            for j, out in enumerate((keep, send)):

                @pl.when(lax.rem(i, 2) == j)
                def _():
                    if more:
                        out[index] = (back + sums[j][index].astype(jnp.float32)).astype(LOW)
                    else:
                        out[index] = back.astype(LOW)

            return carry

        lax.fori_loop(0, parts, token_part, 0)

    return pl.pallas_call(
        kernel,
        out_shape=(shaped((2, rows, model)),) * 2 + (shaped((total, width)),) * 3,
        in_specs=[SMEM] + [ANY] * 7 + [VMEM] * len(before) + [ANY] * len(later),
        out_specs=(VMEM,) * 5,
        scratch_shapes=[pltpu.VMEM((total, model), LOW)] * 2
        + [pltpu.VMEM((model, width), LOW)] * 3
        + [pltpu.SemaphoreType.DMA((4,))] * 2
        + [pltpu.SemaphoreType.DMA((size * parts,))] * 3,
        compiler_params=PARAMS,
        name="ffn",
        cost_estimate=cost(15),
    )(where, *tokens, *pulled, weights, *before, *later)


def ffn_out(where, middles, weights, later):
    count = len(weights)
    size, parts, _, share, _ = weights[0].shape
    model = parts * size * share
    rows = middles[0].shape[0] // parts

    def kernel(where_ref, *refs):
        mids, weight_refs = refs[:count], refs[count : 2 * count]
        keep, send = refs[2 * count + 1 : 2 * count + 3]
        downs, sems = refs[2 * count + 3 : 3 * count + 3], refs[3 * count + 3 :]
        copies = [
            weight_copies(where_ref, weight_refs[j], 2, downs[j], sems[j]) for j in range(count)
        ]
        for each in copies:
            begin(each)
        for each in copies:
            finish(each)

        def token_part(i, carry):
            at = pl.ds(pl.multiple_of(i * rows, rows), rows)
            d = sum(contract_cols(mids[j][at], downs[j][...]) for j in range(count)).astype(LOW)
            index = i // 2

            @pl.when(lax.rem(i, 2) == 0)
            def _():
                keep[index] = d

            @pl.when(lax.rem(i, 2) == 1)
            def _():
                send[index] = d

            return carry

        lax.fori_loop(0, parts, token_part, 0)

    return pl.pallas_call(
        kernel,
        out_shape=(shaped((2, rows, model)), shaped((2, rows, model))),
        in_specs=[SMEM] + [VMEM] * count + [ANY] * (count + 1),
        out_specs=(VMEM,) * 2,
        scratch_shapes=[pltpu.VMEM((model, each.shape[-1]), LOW) for each in weights]
        + [pltpu.SemaphoreType.DMA((size * parts,))] * count,
        compiler_params=PARAMS,
        name="ffn_out",
        cost_estimate=cost(9),
    )(where, *middles, *weights, later)


def hidden_grads(where, tokens, rights, pulled, lasts, later=()):
    rows, model = tokens[0].shape
    lefts = len(rights)
    rights = rights + lasts
    count = len(rights)
    size = where.shape[0] - 2
    total, width = rights[0].shape
    parts = total // rows
    tall = model // parts
    share = tall // size

    def kernel(where_ref, *refs):
        refs = refs[: 6 + count] + refs[6 + count + len(later) :]
        out = refs[6 + count]
        left, right, stage, sem_h, sem_c, sem_r, sem_o = refs[7 + count :]
        me = where_ref[size + 1]
        reads = token_copies(refs[:3], left.at[0], sem_h)
        pulls = token_copies(refs[3:6], left.at[1], sem_c)
        operands = [
            pltpu.make_async_copy(refs[6 + m], right.at[m], sem_r.at[m]) for m in range(count)
        ]
        begin(reads)
        begin(operands)
        begin(pulls)

        def write(i, c):
            m, part = i // parts, lax.rem(i, parts)
            return pltpu.make_async_copy(
                stage.at[i, pl.ds(c * share, share)], out.at[c, me ^ part, m], sem_o.at[i, c]
            )

        def block(i, carry):
            m, part = i // parts, lax.rem(i, parts)

            @pl.when(i == 0)
            def _():
                finish(reads)

            for k in range(count):

                @pl.when(i == k * parts)
                def _():
                    operands[k].wait()

            @pl.when(i == lefts * parts)
            def _():
                finish(pulls)

            column = pl.multiple_of(part * tall, tall)
            which = (m >= lefts).astype(jnp.int32)
            stage[i] = contract_rows(left[which, :, pl.ds(column, tall)], right[m]).astype(LOW)
            for c in range(size):
                write(i, c).start()
            return carry

        lax.fori_loop(0, count * parts, block, 0)

        def drain(i, carry):
            for c in range(size):
                write(i, c).wait()
            return carry

        lax.fori_loop(0, count * parts, drain, 0)

    return pl.pallas_call(
        kernel,
        out_shape=shaped((size, parts, count, share, width)),
        in_specs=[SMEM] + [ANY] * (6 + count + len(later)),
        out_specs=ANY,
        scratch_shapes=[
            pltpu.VMEM((2, total, model), LOW),
            pltpu.VMEM((count, total, width), LOW),
            pltpu.VMEM((count * parts, tall, width), LOW),
            pltpu.SemaphoreType.DMA((4,)),
            pltpu.SemaphoreType.DMA((4,)),
            pltpu.SemaphoreType.DMA((count,)),
            pltpu.SemaphoreType.DMA((count * parts, size)),
        ],
        compiler_params=PARAMS,
        name="hidden_grads",
        cost_estimate=cost(3 * count),
    )(where, *tokens, *pulled, *rights, *later)


def head_grads(where, lefts, rights, gains=None, small=0, later=()):
    count = len(lefts)
    model = lefts[0].shape[1]
    each = rights[0].shape[1]
    width = each * count
    size = where.shape[0] - 2
    parts = 4
    tall = model // parts
    share = tall // size
    pad = 16 if gains else 0
    gains = gains or []

    def kernel(where_ref, *refs):
        left_refs, right_refs, refs = refs[:count], refs[count : 2 * count], refs[2 * count :]
        keep, send = refs[-2:]
        me = where_ref[size + 1]
        here = where_ref[size]

        def place(bit, c):
            return bit // 2, lax.rem(here - c + size, size) if size <= LINE else c

        def block(part, carry):
            column = pl.multiple_of(part * tall, tall)
            bit = me ^ part
            for m in range(count):
                grads = contract_rows(
                    left_refs[m][:, pl.ds(column, tall)], right_refs[m][...]
                ).astype(LOW)
                for out, odd in ((keep, 0), (send, 1)):

                    @pl.when(lax.rem(bit, 2) == odd)
                    def _():
                        for c in range(size):
                            index, step = place(bit, c)
                            out[index, step, :share, m * each : (m + 1) * each] = grads[
                                c * share : (c + 1) * share
                            ]

            return carry

        lax.fori_loop(0, parts, block, 0)
        if pad:
            pairs = [gain[:, :HEAD] + gain[:, HEAD:] for gain in refs[2:4]]
            for part in range(parts):
                bit = me ^ part
                for c in range(size):
                    i = part * size + c
                    index, step = place(bit, c)
                    pieces = [gain[:, i * share : (i + 1) * share] for gain in refs[:2]]
                    pieces += [pair[:, i * small : (i + 1) * small] for pair in pairs]
                    row = jnp.concatenate(
                        [
                            jnp.concatenate(
                                [piece, jnp.zeros((1, 128 - piece.shape[1]), jnp.float32)], axis=1
                            )
                            for piece in pieces
                        ],
                        axis=1,
                    )
                    tile = jnp.broadcast_to(row, (pad, width)).astype(LOW)
                    for out, odd in ((keep, 0), (send, 1)):

                        @pl.when(lax.rem(bit, 2) == odd)
                        def _():
                            out[index, step, share:] = tile

    return pl.pallas_call(
        kernel,
        out_shape=(shaped((2, size, share + pad, width)),) * 2,
        in_specs=[SMEM] + [VMEM] * (2 * count + len(gains)) + [ANY] * len(later),
        out_specs=(VMEM,) * 2,
        compiler_params=PARAMS,
        name="head_grads",
        cost_estimate=cost(3),
    )(where, *lefts, *rights, *gains, *later)


def flip(part, bit):
    size = lax.axis_size("fsdp")
    return lax.ppermute(part, "fsdp", [(i, i ^ bit) for i in range(size)])


def swap(part):
    return lax.ppermute(part, "tp", [(0, 1), (1, 0)])


def turn(part):
    size = lax.axis_size("ctx")
    return lax.ppermute(part, "ctx", [(i, (i + 1) % size) for i in range(size)])


def ctx_slots(part):
    size = lax.axis_size("ctx")
    if size > LINE:
        whole = lax.all_gather(part, "ctx", axis=0)
        return [whole[i] for i in range(size)]
    slots = [part]
    for _ in range(1, size):
        slots.append(turn(slots[-1]))
    return slots


def ctx_sum(terms):
    size = lax.axis_size("ctx")
    if size > LINE:
        return lax.psum_scatter(terms, "ctx", scatter_dimension=0, tiled=False).astype(jnp.float32)
    moving = terms[1]
    for step in range(1, size):
        total = turn(moving).astype(jnp.float32) + terms[(step + 1) % size].astype(jnp.float32)
        moving = total.astype(LOW)
    return total


def back_slots(part):
    size = lax.axis_size("ctx")
    if size > LINE:
        whole = lax.all_gather(part, "ctx", axis=0)
        return [whole[i] for i in range(size)]
    slots = [part]
    for step in range(1, size):
        slots.append(lax.ppermute(part, "ctx", [(i, i + step) for i in range(size - step)]))
    return slots


def back_sum(terms):
    size = lax.axis_size("ctx")
    if size > LINE:
        total = lax.psum_scatter(jnp.stack(terms), "ctx", scatter_dimension=0, tiled=False)
        return total.astype(jnp.float32), total
    parts = [terms[0]] + [
        lax.ppermute(terms[step], "ctx", [(i, i - step) for i in range(step, size)])
        for step in range(1, size)
    ]
    return sum(part.astype(jnp.float32) for part in parts), parts[1]


def group_tokens(part):
    across = flip(part, 2)
    return (part, flip(collect([part, across]), 1), across)


def chip_sum(keep, send):
    beside = flip(send, 1)
    far = keep[1].astype(jnp.float32) + beside[1].astype(jnp.float32)
    near = keep[0].astype(jnp.float32) + beside[0].astype(jnp.float32)
    return near, far.astype(LOW)


def pair_sum(near, far):
    return near + flip(far, 2).astype(jnp.float32)


def group_sum(keep, send):
    return pair_sum(*chip_sum(keep, send))


def gather_all(where, slots, share, later=()):
    own = collect(slots, later)
    across = flip(own, 2)
    both = flip(collect([own, across]), 1)
    return arrange(where, [own, both, across], share, 1), across


def scatter_hidden(terms):
    size, parts, count, share, width = terms.shape
    own = lax.psum_scatter(terms.reshape(-1, width), "ctx", scatter_dimension=0, tiled=True)
    own = own.reshape(parts, count, share, width)
    return [own[0]] + [flip(own[bit], bit) for bit in range(1, parts)]


def body(
    inputs,
    cotangent,
    doc_bounds,
    attn_gain,
    w_query,
    w_key,
    w_value,
    w_output,
    query_gain,
    key_gain,
    ffn_gain,
    w_gate,
    w_up,
    w_down,
):
    parts = lax.axis_size("fsdp")
    size = lax.axis_size("ctx")
    tensor = lax.axis_size("tp")
    me = lax.axis_index("ctx")
    share = w_query.shape[0]
    model = share * parts * size
    width = HQ // tensor * HEAD
    kv_width = HK // tensor * HEAD
    small = query_gain.shape[0]
    shards = parts * size
    steps = jnp.arange(size, dtype=jnp.int32)
    slots_at = lax.rem(me - steps + size, size) if size <= LINE else steps
    where = jnp.concatenate(
        [slots_at, jnp.stack([me, lax.axis_index("fsdp")]).astype(jnp.int32)]
    )
    bounds = doc_bounds[0]

    split = split_columns(where, [w_gate, w_up, w_down.T])
    gains = jnp.concatenate([attn_gain, ffn_gain, query_gain, key_gain])
    pad = 16
    gain_rows = jnp.zeros((pad, 2 * kv_width), LOW).at[0, : gains.shape[0]].set(gains)
    kv_block = jnp.concatenate([jnp.concatenate([w_key, w_value], axis=1), gain_rows], axis=0)
    traded = [
        [part[0]] + [flip(part[bit], bit) for bit in range(1, parts)] for part in split
    ]
    kv_slots = ctx_slots(kv_block)
    query_slots = ctx_slots(w_query)
    output_slots = ctx_slots(w_output.T)
    (full_kv, gain_rows), kv_across = gather_all(where, kv_slots, share)
    (full_query,), query_across = gather_all(where, query_slots, share, [kv_across])
    (full_output,), output_across = gather_all(where, output_slots, share, [query_across])
    weights = []
    for chunk in traded:
        block = collect(chunk, [kv_slots[-1]])
        weights.append(
            lax.all_gather(
                block.reshape(-1, block.shape[-1]), "ctx", axis=0, tiled=True
            ).reshape(size, *block.shape)
        )
    pulled_all = group_tokens(collect([cotangent[0]], [output_across])[0])
    all_gains = gain_rows[:, 0].astype(jnp.float32)
    gain_attn = all_gains[:, :share].reshape(model)
    gain_ffn = all_gains[:, share : 2 * share].reshape(model)
    gain_query = jnp.tile(all_gains[:, 2 * share : 2 * share + small].reshape(HEAD), 2)[None]
    gain_key = jnp.tile(
        all_gains[:, 2 * share + small : 2 * share + 2 * small].reshape(HEAD), 2
    )[None]

    pulled = cotangent[0]

    tokens = inputs[0].astype(jnp.float32)
    rows = tokens.shape[0]
    cosine, sine = tables(me * rows, rows, bounds)
    first_inv = inverse_rms(tokens)
    normed = (tokens * first_inv * gain_attn).astype(LOW)
    keys_values = jnp.dot(normed, full_kv, preferred_element_type=jnp.float32)
    own_kv = prepare_keys(keys_values, gain_key, cosine, sine)
    kv = back_slots(own_kv)
    queries = jnp.dot(normed, full_query, preferred_element_type=jnp.float32)
    query_rot, mixed_low, mixed = attend(where, bounds, queries, kv, gain_query, cosine, sine)
    branch_part = contract_cols(mixed_low, full_output).astype(LOW)
    branch = branch_part.astype(jnp.float32) + swap(branch_part).astype(jnp.float32)
    hidden = tokens + branch
    second_inv = inverse_rms(hidden)
    hidden_normed = (hidden * second_inv * gain_ffn).astype(LOW)

    hidden_all = group_tokens(hidden_normed)
    keep, send, middle, grad_gate_low, grad_up_low = ffn(
        where, hidden_all, pulled_all, weights[0]
    )
    near, far = chip_sum(keep, send)
    normed_part = pair_sum(near, far).astype(LOW)
    terms = hidden_grads(
        where, hidden_all, [grad_gate_low, grad_up_low], pulled_all, [middle], [far]
    )
    grad_gate, grad_up, grad_down = join_columns(where, [scatter_hidden(terms)])
    grad_down = grad_down.T
    feed_terms = ffn_out(where, [middle], weights, normed_part)
    grad_normed_ffn = normed_part.astype(jnp.float32) + swap(normed_part).astype(jnp.float32)

    ffn_gain_part = jnp.sum(grad_normed_ffn * hidden * second_inv, axis=0) * 0.5
    grad_hidden = pulled.astype(jnp.float32) + norm_back(
        hidden, second_inv, gain_ffn, grad_normed_ffn
    )
    grad_hidden_low = grad_hidden.astype(LOW)
    grad_mixed = jnp.dot(
        grad_hidden_low, full_output, preferred_element_type=jnp.float32
    ).astype(LOW)
    grad_query_low, *key_terms, query_gain_pair = attend_back(
        where, bounds, queries, query_rot, grad_mixed, mixed, kv, gain_query, cosine, sine,
        [terms, feed_terms[0]],
    )
    near, far = chip_sum(
        *head_grads(where, [normed, grad_hidden_low], [grad_query_low, mixed_low])
    )
    heads_sum = ctx_sum(pair_sum(near, far).astype(LOW))
    moved = collect(key_terms[1:], [far])
    own_terms, _ = back_sum([key_terms[0]] + [moved[i] for i in range(size - 1)])
    grad_query = heads_sum[:, :width]
    grad_output = heads_sum[:, width:].T
    feed_part = group_sum(*feed_terms).astype(LOW)
    feed = feed_part.astype(jnp.float32) + swap(feed_part).astype(jnp.float32)
    result = (hidden + feed).astype(LOW)[None]
    grad_kv_low, key_gain_pair = keys_back(
        keys_values,
        own_terms,
        gain_key,
        cosine,
        sine,
    )
    normed_low, attn_gain_part = normed_back(
        grad_query_low, grad_kv_low, full_query, full_kv, inputs[0], first_inv
    )
    own_kv = ctx_sum(
        group_sum(
            *head_grads(
                where,
                [normed],
                [grad_kv_low],
                [attn_gain_part, ffn_gain_part[None], query_gain_pair, key_gain_pair],
                small,
            )
        ).astype(LOW)
    )
    grad_key = own_kv[:share, :kv_width]
    grad_value = own_kv[:share, kv_width:]
    grad_normed = normed_low.astype(jnp.float32) + swap(normed_low).astype(jnp.float32)
    own_gains = own_kv[share].astype(LOW)
    grad_gains = own_gains.astype(jnp.float32) + swap(own_gains).astype(jnp.float32)
    grad_inputs = grad_hidden + norm_back(tokens, first_inv, gain_attn, grad_normed)
    return (
        result,
        grad_inputs[None],
        grad_gains[:share],
        grad_query,
        grad_key,
        grad_value,
        grad_output,
        grad_gains[256 : 256 + small],
        grad_gains[384 : 384 + small],
        grad_gains[128 : 128 + share],
        grad_gate,
        grad_up,
        grad_down,
    )


def solution(mesh):
    vector = P(("fsdp", "ctx"))
    columns = P(("fsdp", "ctx"), "tp")
    tall = P("tp", ("fsdp", "ctx"))
    act = P("fsdp", "ctx", None)
    return jax.shard_map(
        body,
        mesh=mesh,
        in_specs=(
            act,
            act,
            P("fsdp", None),
            vector,
            columns,
            columns,
            columns,
            tall,
            vector,
            vector,
            vector,
            columns,
            columns,
            tall,
        ),
        out_specs=(
            act,
            act,
            vector,
            columns,
            columns,
            columns,
            tall,
            vector,
            vector,
            vector,
            columns,
            columns,
            tall,
        ),
        check_vma=False,
    )
```

```python
import functools
import math

import jax
import jax.numpy as jnp
from jax import lax
from jax.experimental import pallas as pl
from jax.experimental.pallas import tpu as pltpu
from jax.sharding import PartitionSpec as P

HQ = 24
HK = 8
HEAD = 64
GROUP = HQ // HK


EPS = 1e-05
THETA = 1000000.0
LINE = 4
LOG2E = math.log2(math.e)
LOW = jnp.bfloat16
VMEM = pl.BlockSpec(memory_space=pltpu.VMEM)
SMEM = pl.BlockSpec(memory_space=pltpu.SMEM)
ANY = pl.BlockSpec(memory_space=pl.ANY)
PARAMS = pltpu.CompilerParams(vmem_limit_bytes=52 * 1024 * 1024)


def inverse_rms(values):
    return lax.rsqrt(jnp.mean(values * values, axis=-1, keepdims=True) + EPS)


def norm_back(values, inverse, gain, grads):
    scaled = grads * gain
    return inverse * scaled - values * (inverse * inverse * inverse) * jnp.mean(
        scaled * values, axis=-1, keepdims=True
    )


def contract_rows(left, right):
    return lax.dot_general(
        left, right, (((0,), (0,)), ((), ())), preferred_element_type=jnp.float32
    )


def contract_cols(left, right):
    return lax.dot_general(
        left, right, (((1,), (1,)), ((), ())), preferred_element_type=jnp.float32
    )


def tables(first, rows, bounds):
    index = first + jnp.arange(rows, dtype=jnp.int32)
    begin = jnp.where(index >= bounds[1], bounds[1], jnp.where(index >= bounds[0], bounds[0], 0))
    freq = THETA ** (-(jnp.arange(HEAD // 2, dtype=jnp.float32) * 2.0 / HEAD))
    angle = (index - begin).astype(jnp.float32)[:, None] * freq[None, :]
    cosine = jnp.cos(angle)
    sine = jnp.sin(angle)
    return (
        jnp.concatenate([cosine, cosine, cosine, cosine], axis=1),
        jnp.concatenate([-sine, sine, -sine, sine], axis=1),
    )


def shaped(shape, dtype=LOW):
    return jax.ShapeDtypeStruct(shape, dtype)


def cost(micros):
    return pl.CostEstimate(
        flops=int(micros * 900000000.0), bytes_accessed=int(micros * 1000000.0), transcendentals=0
    )


def pair_inverse(x):
    lane=lax.broadcasted_iota(jnp.int32,x.shape,1)
    left=lane<HEAD
    sq=x*x
    a=jnp.sum(jnp.where(left,sq,0.0),axis=-1,keepdims=True)
    b=jnp.sum(jnp.where(left,0.0,sq),axis=-1,keepdims=True)
    return lax.rsqrt(jnp.where(left,a,b)*(1.0/HEAD)+EPS)

def pair_mean(x):
    lane=lax.broadcasted_iota(jnp.int32,x.shape,1)
    left=lane<HEAD
    a=jnp.sum(jnp.where(left,x,0.0),axis=-1,keepdims=True)
    b=jnp.sum(jnp.where(left,0.0,x),axis=-1,keepdims=True)
    return jnp.where(left,a,b)*(1.0/HEAD)

def partner(x):
    lane=lax.broadcasted_iota(jnp.int32,x.shape,1)
    front=lax.rem(lane,HEAD)<HEAD//2
    return jnp.where(front,pltpu.roll(x,2*HEAD-HEAD//2,1),pltpu.roll(x,HEAD//2,1))

def kprep_kernel(kv_ref,gain_ref,cos_ref,sin_ref,out_ref):
    width=kv_ref.shape[1]//2
    for i in range(width//128):
        x=kv_ref[:,128*i:128*(i+1)]
        xn=x*pair_inverse(x)*gain_ref[...]
        out_ref[:,128*i:128*(i+1)]=(xn*cos_ref[...]+partner(xn)*sin_ref[...]).astype(jnp.bfloat16)
    out_ref[:,width:]=kv_ref[:,width:].astype(jnp.bfloat16)

def bias_of(first_key,first_row,bounds_ref,keys,rows):
    key=first_key+lax.broadcasted_iota(jnp.int32,(keys,rows),0)
    row=first_row+lax.broadcasted_iota(jnp.int32,(keys,rows),1)
    b0=bounds_ref[0]; b1=bounds_ref[1]
    begin=jnp.where(row>=b1,b1,jnp.where(row>=b0,b0,0))
    return jnp.where((key<=row)&(key>=begin),0.0,-1e30)

def fwd_kernel(slots, where_ref, bounds_ref, q_ref, *refs):
    kv_refs = refs[:slots]
    gain_ref, cos_ref, sin_ref, qr_ref, ob_ref, oT_ref, qs, ks, vs, bias = refs[slots:]
    rows, width = kv_refs[0].shape
    width //= 2
    heads = q_ref.shape[1] // HEAD
    kvh = width // HEAD
    me = where_ref[slots]
    for i in range(heads // 2):
        at = slice(2 * HEAD * i, 2 * HEAD * (i + 1))
        x = q_ref[:, at]
        xn = x * pair_inverse(x) * gain_ref[...]
        qr_ref[:, at] = (xn * cos_ref[...] + partner(xn) * sin_ref[...]).astype(LOW)
    for h in range(heads):
        qs[h // GROUP, (h % GROUP) * rows : (h % GROUP + 1) * rows] = qr_ref[
            :, HEAD * h : HEAD * (h + 1)
        ]
    for j in range(slots):
        for k in range(kvh):
            ks[j * kvh + k] = kv_refs[j][:, HEAD * k : HEAD * (k + 1)]
            vT = kv_refs[j][:, width + HEAD * k : width + HEAD * (k + 1)].astype(jnp.float32).T
            vs[j * kvh + k] = jnp.concatenate([vT, jnp.ones_like(vT)], axis=0).astype(LOW)
    oT_ref[...] = jnp.zeros_like(oT_ref)

    def step(j, carry):
        c = where_ref[j]

        @pl.when((c <= me) & (c >= 0))
        def _():
            mask = bias_of(c * rows, me * rows, bounds_ref, rows, rows)
            for g in range(GROUP):
                bias[:, g * rows : (g + 1) * rows] = mask
            for k in range(kvh):
                s = contract_cols(ks[j * kvh + k], qs[k])
                p = jnp.exp2(s * (0.125 * LOG2E) + bias[...]).astype(LOW)
                oT_ref[k] += jnp.dot(vs[j * kvh + k], p, preferred_element_type=jnp.float32)

        return carry

    lax.fori_loop(0, slots, step, 0)
    for k in range(kvh):
        oT = oT_ref[k, :HEAD, :] * (1.0 / oT_ref[k, HEAD : HEAD + 1, :])
        oT_ref[k, :HEAD, :] = oT
        for g in range(GROUP):
            h = k * GROUP + g
            ob_ref[:, HEAD * h : HEAD * (h + 1)] = oT[:, g * rows : (g + 1) * rows].T.astype(LOW)


def bwd_kernel(slots, where_ref, bounds_ref, q_ref, qr_ref, dob_ref, oT_ref, *refs):
    kv_refs = refs[:slots]
    gain_ref, cos_ref, sin_ref, _, dqb_ref = refs[slots : slots + 5]
    dkv_refs = refs[slots + 5 : 2 * slots + 5]
    gg_ref, qs, ds_, ks, vs, kTs, dks, dvs, logl, delta, dqT, bias = refs[2 * slots + 5 :]
    rows, width = kv_refs[0].shape
    width //= 2
    heads = q_ref.shape[1] // HEAD
    kvh = width // HEAD
    me = where_ref[slots]
    for h in range(heads):
        k, g = h // GROUP, h % GROUP
        at = slice(g * rows, (g + 1) * rows)
        qs[k, at] = qr_ref[:, HEAD * h : HEAD * (h + 1)]
        d = dob_ref[:, HEAD * h : HEAD * (h + 1)]
        ds_[k, at] = d
        dT = d.astype(jnp.float32).T
        delta[k, :, at] = jnp.broadcast_to(
            jnp.sum(dT * oT_ref[k, :HEAD, at], axis=0, keepdims=True), (8, rows)
        )
    for k in range(kvh):
        logl[k] = jnp.broadcast_to(jnp.log2(oT_ref[k, HEAD : HEAD + 1, :]), logl.shape[1:])
    for j in range(slots):
        for k in range(kvh):
            t = j * kvh + k
            kb = kv_refs[j][:, HEAD * k : HEAD * (k + 1)]
            ks[t] = kb
            vs[t] = kv_refs[j][:, width + HEAD * k : width + HEAD * (k + 1)]
            kTs[t] = kb.astype(jnp.float32).T.astype(LOW)
    dqT[...] = jnp.zeros_like(dqT)

    def step(j, carry):
        c = where_ref[j]
        seen = (c <= me) & (c >= 0)

        @pl.when(seen)
        def _():
            mask = bias_of(c * rows, me * rows, bounds_ref, rows, rows)
            for g in range(GROUP):
                bias[:, g * rows : (g + 1) * rows] = mask
            for k in range(kvh):
                t = j * kvh + k
                s = contract_cols(ks[t], qs[k])
                dp = contract_cols(vs[t], ds_[k])
                p = jnp.exp2(s * (0.125 * LOG2E) + (bias[...] - logl[k, 0:1]))
                ds = (p * (dp - delta[k, 0:1])).astype(LOW)
                dvs[t] = jnp.dot(p.astype(LOW), ds_[k], preferred_element_type=jnp.float32).astype(LOW)
                dk = jnp.dot(ds, qs[k], preferred_element_type=jnp.float32)
                dks[t] = (dk * 0.125).astype(LOW)
                dqT[k] += jnp.dot(kTs[t], ds, preferred_element_type=jnp.float32)

        @pl.when(jnp.logical_not(seen))
        def _():
            for k in range(kvh):
                dks[j * kvh + k] = jnp.zeros((rows, HEAD), LOW)
                dvs[j * kvh + k] = jnp.zeros((rows, HEAD), LOW)

        return carry

    lax.fori_loop(0, slots, step, 0)
    for j in range(slots):
        for k in range(kvh):
            t = j * kvh + k
            dkv_refs[j][:, HEAD * k : HEAD * (k + 1)] = dks[t]
            dkv_refs[j][:, width + HEAD * k : width + HEAD * (k + 1)] = dvs[t]
    gg = jnp.zeros((1, 2 * HEAD), jnp.float32)
    for i in range(heads // 2):
        at = slice(2 * HEAD * i, 2 * HEAD * (i + 1))
        pair = []
        for h in (2 * i, 2 * i + 1):
            k, g = h // GROUP, h % GROUP
            pair.append(dqT[k, :, g * rows : (g + 1) * rows].T * 0.125)
        d = jnp.concatenate(pair, axis=1)
        x = q_ref[:, at]
        inv = pair_inverse(x)
        dn = d * cos_ref[...] - partner(d) * sin_ref[...]
        gg += jnp.sum(dn * x * inv, axis=0, keepdims=True)
        sc = dn * gain_ref[...]
        dqb_ref[:, at] = (inv * sc - x * (inv * inv * inv) * pair_mean(sc * x)).astype(LOW)
    gg_ref[...] = gg


def kback_kernel(kv_ref, d_ref, gain_ref, cos_ref, sin_ref, *refs):
    out_ref, gg_ref = refs[-2:]
    width = kv_ref.shape[1] // 2
    gg = jnp.zeros((1, 2 * HEAD), jnp.float32)
    for i in range(width // (2 * HEAD)):
        at = slice(2 * HEAD * i, 2 * HEAD * (i + 1))
        x = kv_ref[:, at]
        d = d_ref[:, at]
        inv = pair_inverse(x)
        dn = d * cos_ref[...] - partner(d) * sin_ref[...]
        gg += jnp.sum(dn * x * inv, axis=0, keepdims=True)
        sc = dn * gain_ref[...]
        out_ref[:, at] = (inv * sc - x * (inv * inv * inv) * pair_mean(sc * x)).astype(LOW)
    out_ref[:, width:] = d_ref[:, width:].astype(LOW)
    gg_ref[...] = gg


def prepare_keys(kv, gain, cosine, sine):
    return pl.pallas_call(
        kprep_kernel,
        out_shape=shaped(kv.shape),
        in_specs=[VMEM] * 4,
        out_specs=VMEM,
        compiler_params=PARAMS,
        name="keys",
        cost_estimate=cost(1),
    )(kv, gain, cosine, sine)


def attend(where, bounds, q, kv, gain, cosine, sine):
    slots = len(kv)
    rows, width = kv[0].shape
    heads = width // 2 // HEAD
    return pl.pallas_call(
        functools.partial(fwd_kernel, slots),
        out_shape=(
            shaped(q.shape),
            shaped(q.shape),
            shaped((heads, 2 * HEAD, GROUP * rows), jnp.float32),
        ),
        in_specs=[SMEM, SMEM] + [VMEM] * (4 + slots),
        out_specs=(VMEM,) * 3,
        scratch_shapes=[
            pltpu.VMEM((heads, GROUP * rows, HEAD), LOW),
            pltpu.VMEM((slots * heads, rows, HEAD), LOW),
            pltpu.VMEM((slots * heads, 2 * HEAD, rows), LOW),
            pltpu.VMEM((rows, GROUP * rows), jnp.float32),
        ],
        compiler_params=PARAMS,
        name="attend",
        cost_estimate=cost(14),
    )(where, bounds, q, *kv, gain, cosine, sine)


def attend_back(where, bounds, q, qr, dob, mixed, kv, gain, cosine, sine, later):
    slots = len(kv)
    rows, width = kv[0].shape
    heads = width // 2 // HEAD
    return pl.pallas_call(
        functools.partial(bwd_kernel, slots),
        out_shape=(shaped(q.shape),)
        + (shaped(kv[0].shape),) * slots
        + (shaped((1, 2 * HEAD), jnp.float32),),
        in_specs=[SMEM, SMEM] + [VMEM] * (7 + slots) + [ANY],
        out_specs=(VMEM,) * (2 + slots),
        scratch_shapes=[
            pltpu.VMEM((heads, GROUP * rows, HEAD), LOW),
            pltpu.VMEM((heads, GROUP * rows, HEAD), LOW),
            pltpu.VMEM((slots * heads, rows, HEAD), LOW),
            pltpu.VMEM((slots * heads, rows, HEAD), LOW),
            pltpu.VMEM((slots * heads, HEAD, rows), LOW),
            pltpu.VMEM((slots * heads, rows, HEAD), LOW),
            pltpu.VMEM((slots * heads, rows, HEAD), LOW),
            pltpu.VMEM((heads, 8, GROUP * rows), jnp.float32),
            pltpu.VMEM((heads, 8, GROUP * rows), jnp.float32),
            pltpu.VMEM((heads, HEAD, GROUP * rows), jnp.float32),
            pltpu.VMEM((rows, GROUP * rows), jnp.float32),
        ],
        compiler_params=PARAMS,
        name="attend_back",
        cost_estimate=cost(17),
    )(where, bounds, q, qr, dob, mixed, *kv, gain, cosine, sine, *later)


def keys_back(kv, grads, gain, cosine, sine, later=()):
    return pl.pallas_call(
        kback_kernel,
        out_shape=(shaped(kv.shape), shaped((1, 2 * HEAD), jnp.float32)),
        in_specs=[VMEM] * 5 + [ANY] * len(later),
        out_specs=(VMEM,) * 2,
        compiler_params=PARAMS,
        name="keys_back",
        cost_estimate=cost(1),
    )(kv, grads, gain, cosine, sine, *later)


def normed_back(grad_query, grad_kv, query, kv, tokens, inverse):
    def kernel(dq, dkv, wq, wkv, x, inv, out, gain):
        terms = contract_cols(dq[...], wq[...]) + contract_cols(dkv[...], wkv[...])
        out[...] = terms.astype(LOW)
        gain[...] = jnp.sum(
            terms * (x[...].astype(jnp.float32) * inv[...]), axis=0, keepdims=True
        )

    rows, model = tokens.shape
    return pl.pallas_call(
        kernel,
        out_shape=(shaped((rows, model)), shaped((1, model), jnp.float32)),
        in_specs=[VMEM] * 6,
        out_specs=(VMEM,) * 2,
        compiler_params=PARAMS,
        name="normed_back",
        cost_estimate=cost(4),
    )(grad_query, grad_kv, query, kv, tokens, inverse)


def begin(copies):
    for copy in copies:
        copy.start()


def finish(copies):
    for copy in copies:
        copy.wait()


def collect(parts, later=()):
    count = len(parts)

    def kernel(*refs):
        out, sems = refs[-2:]
        copies = [pltpu.make_async_copy(refs[i], out.at[i], sems.at[i]) for i in range(count)]
        begin(copies)
        finish(copies)

    return pl.pallas_call(
        kernel,
        out_shape=shaped((count,) + parts[0].shape, parts[0].dtype),
        in_specs=[ANY] * (count + len(later)),
        out_specs=VMEM,
        scratch_shapes=[pltpu.SemaphoreType.DMA((count,))],
        compiler_params=PARAMS,
        name="collect",
        cost_estimate=cost(1),
    )(*parts, *later)


def chunks_of(width):
    return ((0, width),)


def split_columns(where, weights):
    count = len(weights)
    share, width = weights[0].shape
    parts = 4
    width //= parts
    chunks = chunks_of(width)

    def kernel(where_ref, *refs):
        me = where_ref[where.shape[0] - 1]
        ins, outs = refs[:count], refs[count:]
        for column in range(parts):
            for bit in range(parts):

                @pl.when(column ^ bit == me)
                def _():
                    for j, (begin, end) in enumerate(chunks):
                        at = slice(column * width + begin, column * width + end)
                        for i in range(count):
                            outs[j * parts + bit][i] = ins[i][:, at]

    outs = pl.pallas_call(
        kernel,
        out_shape=tuple(
            shaped((count, share, end - begin)) for begin, end in chunks for _ in range(parts)
        ),
        in_specs=[SMEM] + [VMEM] * count,
        out_specs=(VMEM,) * (parts * len(chunks)),
        compiler_params=PARAMS,
        name="split_columns",
        cost_estimate=cost(3),
    )(where, *weights)
    return [outs[j * parts : (j + 1) * parts] for j in range(len(chunks))]


def join_columns(where, slots):
    parts = len(slots[0])
    count, share, _ = slots[0][0].shape
    width = sum(chunk[0].shape[-1] for chunk in slots)
    chunks = chunks_of(width)

    def kernel(where_ref, *refs):
        me = where_ref[where.shape[0] - 1]
        ins, outs = refs[: parts * len(chunks)], refs[parts * len(chunks) :]
        for column in range(parts):
            for bit in range(parts):

                @pl.when(column ^ bit == me)
                def _():
                    for j, (begin, end) in enumerate(chunks):
                        at = slice(column * width + begin, column * width + end)
                        for i in range(count):
                            outs[i][:, at] = ins[j * parts + bit][i].astype(jnp.float32)

    return pl.pallas_call(
        kernel,
        out_shape=(shaped((share, width * parts), jnp.float32),) * count,
        in_specs=[SMEM] + [VMEM] * (parts * len(chunks)),
        out_specs=(VMEM,) * count,
        compiler_params=PARAMS,
        name="join_columns",
        cost_estimate=cost(4),
    )(where, *[part for chunk in slots for part in chunk])


def arrange(where, slots, share, pieces):
    own, both, across = slots
    size, rows, width = own.shape
    parts = 4
    more = rows - share
    piece = width // pieces

    def kernel(where_ref, *refs):
        me = where_ref[size + 1]
        own, both, across = refs[:3]
        outs, sems = refs[3:-1], refs[-1]
        ins = [own, both.at[0], across, both.at[1]]
        copies = []
        for bit in range(parts):
            for step in range(size):
                index = (me ^ bit) * size + where_ref[step]
                row = pl.multiple_of(index * share, share)
                for i in range(pieces):
                    copies.append(
                        pltpu.make_async_copy(
                            ins[bit].at[step, pl.ds(0, share), pl.ds(i * piece, piece)],
                            outs[i].at[pl.ds(row, share)],
                            sems.at[i, bit, step],
                        )
                    )
                if more:
                    copies.append(
                        pltpu.make_async_copy(
                            ins[bit].at[step, pl.ds(share, more)],
                            outs[pieces].at[index],
                            sems.at[pieces, bit, step],
                        )
                    )
        begin(copies)
        finish(copies)

    shapes = [shaped((parts * size * share, piece))] * pieces
    if more:
        shapes.append(shaped((parts * size, more, width)))
    return pl.pallas_call(
        kernel,
        out_shape=tuple(shapes),
        in_specs=[SMEM] + [ANY] * 3,
        out_specs=(VMEM,) * len(shapes),
        scratch_shapes=[pltpu.SemaphoreType.DMA((pieces + 1, parts, size))],
        compiler_params=PARAMS,
        name="arrange",
        cost_estimate=cost(2),
    )(where, *slots)


def token_copies(refs, whole, sems):
    own, both, across = refs
    rows = own.shape[0]
    pairs = ((own, 0), (both.at[0], 1), (across, 2), (both.at[1], 3))
    return [
        pltpu.make_async_copy(ref, whole.at[pl.ds(i * rows, rows)], sems.at[i]) for ref, i in pairs
    ]


def weight_copies(where_ref, ref, m, whole, sems):
    size, parts, _, share, _ = ref.shape
    me = where_ref[size + 1]
    copies = []
    for c in range(size):
        for bit in range(parts):
            row = pl.multiple_of(((me ^ bit) * size + c) * share, share)
            copies.append(
                pltpu.make_async_copy(
                    ref.at[c, bit, m], whole.at[pl.ds(row, share)], sems.at[c * parts + bit]
                )
            )
    return copies


def ffn(where, tokens, pulled, weights):
    rows, model = tokens[0].shape
    size, parts, count, share, width = weights.shape
    total = rows * parts
    tall = model // parts

    def kernel(where_ref, *refs):
        weights_ref = refs[6]
        sums, grads = refs[7:11], refs[11]
        left, w_gate, w_up, w_down, right, back, stage = refs[12:19]
        sem_h, sem_c, sem_g, sem_u, sem_d, sem_s, sem_o = refs[19:]
        me = where_ref[size + 1]
        gates = weight_copies(where_ref, weights_ref, 0, w_gate, sem_g)
        reads = token_copies(refs[:3], left.at[0], sem_h)
        ups = weight_copies(where_ref, weights_ref, 1, w_up, sem_u)
        pulls = token_copies(refs[3:6], left.at[1], sem_c)
        downs = weight_copies(where_ref, weights_ref, 2, w_down, sem_d)
        for copies in (gates, reads, ups, pulls, downs):
            begin(copies)

        def sum_copies(i):
            return [
                pltpu.make_async_copy(
                    back.at[j, pl.ds((2 * i + odd) * rows, rows)],
                    sums[2 * j + odd].at[i],
                    sem_s.at[j, 2 * i + odd],
                )
                for j in (0, 1)
                for odd in (0, 1)
            ]

        def token_part(i, carry):
            at = pl.ds(pl.multiple_of(i * 2 * rows, 2 * rows), 2 * rows)

            @pl.when(i == 0)
            def _():
                finish(gates)
                finish(reads)

            g = jnp.dot(left[0, at], w_gate[...], preferred_element_type=jnp.float32)

            @pl.when(i == 0)
            def _():
                finish(ups)

            u = jnp.dot(left[0, at], w_up[...], preferred_element_type=jnp.float32)
            sigma = jax.nn.sigmoid(g)
            active = g * sigma
            right[2, at] = (active * u).astype(LOW)

            @pl.when(i == 0)
            def _():
                finish(pulls)
                finish(downs)

            d = jnp.dot(left[1, at], w_down[...], preferred_element_type=jnp.float32)
            right[0, at] = (d * u * sigma * (1.0 + g * (1.0 - sigma))).astype(LOW)
            right[1, at] = (d * active).astype(LOW)
            back[0, at] = (
                contract_cols(right[0, at], w_gate[...]) + contract_cols(right[1, at], w_up[...])
            ).astype(LOW)
            back[1, at] = contract_cols(right[2, at], w_down[...]).astype(LOW)
            begin(sum_copies(i))
            return carry

        lax.fori_loop(0, parts // 2, token_part, 0)

        def write(i, c):
            return pltpu.make_async_copy(
                stage.at[i, pl.ds(c * share, share)],
                grads.at[c, me ^ lax.rem(i, parts), i // parts],
                sem_o.at[i, c],
            )

        def block(i, carry):
            m, part = i // parts, lax.rem(i, parts)
            column = pl.multiple_of(part * tall, tall)
            stage[i] = contract_rows(left[m // 2, :, pl.ds(column, tall)], right[m]).astype(LOW)
            for c in range(size):
                write(i, c).start()
            return carry

        lax.fori_loop(0, count * parts, block, 0)

        def drain(i, carry):
            for c in range(size):
                write(i, c).wait()
            return carry

        lax.fori_loop(0, count * parts, drain, 0)

        def drain_sums(i, carry):
            finish(sum_copies(i))
            return carry

        lax.fori_loop(0, parts // 2, drain_sums, 0)

    return pl.pallas_call(
        kernel,
        out_shape=(shaped((2, rows, model)),) * 4 + (shaped((size, parts, count, share, width)),),
        in_specs=[SMEM] + [ANY] * 7,
        out_specs=(ANY,) * 5,
        scratch_shapes=[pltpu.VMEM((2, total, model), LOW)]
        + [pltpu.VMEM((model, width), LOW)] * 3
        + [
            pltpu.VMEM((3, total, width), LOW),
            pltpu.VMEM((2, total, model), LOW),
            pltpu.VMEM((count * parts, tall, width), LOW),
        ]
        + [pltpu.SemaphoreType.DMA((4,))] * 2
        + [pltpu.SemaphoreType.DMA((size * parts,))] * 3
        + [pltpu.SemaphoreType.DMA((2, parts)), pltpu.SemaphoreType.DMA((count * parts, size))],
        compiler_params=PARAMS,
        name="ffn",
        cost_estimate=cost(37),
    )(where, *tokens, *pulled, weights)


def head_grads(where, lefts, rights, gains=None, small=0, later=()):
    count = len(lefts)
    model = lefts[0].shape[1]
    each = rights[0].shape[1]
    width = each * count
    size = where.shape[0] - 2
    parts = 4
    tall = model // parts
    share = tall // size
    pad = 16 if gains else 0
    gains = gains or []

    def kernel(where_ref, *refs):
        left_refs, right_refs, refs = refs[:count], refs[count : 2 * count], refs[2 * count :]
        *gain_refs, keep, send, stage, sems = refs[: len(gains)] + refs[len(gains) + len(later) :]
        me = where_ref[size + 1]
        here = where_ref[size]

        def block(part, carry):
            column = pl.multiple_of(part * tall, tall)
            for m in range(count):
                grads = contract_rows(
                    left_refs[m][:, pl.ds(column, tall)], right_refs[m][...]
                ).astype(LOW)
                for c in range(size):
                    stage[part * size + c, :share, m * each : (m + 1) * each] = grads[
                        c * share : (c + 1) * share
                    ]
            return carry

        lax.fori_loop(0, parts, block, 0)
        if pad:
            pairs = [gain[:, :HEAD] + gain[:, HEAD:] for gain in gain_refs[2:4]]
            for i in range(parts * size):
                pieces = [gain[:, i * share : (i + 1) * share] for gain in gain_refs[:2]]
                pieces += [pair[:, i * small : (i + 1) * small] for pair in pairs]
                row = jnp.concatenate(
                    [
                        jnp.concatenate(
                            [piece, jnp.zeros((1, 128 - piece.shape[1]), jnp.float32)], axis=1
                        )
                        for piece in pieces
                    ],
                    axis=1,
                )
                stage[i, share:] = jnp.broadcast_to(row, (pad, width)).astype(LOW)

        def each_copy(do):
            for part in range(parts):
                bit = me ^ part
                for odd, out in ((0, keep), (1, send)):

                    @pl.when(lax.rem(bit, 2) == odd)
                    def _():
                        for c in range(size):
                            step = lax.rem(here - c + size, size) if size <= LINE else c
                            i = part * size + c
                            do(
                                pltpu.make_async_copy(
                                    stage.at[i], out.at[bit // 2, step], sems.at[i]
                                )
                            )

        each_copy(lambda copy: copy.start())
        each_copy(lambda copy: copy.wait())

    return pl.pallas_call(
        kernel,
        out_shape=(shaped((2, size, share + pad, width)),) * 2,
        in_specs=[SMEM] + [VMEM] * (2 * count + len(gains)) + [ANY] * len(later),
        out_specs=(ANY,) * 2,
        scratch_shapes=[
            pltpu.VMEM((parts * size, share + pad, width), LOW),
            pltpu.SemaphoreType.DMA((parts * size,)),
        ],
        compiler_params=PARAMS,
        name="head_grads",
        cost_estimate=cost(3),
    )(where, *lefts, *rights, *gains, *later)


def flip(part, bit):
    size = lax.axis_size("fsdp")
    return lax.ppermute(part, "fsdp", [(i, i ^ bit) for i in range(size)])


def swap(part):
    return lax.ppermute(part, "tp", [(0, 1), (1, 0)])


def turn(part):
    size = lax.axis_size("ctx")
    return lax.ppermute(part, "ctx", [(i, (i + 1) % size) for i in range(size)])


def ctx_slots(part):
    size = lax.axis_size("ctx")
    if size > LINE:
        whole = lax.all_gather(part, "ctx", axis=0)
        return [whole[i] for i in range(size)]
    slots = [part]
    for _ in range(1, size):
        slots.append(turn(slots[-1]))
    return slots


def ctx_sum(terms):
    size = lax.axis_size("ctx")
    if size > LINE:
        return lax.psum_scatter(terms, "ctx", scatter_dimension=0, tiled=False).astype(jnp.float32)
    moving = terms[1]
    for step in range(1, size):
        total = turn(moving).astype(jnp.float32) + terms[(step + 1) % size].astype(jnp.float32)
        moving = total.astype(LOW)
    return total


def ctx_sum_direct(terms):
    size = lax.axis_size("ctx")
    if size > LINE:
        return ctx_sum(terms)
    total = terms[0].astype(jnp.float32)
    for step in range(1, size):
        part = lax.ppermute(terms[step], "ctx", [(i, (i - step) % size) for i in range(size)])
        total = total + part.astype(jnp.float32)
    return total


def back_slots(part):
    size = lax.axis_size("ctx")
    if size > LINE:
        whole = lax.all_gather(part, "ctx", axis=0)
        return [whole[i] for i in range(size)]
    slots = [part]
    for step in range(1, size):
        slots.append(lax.ppermute(part, "ctx", [(i, i + step) for i in range(size - step)]))
    return slots


def back_sum(terms):
    size = lax.axis_size("ctx")
    if size > LINE:
        total = lax.psum_scatter(jnp.stack(terms), "ctx", scatter_dimension=0, tiled=False)
        return total.astype(jnp.float32), total
    parts = [terms[0]] + [
        lax.ppermute(terms[step], "ctx", [(i, i - step) for i in range(step, size)])
        for step in range(1, size)
    ]
    return sum(part.astype(jnp.float32) for part in parts), parts[1]


def group_tokens(part):
    across = flip(part, 2)
    return (part, flip(collect([part, across]), 1), across)


def chip_sum(keep, send):
    beside = flip(send, 1)
    far = keep[1].astype(jnp.float32) + beside[1].astype(jnp.float32)
    near = keep[0].astype(jnp.float32) + beside[0].astype(jnp.float32)
    return near, far.astype(LOW)


def pair_sum(near, far):
    return near + flip(far, 2).astype(jnp.float32)


def group_sum(keep, send):
    return pair_sum(*chip_sum(keep, send))


def gather_all(where, slots, share, later=()):
    own = collect(slots, later)
    across = flip(own, 2)
    both = flip(collect([own, across]), 1)
    return arrange(where, [own, both, across], share, 1), across


def scatter_hidden(terms):
    size, parts, count, share, width = terms.shape
    own = lax.psum_scatter(terms.reshape(-1, width), "ctx", scatter_dimension=0, tiled=True)
    own = own.reshape(parts, count, share, width)
    return own, [own[0]] + [flip(own[bit], bit) for bit in range(1, parts)]


def body(
    inputs,
    cotangent,
    doc_bounds,
    attn_gain,
    w_query,
    w_key,
    w_value,
    w_output,
    query_gain,
    key_gain,
    ffn_gain,
    w_gate,
    w_up,
    w_down,
):
    parts = lax.axis_size("fsdp")
    size = lax.axis_size("ctx")
    tensor = lax.axis_size("tp")
    me = lax.axis_index("ctx")
    share = w_query.shape[0]
    model = share * parts * size
    width = HQ // tensor * HEAD
    kv_width = HK // tensor * HEAD
    small = query_gain.shape[0]
    shards = parts * size
    steps = jnp.arange(size, dtype=jnp.int32)
    slots_at = lax.rem(me - steps + size, size) if size <= LINE else steps
    where = jnp.concatenate(
        [slots_at, jnp.stack([me, lax.axis_index("fsdp")]).astype(jnp.int32)]
    )
    bounds = doc_bounds[0]

    split = split_columns(where, [w_gate, w_up, w_down.T])
    gains = jnp.concatenate([attn_gain, ffn_gain, query_gain, key_gain])
    pad = 16
    gain_rows = jnp.zeros((pad, 2 * kv_width), LOW).at[0, : gains.shape[0]].set(gains)
    kv_block = jnp.concatenate([jnp.concatenate([w_key, w_value], axis=1), gain_rows], axis=0)
    traded = [
        [part[0]] + [flip(part[bit], bit) for bit in range(1, parts)] for part in split
    ]
    kv_slots = ctx_slots(kv_block)
    query_slots = ctx_slots(w_query)
    output_slots = ctx_slots(w_output.T)
    (full_kv, gain_rows), kv_across = gather_all(where, kv_slots, share)
    (full_query,), query_across = gather_all(where, query_slots, share, [kv_across])
    (full_output,), output_across = gather_all(where, output_slots, share, [query_across])
    weights = []
    for chunk in traded:
        block = collect(chunk, [kv_slots[-1]])
        weights.append(
            lax.all_gather(
                block.reshape(-1, block.shape[-1]), "ctx", axis=0, tiled=True
            ).reshape(size, *block.shape)
        )
    pulled_all = group_tokens(collect([cotangent[0]], [output_across])[0])
    all_gains = gain_rows[:, 0].astype(jnp.float32)
    gain_attn = all_gains[:, :share].reshape(model)
    gain_ffn = all_gains[:, share : 2 * share].reshape(model)
    gain_query = jnp.tile(all_gains[:, 2 * share : 2 * share + small].reshape(HEAD), 2)[None]
    gain_key = jnp.tile(
        all_gains[:, 2 * share + small : 2 * share + 2 * small].reshape(HEAD), 2
    )[None]

    pulled = cotangent[0]

    tokens = inputs[0].astype(jnp.float32)
    rows = tokens.shape[0]
    cosine, sine = tables(me * rows, rows, bounds)
    first_inv = inverse_rms(tokens)
    normed = (tokens * first_inv * gain_attn).astype(LOW)
    keys_values = jnp.dot(normed, full_kv, preferred_element_type=jnp.float32)
    own_kv = prepare_keys(keys_values, gain_key, cosine, sine)
    kv = back_slots(own_kv)
    queries = jnp.dot(normed, full_query, preferred_element_type=jnp.float32)
    query_rot, mixed_low, mixed = attend(where, bounds, queries, kv, gain_query, cosine, sine)
    branch_part = contract_cols(mixed_low, full_output).astype(LOW)
    branch = branch_part.astype(jnp.float32) + swap(branch_part).astype(jnp.float32)
    hidden = tokens + branch
    second_inv = inverse_rms(hidden)
    hidden_normed = (hidden * second_inv * gain_ffn).astype(LOW)

    hidden_all = group_tokens(hidden_normed)
    keep, send, keep_out, send_out, terms = ffn(where, hidden_all, pulled_all, weights[0])
    near, far = chip_sum(keep, send)
    normed_part = pair_sum(near, far).astype(LOW)
    hidden_sum, traded_back = scatter_hidden(terms)
    grad_gate, grad_up, grad_down = join_columns(where, [traded_back])
    grad_down = grad_down.T
    grad_normed_ffn = normed_part.astype(jnp.float32) + swap(normed_part).astype(jnp.float32)

    ffn_gain_part = jnp.sum(grad_normed_ffn * hidden * second_inv, axis=0) * 0.5
    grad_hidden = pulled.astype(jnp.float32) + norm_back(
        hidden, second_inv, gain_ffn, grad_normed_ffn
    )
    grad_hidden_low = grad_hidden.astype(LOW)
    grad_mixed = jnp.dot(
        grad_hidden_low, full_output, preferred_element_type=jnp.float32
    ).astype(LOW)
    grad_query_low, *key_terms, query_gain_pair = attend_back(
        where, bounds, queries, query_rot, grad_mixed, mixed, kv, gain_query, cosine, sine,
        [terms],
    )
    near, far = chip_sum(
        *head_grads(where, [normed, grad_hidden_low], [grad_query_low, mixed_low])
    )
    heads_sum = ctx_sum(pair_sum(near, far).astype(LOW))
    moved = collect(key_terms[1:], [far])
    own_terms, _ = back_sum([key_terms[0]] + [moved[i] for i in range(size - 1)])
    grad_query = heads_sum[:, :width]
    grad_output = heads_sum[:, width:].T
    feed_part = group_sum(keep_out, collect([send_out], [grad_hidden_low])[0]).astype(LOW)
    feed = feed_part.astype(jnp.float32) + swap(feed_part).astype(jnp.float32)
    result = (hidden + feed).astype(LOW)[None]
    grad_kv_low, key_gain_pair = keys_back(
        keys_values,
        own_terms,
        gain_key,
        cosine,
        sine,
    )
    normed_low, attn_gain_part = normed_back(
        grad_query_low, grad_kv_low, full_query, full_kv, inputs[0], first_inv
    )
    near, far = chip_sum(
        *head_grads(
            where,
            [normed],
            [grad_kv_low],
            [attn_gain_part, ffn_gain_part[None], query_gain_pair, key_gain_pair],
            small,
        )
    )
    kv_sum = pair_sum(near, far).astype(LOW)
    own_kv = ctx_sum_direct(collect([kv_sum], [hidden_sum])[0])
    grad_key = own_kv[:share, :kv_width]
    grad_value = own_kv[:share, kv_width:]
    normed_low = collect([normed_low], [far])[0]
    grad_normed = normed_low.astype(jnp.float32) + swap(normed_low).astype(jnp.float32)
    own_gains = own_kv[share].astype(LOW)
    grad_gains = own_gains.astype(jnp.float32) + swap(own_gains).astype(jnp.float32)
    grad_inputs = grad_hidden + norm_back(tokens, first_inv, gain_attn, grad_normed)
    return (
        result,
        grad_inputs[None],
        grad_gains[:share],
        grad_query,
        grad_key,
        grad_value,
        grad_output,
        grad_gains[256 : 256 + small],
        grad_gains[384 : 384 + small],
        grad_gains[128 : 128 + share],
        grad_gate,
        grad_up,
        grad_down,
    )


def solution(mesh):
    vector = P(("fsdp", "ctx"))
    columns = P(("fsdp", "ctx"), "tp")
    tall = P("tp", ("fsdp", "ctx"))
    act = P("fsdp", "ctx", None)
    return jax.shard_map(
        body,
        mesh=mesh,
        in_specs=(
            act,
            act,
            P("fsdp", None),
            vector,
            columns,
            columns,
            columns,
            tall,
            vector,
            vector,
            vector,
            columns,
            columns,
            tall,
        ),
        out_specs=(
            act,
            act,
            vector,
            columns,
            columns,
            columns,
            tall,
            vector,
            vector,
            vector,
            columns,
            columns,
            tall,
        ),
        check_vma=False,
    )
```

```python
import functools
import math

import jax
import jax.numpy as jnp
from jax import lax
from jax.experimental import pallas as pl
from jax.experimental.pallas import tpu as pltpu
from jax.sharding import PartitionSpec as P

HQ = 24
HK = 8
HEAD = 64
GROUP = HQ // HK


EPS = 1e-05
THETA = 1000000.0
LINE = 4
LOG2E = math.log2(math.e)
LOW = jnp.bfloat16
VMEM = pl.BlockSpec(memory_space=pltpu.VMEM)
SMEM = pl.BlockSpec(memory_space=pltpu.SMEM)
ANY = pl.BlockSpec(memory_space=pl.ANY)
PARAMS = pltpu.CompilerParams(vmem_limit_bytes=52 * 1024 * 1024)


def inverse_rms(values):
    return lax.rsqrt(jnp.mean(values * values, axis=-1, keepdims=True) + EPS)


def norm_back(values, inverse, gain, grads):
    scaled = grads * gain
    return inverse * scaled - values * (inverse * inverse * inverse) * jnp.mean(
        scaled * values, axis=-1, keepdims=True
    )


def contract_rows(left, right):
    return lax.dot_general(
        left, right, (((0,), (0,)), ((), ())), preferred_element_type=jnp.float32
    )


def contract_cols(left, right):
    return lax.dot_general(
        left, right, (((1,), (1,)), ((), ())), preferred_element_type=jnp.float32
    )


def tables(first, rows, bounds):
    index = first + jnp.arange(rows, dtype=jnp.int32)
    begin = jnp.where(index >= bounds[1], bounds[1], jnp.where(index >= bounds[0], bounds[0], 0))
    freq = THETA ** (-(jnp.arange(HEAD // 2, dtype=jnp.float32) * 2.0 / HEAD))
    angle = (index - begin).astype(jnp.float32)[:, None] * freq[None, :]
    cosine = jnp.cos(angle)
    sine = jnp.sin(angle)
    return (
        jnp.concatenate([cosine, cosine, cosine, cosine], axis=1),
        jnp.concatenate([-sine, sine, -sine, sine], axis=1),
    )


def shaped(shape, dtype=LOW):
    return jax.ShapeDtypeStruct(shape, dtype)


def cost(micros):
    return pl.CostEstimate(
        flops=int(micros * 900000000.0), bytes_accessed=int(micros * 1000000.0), transcendentals=0
    )


def pair_inverse(x):
    lane=lax.broadcasted_iota(jnp.int32,x.shape,1)
    left=lane<HEAD
    sq=x*x
    a=jnp.sum(jnp.where(left,sq,0.0),axis=-1,keepdims=True)
    b=jnp.sum(jnp.where(left,0.0,sq),axis=-1,keepdims=True)
    return lax.rsqrt(jnp.where(left,a,b)*(1.0/HEAD)+EPS)

def pair_mean(x):
    lane=lax.broadcasted_iota(jnp.int32,x.shape,1)
    left=lane<HEAD
    a=jnp.sum(jnp.where(left,x,0.0),axis=-1,keepdims=True)
    b=jnp.sum(jnp.where(left,0.0,x),axis=-1,keepdims=True)
    return jnp.where(left,a,b)*(1.0/HEAD)

def partner(x):
    lane=lax.broadcasted_iota(jnp.int32,x.shape,1)
    front=lax.rem(lane,HEAD)<HEAD//2
    return jnp.where(front,pltpu.roll(x,2*HEAD-HEAD//2,1),pltpu.roll(x,HEAD//2,1))

def kprep_kernel(kv_ref,gain_ref,cos_ref,sin_ref,out_ref):
    width=kv_ref.shape[1]//2
    for i in range(width//128):
        x=kv_ref[:,128*i:128*(i+1)]
        xn=x*pair_inverse(x)*gain_ref[...]
        out_ref[:,128*i:128*(i+1)]=(xn*cos_ref[...]+partner(xn)*sin_ref[...]).astype(jnp.bfloat16)
    out_ref[:,width:]=kv_ref[:,width:].astype(jnp.bfloat16)

def bias_of(first_key,first_row,bounds_ref,keys,rows):
    key=first_key+lax.broadcasted_iota(jnp.int32,(keys,rows),0)
    row=first_row+lax.broadcasted_iota(jnp.int32,(keys,rows),1)
    b0=bounds_ref[0]; b1=bounds_ref[1]
    begin=jnp.where(row>=b1,b1,jnp.where(row>=b0,b0,0))
    return jnp.where((key<=row)&(key>=begin),0.0,-1e30)

def fwd_kernel(slots, where_ref, bounds_ref, q_ref, *refs):
    kv_refs = refs[:slots]
    gain_ref, cos_ref, sin_ref, qr_ref, ob_ref, oT_ref, qs, ks, vs, bias = refs[slots:]
    rows, width = kv_refs[0].shape
    width //= 2
    heads = q_ref.shape[1] // HEAD
    kvh = width // HEAD
    me = where_ref[slots]
    for i in range(heads // 2):
        at = slice(2 * HEAD * i, 2 * HEAD * (i + 1))
        x = q_ref[:, at]
        xn = x * pair_inverse(x) * gain_ref[...]
        qr_ref[:, at] = (xn * cos_ref[...] + partner(xn) * sin_ref[...]).astype(LOW)
    for h in range(heads):
        qs[h // GROUP, (h % GROUP) * rows : (h % GROUP + 1) * rows] = qr_ref[
            :, HEAD * h : HEAD * (h + 1)
        ]
    for j in range(slots):
        for k in range(kvh):
            ks[j * kvh + k] = kv_refs[j][:, HEAD * k : HEAD * (k + 1)]
            vT = kv_refs[j][:, width + HEAD * k : width + HEAD * (k + 1)].astype(jnp.float32).T
            vs[j * kvh + k] = jnp.concatenate([vT, jnp.ones_like(vT)], axis=0).astype(LOW)
    oT_ref[...] = jnp.zeros_like(oT_ref)

    def step(j, carry):
        c = where_ref[j]

        @pl.when((c <= me) & (c >= 0))
        def _():
            mask = bias_of(c * rows, me * rows, bounds_ref, rows, rows)
            for g in range(GROUP):
                bias[:, g * rows : (g + 1) * rows] = mask
            for k in range(kvh):
                s = contract_cols(ks[j * kvh + k], qs[k])
                p = jnp.exp2(s * (0.125 * LOG2E) + bias[...]).astype(LOW)
                oT_ref[k] += jnp.dot(vs[j * kvh + k], p, preferred_element_type=jnp.float32)

        return carry

    lax.fori_loop(0, slots, step, 0)
    for k in range(kvh):
        oT = oT_ref[k, :HEAD, :] * (1.0 / oT_ref[k, HEAD : HEAD + 1, :])
        oT_ref[k, :HEAD, :] = oT
        for g in range(GROUP):
            h = k * GROUP + g
            ob_ref[:, HEAD * h : HEAD * (h + 1)] = oT[:, g * rows : (g + 1) * rows].T.astype(LOW)


def bwd_kernel(slots, where_ref, bounds_ref, q_ref, qr_ref, dob_ref, oT_ref, *refs):
    kv_refs = refs[:slots]
    gain_ref, cos_ref, sin_ref, _, dqb_ref = refs[slots : slots + 5]
    dkv_refs = refs[slots + 5 : 2 * slots + 5]
    gg_ref, qs, ds_, ks, vs, kTs, dks, dvs, logl, delta, dqT, bias = refs[2 * slots + 5 :]
    rows, width = kv_refs[0].shape
    width //= 2
    heads = q_ref.shape[1] // HEAD
    kvh = width // HEAD
    me = where_ref[slots]
    for h in range(heads):
        k, g = h // GROUP, h % GROUP
        at = slice(g * rows, (g + 1) * rows)
        qs[k, at] = qr_ref[:, HEAD * h : HEAD * (h + 1)]
        d = dob_ref[:, HEAD * h : HEAD * (h + 1)]
        ds_[k, at] = d
        dT = d.astype(jnp.float32).T
        delta[k, :, at] = jnp.broadcast_to(
            jnp.sum(dT * oT_ref[k, :HEAD, at], axis=0, keepdims=True), (8, rows)
        )
    for k in range(kvh):
        logl[k] = jnp.broadcast_to(jnp.log2(oT_ref[k, HEAD : HEAD + 1, :]), logl.shape[1:])
    for j in range(slots):
        for k in range(kvh):
            t = j * kvh + k
            kb = kv_refs[j][:, HEAD * k : HEAD * (k + 1)]
            ks[t] = kb
            vs[t] = kv_refs[j][:, width + HEAD * k : width + HEAD * (k + 1)]
            kTs[t] = kb.astype(jnp.float32).T.astype(LOW)
    dqT[...] = jnp.zeros_like(dqT)

    def step(j, carry):
        c = where_ref[j]
        seen = (c <= me) & (c >= 0)

        @pl.when(seen)
        def _():
            mask = bias_of(c * rows, me * rows, bounds_ref, rows, rows)
            for g in range(GROUP):
                bias[:, g * rows : (g + 1) * rows] = mask
            for k in range(kvh):
                t = j * kvh + k
                s = contract_cols(ks[t], qs[k])
                dp = contract_cols(vs[t], ds_[k])
                p = jnp.exp2(s * (0.125 * LOG2E) + (bias[...] - logl[k, 0:1]))
                ds = (p * (dp - delta[k, 0:1])).astype(LOW)
                dvs[t] = jnp.dot(p.astype(LOW), ds_[k], preferred_element_type=jnp.float32).astype(LOW)
                dk = jnp.dot(ds, qs[k], preferred_element_type=jnp.float32)
                dks[t] = (dk * 0.125).astype(LOW)
                dqT[k] += jnp.dot(kTs[t], ds, preferred_element_type=jnp.float32)

        @pl.when(jnp.logical_not(seen))
        def _():
            for k in range(kvh):
                dks[j * kvh + k] = jnp.zeros((rows, HEAD), LOW)
                dvs[j * kvh + k] = jnp.zeros((rows, HEAD), LOW)

        return carry

    lax.fori_loop(0, slots, step, 0)
    for j in range(slots):
        for k in range(kvh):
            t = j * kvh + k
            dkv_refs[j][:, HEAD * k : HEAD * (k + 1)] = dks[t]
            dkv_refs[j][:, width + HEAD * k : width + HEAD * (k + 1)] = dvs[t]
    gg = jnp.zeros((1, 2 * HEAD), jnp.float32)
    for i in range(heads // 2):
        at = slice(2 * HEAD * i, 2 * HEAD * (i + 1))
        pair = []
        for h in (2 * i, 2 * i + 1):
            k, g = h // GROUP, h % GROUP
            pair.append(dqT[k, :, g * rows : (g + 1) * rows].T * 0.125)
        d = jnp.concatenate(pair, axis=1)
        x = q_ref[:, at]
        inv = pair_inverse(x)
        dn = d * cos_ref[...] - partner(d) * sin_ref[...]
        gg += jnp.sum(dn * x * inv, axis=0, keepdims=True)
        sc = dn * gain_ref[...]
        dqb_ref[:, at] = (inv * sc - x * (inv * inv * inv) * pair_mean(sc * x)).astype(LOW)
    gg_ref[...] = gg


def kback_kernel(kv_ref, d_ref, gain_ref, cos_ref, sin_ref, *refs):
    out_ref, gg_ref = refs[-2:]
    width = kv_ref.shape[1] // 2
    gg = jnp.zeros((1, 2 * HEAD), jnp.float32)
    for i in range(width // (2 * HEAD)):
        at = slice(2 * HEAD * i, 2 * HEAD * (i + 1))
        x = kv_ref[:, at]
        d = d_ref[:, at]
        inv = pair_inverse(x)
        dn = d * cos_ref[...] - partner(d) * sin_ref[...]
        gg += jnp.sum(dn * x * inv, axis=0, keepdims=True)
        sc = dn * gain_ref[...]
        out_ref[:, at] = (inv * sc - x * (inv * inv * inv) * pair_mean(sc * x)).astype(LOW)
    out_ref[:, width:] = d_ref[:, width:].astype(LOW)
    gg_ref[...] = gg


def prepare_keys(kv, gain, cosine, sine):
    return pl.pallas_call(
        kprep_kernel,
        out_shape=shaped(kv.shape),
        in_specs=[VMEM] * 4,
        out_specs=VMEM,
        compiler_params=PARAMS,
        name="keys",
        cost_estimate=cost(1),
    )(kv, gain, cosine, sine)


def attend(where, bounds, q, kv, gain, cosine, sine):
    slots = len(kv)
    rows, width = kv[0].shape
    heads = width // 2 // HEAD
    return pl.pallas_call(
        functools.partial(fwd_kernel, slots),
        out_shape=(
            shaped(q.shape),
            shaped(q.shape),
            shaped((heads, 2 * HEAD, GROUP * rows), jnp.float32),
        ),
        in_specs=[SMEM, SMEM] + [VMEM] * (4 + slots),
        out_specs=(VMEM,) * 3,
        scratch_shapes=[
            pltpu.VMEM((heads, GROUP * rows, HEAD), LOW),
            pltpu.VMEM((slots * heads, rows, HEAD), LOW),
            pltpu.VMEM((slots * heads, 2 * HEAD, rows), LOW),
            pltpu.VMEM((rows, GROUP * rows), jnp.float32),
        ],
        compiler_params=PARAMS,
        name="attend",
        cost_estimate=cost(14),
    )(where, bounds, q, *kv, gain, cosine, sine)


def attend_back(where, bounds, q, qr, dob, mixed, kv, gain, cosine, sine, later):
    slots = len(kv)
    rows, width = kv[0].shape
    heads = width // 2 // HEAD
    return pl.pallas_call(
        functools.partial(bwd_kernel, slots),
        out_shape=(shaped(q.shape),)
        + (shaped(kv[0].shape),) * slots
        + (shaped((1, 2 * HEAD), jnp.float32),),
        in_specs=[SMEM, SMEM] + [VMEM] * (7 + slots) + [ANY],
        out_specs=(VMEM,) * (2 + slots),
        scratch_shapes=[
            pltpu.VMEM((heads, GROUP * rows, HEAD), LOW),
            pltpu.VMEM((heads, GROUP * rows, HEAD), LOW),
            pltpu.VMEM((slots * heads, rows, HEAD), LOW),
            pltpu.VMEM((slots * heads, rows, HEAD), LOW),
            pltpu.VMEM((slots * heads, HEAD, rows), LOW),
            pltpu.VMEM((slots * heads, rows, HEAD), LOW),
            pltpu.VMEM((slots * heads, rows, HEAD), LOW),
            pltpu.VMEM((heads, 8, GROUP * rows), jnp.float32),
            pltpu.VMEM((heads, 8, GROUP * rows), jnp.float32),
            pltpu.VMEM((heads, HEAD, GROUP * rows), jnp.float32),
            pltpu.VMEM((rows, GROUP * rows), jnp.float32),
        ],
        compiler_params=PARAMS,
        name="attend_back",
        cost_estimate=cost(17),
    )(where, bounds, q, qr, dob, mixed, *kv, gain, cosine, sine, *later)


def keys_back(kv, grads, gain, cosine, sine, later=()):
    return pl.pallas_call(
        kback_kernel,
        out_shape=(shaped(kv.shape), shaped((1, 2 * HEAD), jnp.float32)),
        in_specs=[VMEM] * 5 + [ANY] * len(later),
        out_specs=(VMEM,) * 2,
        compiler_params=PARAMS,
        name="keys_back",
        cost_estimate=cost(1),
    )(kv, grads, gain, cosine, sine, *later)


def normed_back(grad_query, grad_kv, query, kv, tokens, inverse):
    def kernel(dq, dkv, wq, wkv, x, inv, out, gain):
        terms = contract_cols(dq[...], wq[...]) + contract_cols(dkv[...], wkv[...])
        out[...] = terms.astype(LOW)
        gain[...] = jnp.sum(
            terms * (x[...].astype(jnp.float32) * inv[...]), axis=0, keepdims=True
        )

    rows, model = tokens.shape
    return pl.pallas_call(
        kernel,
        out_shape=(shaped((rows, model)), shaped((1, model), jnp.float32)),
        in_specs=[VMEM] * 6,
        out_specs=(VMEM,) * 2,
        compiler_params=PARAMS,
        name="normed_back",
        cost_estimate=cost(4),
    )(grad_query, grad_kv, query, kv, tokens, inverse)


def begin(copies):
    for copy in copies:
        copy.start()


def finish(copies):
    for copy in copies:
        copy.wait()


def collect(parts, later=()):
    count = len(parts)

    def kernel(*refs):
        out, sems = refs[-2:]
        copies = [pltpu.make_async_copy(refs[i], out.at[i], sems.at[i]) for i in range(count)]
        begin(copies)
        finish(copies)

    return pl.pallas_call(
        kernel,
        out_shape=shaped((count,) + parts[0].shape, parts[0].dtype),
        in_specs=[ANY] * (count + len(later)),
        out_specs=VMEM,
        scratch_shapes=[pltpu.SemaphoreType.DMA((count,))],
        compiler_params=PARAMS,
        name="collect",
        cost_estimate=cost(1),
    )(*parts, *later)


def chunks_of(width):
    return ((0, width),)


def split_columns(where, weights):
    count = len(weights)
    share, width = weights[0].shape
    parts = 4
    width //= parts
    chunks = chunks_of(width)

    def kernel(where_ref, *refs):
        me = where_ref[where.shape[0] - 1]
        ins, outs = refs[:count], refs[count:]
        for column in range(parts):
            for bit in range(parts):

                @pl.when(column ^ bit == me)
                def _():
                    for j, (begin, end) in enumerate(chunks):
                        at = slice(column * width + begin, column * width + end)
                        for i in range(count):
                            outs[j * parts + bit][i] = ins[i][:, at]

    outs = pl.pallas_call(
        kernel,
        out_shape=tuple(
            shaped((count, share, end - begin)) for begin, end in chunks for _ in range(parts)
        ),
        in_specs=[SMEM] + [VMEM] * count,
        out_specs=(VMEM,) * (parts * len(chunks)),
        compiler_params=PARAMS,
        name="split_columns",
        cost_estimate=cost(3),
    )(where, *weights)
    return [outs[j * parts : (j + 1) * parts] for j in range(len(chunks))]


def join_columns(where, slots):
    parts = len(slots[0])
    count, share, _ = slots[0][0].shape
    width = sum(chunk[0].shape[-1] for chunk in slots)
    chunks = chunks_of(width)

    def kernel(where_ref, *refs):
        me = where_ref[where.shape[0] - 1]
        ins, outs = refs[: parts * len(chunks)], refs[parts * len(chunks) :]
        for column in range(parts):
            for bit in range(parts):

                @pl.when(column ^ bit == me)
                def _():
                    for j, (begin, end) in enumerate(chunks):
                        at = slice(column * width + begin, column * width + end)
                        for i in range(count):
                            outs[i][:, at] = ins[j * parts + bit][i].astype(jnp.float32)

    return pl.pallas_call(
        kernel,
        out_shape=(shaped((share, width * parts), jnp.float32),) * count,
        in_specs=[SMEM] + [VMEM] * (parts * len(chunks)),
        out_specs=(VMEM,) * count,
        compiler_params=PARAMS,
        name="join_columns",
        cost_estimate=cost(4),
    )(where, *[part for chunk in slots for part in chunk])


def arrange(where, slots, share, pieces):
    own, both, across = slots
    size, rows, width = own.shape
    parts = 4
    more = rows - share
    piece = width // pieces

    def kernel(where_ref, *refs):
        me = where_ref[size + 1]
        own, both, across = refs[:3]
        outs, sems = refs[3:-1], refs[-1]
        ins = [own, both.at[0], across, both.at[1]]
        copies = []
        for bit in range(parts):
            for step in range(size):
                index = (me ^ bit) * size + where_ref[step]
                row = pl.multiple_of(index * share, share)
                for i in range(pieces):
                    copies.append(
                        pltpu.make_async_copy(
                            ins[bit].at[step, pl.ds(0, share), pl.ds(i * piece, piece)],
                            outs[i].at[pl.ds(row, share)],
                            sems.at[i, bit, step],
                        )
                    )
                if more:
                    copies.append(
                        pltpu.make_async_copy(
                            ins[bit].at[step, pl.ds(share, more)],
                            outs[pieces].at[index],
                            sems.at[pieces, bit, step],
                        )
                    )
        begin(copies)
        finish(copies)

    shapes = [shaped((parts * size * share, piece))] * pieces
    if more:
        shapes.append(shaped((parts * size, more, width)))
    return pl.pallas_call(
        kernel,
        out_shape=tuple(shapes),
        in_specs=[SMEM] + [ANY] * 3,
        out_specs=(VMEM,) * len(shapes),
        scratch_shapes=[pltpu.SemaphoreType.DMA((pieces + 1, parts, size))],
        compiler_params=PARAMS,
        name="arrange",
        cost_estimate=cost(2),
    )(where, *slots)


def token_copies(refs, whole, sems):
    own, both, across = refs
    rows = own.shape[0]
    pairs = ((own, 0), (both.at[0], 1), (across, 2), (both.at[1], 3))
    return [
        pltpu.make_async_copy(ref, whole.at[pl.ds(i * rows, rows)], sems.at[i]) for ref, i in pairs
    ]


def weight_copies(where_ref, ref, m, whole, sems):
    size, parts, _, share, _ = ref.shape
    me = where_ref[size + 1]
    copies = []
    for c in range(size):
        for bit in range(parts):
            row = pl.multiple_of(((me ^ bit) * size + c) * share, share)
            copies.append(
                pltpu.make_async_copy(
                    ref.at[c, bit, m], whole.at[pl.ds(row, share)], sems.at[c * parts + bit]
                )
            )
    return copies


def ffn(where, tokens, pulled, weights):
    rows, model = tokens[0].shape
    size, parts, count, share, width = weights.shape
    total = rows * parts
    tall = model // parts

    def kernel(where_ref, *refs):
        weights_ref = refs[6]
        sums, grads = refs[7:11], refs[11]
        left, w_gate, w_up, w_down, right, back, stage = refs[12:19]
        sem_h, sem_c, sem_g, sem_u, sem_d, sem_s, sem_o = refs[19:]
        me = where_ref[size + 1]
        gates = weight_copies(where_ref, weights_ref, 0, w_gate, sem_g)
        reads = token_copies(refs[:3], left.at[0], sem_h)
        ups = weight_copies(where_ref, weights_ref, 1, w_up, sem_u)
        pulls = token_copies(refs[3:6], left.at[1], sem_c)
        downs = weight_copies(where_ref, weights_ref, 2, w_down, sem_d)
        for copies in (gates, reads, ups, pulls, downs):
            begin(copies)

        def sum_copies(i):
            return [
                pltpu.make_async_copy(
                    back.at[j, pl.ds((2 * i + odd) * rows, rows)],
                    sums[2 * j + odd].at[i],
                    sem_s.at[j, 2 * i + odd],
                )
                for j in (0, 1)
                for odd in (0, 1)
            ]

        def token_part(i, carry):
            at = pl.ds(pl.multiple_of(i * 2 * rows, 2 * rows), 2 * rows)

            @pl.when(i == 0)
            def _():
                finish(gates)
                finish(reads)

            g = jnp.dot(left[0, at], w_gate[...], preferred_element_type=jnp.float32)

            @pl.when(i == 0)
            def _():
                finish(ups)

            u = jnp.dot(left[0, at], w_up[...], preferred_element_type=jnp.float32)
            sigma = jax.nn.sigmoid(g)
            active = g * sigma
            right[2, at] = (active * u).astype(LOW)

            @pl.when(i == 0)
            def _():
                finish(pulls)
                finish(downs)

            d = jnp.dot(left[1, at], w_down[...], preferred_element_type=jnp.float32)
            right[0, at] = (d * u * sigma * (1.0 + g * (1.0 - sigma))).astype(LOW)
            right[1, at] = (d * active).astype(LOW)
            back[0, at] = (
                contract_cols(right[0, at], w_gate[...]) + contract_cols(right[1, at], w_up[...])
            ).astype(LOW)
            back[1, at] = contract_cols(right[2, at], w_down[...]).astype(LOW)
            begin(sum_copies(i))
            return carry

        lax.fori_loop(0, parts // 2, token_part, 0)

        def write(i, c):
            return pltpu.make_async_copy(
                stage.at[i, pl.ds(c * share, share)],
                grads.at[c, me ^ lax.rem(i, parts), i // parts],
                sem_o.at[i, c],
            )

        def block(i, carry):
            m, half = i // 2, lax.rem(i, 2)
            column = pl.multiple_of(half * 2 * tall, 2 * tall)
            both = contract_rows(left[m // 2, :, pl.ds(column, 2 * tall)], right[m]).astype(LOW)
            for j in range(2):
                stage[2 * i + j] = both[j * tall : (j + 1) * tall]
                for c in range(size):
                    write(2 * i + j, c).start()
            return carry

        lax.fori_loop(0, count * parts // 2, block, 0)

        def drain(i, carry):
            for c in range(size):
                write(i, c).wait()
            return carry

        lax.fori_loop(0, count * parts, drain, 0)

        def drain_sums(i, carry):
            finish(sum_copies(i))
            return carry

        lax.fori_loop(0, parts // 2, drain_sums, 0)

    return pl.pallas_call(
        kernel,
        out_shape=(shaped((2, rows, model)),) * 4 + (shaped((size, parts, count, share, width)),),
        in_specs=[SMEM] + [ANY] * 7,
        out_specs=(ANY,) * 5,
        scratch_shapes=[pltpu.VMEM((2, total, model), LOW)]
        + [pltpu.VMEM((model, width), LOW)] * 3
        + [
            pltpu.VMEM((3, total, width), LOW),
            pltpu.VMEM((2, total, model), LOW),
            pltpu.VMEM((count * parts, tall, width), LOW),
        ]
        + [pltpu.SemaphoreType.DMA((4,))] * 2
        + [pltpu.SemaphoreType.DMA((size * parts,))] * 3
        + [pltpu.SemaphoreType.DMA((2, parts)), pltpu.SemaphoreType.DMA((count * parts, size))],
        compiler_params=PARAMS,
        name="ffn",
        cost_estimate=cost(37),
    )(where, *tokens, *pulled, weights)


def head_grads(where, lefts, rights, gains=None, small=0, later=()):
    count = len(lefts)
    model = lefts[0].shape[1]
    each = rights[0].shape[1]
    width = each * count
    size = where.shape[0] - 2
    parts = 4
    tall = model // parts
    share = tall // size
    pad = 16 if gains else 0
    gains = gains or []

    def kernel(where_ref, *refs):
        left_refs, right_refs, refs = refs[:count], refs[count : 2 * count], refs[2 * count :]
        *gain_refs, keep, send, stage, sems = refs[: len(gains)] + refs[len(gains) + len(later) :]
        me = where_ref[size + 1]
        here = where_ref[size]

        def block(part, carry):
            column = pl.multiple_of(part * tall, tall)
            for m in range(count):
                grads = contract_rows(
                    left_refs[m][:, pl.ds(column, tall)], right_refs[m][...]
                ).astype(LOW)
                for c in range(size):
                    stage[part * size + c, :share, m * each : (m + 1) * each] = grads[
                        c * share : (c + 1) * share
                    ]
            return carry

        lax.fori_loop(0, parts, block, 0)
        if pad:
            pairs = [gain[:, :HEAD] + gain[:, HEAD:] for gain in gain_refs[2:4]]
            for i in range(parts * size):
                pieces = [gain[:, i * share : (i + 1) * share] for gain in gain_refs[:2]]
                pieces += [pair[:, i * small : (i + 1) * small] for pair in pairs]
                row = jnp.concatenate(
                    [
                        jnp.concatenate(
                            [piece, jnp.zeros((1, 128 - piece.shape[1]), jnp.float32)], axis=1
                        )
                        for piece in pieces
                    ],
                    axis=1,
                )
                stage[i, share:] = jnp.broadcast_to(row, (pad, width)).astype(LOW)

        def each_copy(do):
            for part in range(parts):
                bit = me ^ part
                for odd, out in ((0, keep), (1, send)):

                    @pl.when(lax.rem(bit, 2) == odd)
                    def _():
                        for c in range(size):
                            step = lax.rem(here - c + size, size) if size <= LINE else c
                            i = part * size + c
                            do(
                                pltpu.make_async_copy(
                                    stage.at[i], out.at[bit // 2, step], sems.at[i]
                                )
                            )

        each_copy(lambda copy: copy.start())
        each_copy(lambda copy: copy.wait())

    return pl.pallas_call(
        kernel,
        out_shape=(shaped((2, size, share + pad, width)),) * 2,
        in_specs=[SMEM] + [VMEM] * (2 * count + len(gains)) + [ANY] * len(later),
        out_specs=(ANY,) * 2,
        scratch_shapes=[
            pltpu.VMEM((parts * size, share + pad, width), LOW),
            pltpu.SemaphoreType.DMA((parts * size,)),
        ],
        compiler_params=PARAMS,
        name="head_grads",
        cost_estimate=cost(3),
    )(where, *lefts, *rights, *gains, *later)


def flip(part, bit):
    size = lax.axis_size("fsdp")
    return lax.ppermute(part, "fsdp", [(i, i ^ bit) for i in range(size)])


def swap(part):
    return lax.ppermute(part, "tp", [(0, 1), (1, 0)])


def turn(part):
    size = lax.axis_size("ctx")
    return lax.ppermute(part, "ctx", [(i, (i + 1) % size) for i in range(size)])


def ctx_slots(part):
    size = lax.axis_size("ctx")
    if size > LINE:
        whole = lax.all_gather(part, "ctx", axis=0)
        return [whole[i] for i in range(size)]
    slots = [part]
    for _ in range(1, size):
        slots.append(turn(slots[-1]))
    return slots


def ctx_sum(terms, later=()):
    size = lax.axis_size("ctx")
    if size > LINE:
        return lax.psum_scatter(terms, "ctx", scatter_dimension=0, tiled=False).astype(jnp.float32)
    moving = terms[1]
    for step in range(1, size):
        total = turn(moving).astype(jnp.float32) + terms[(step + 1) % size].astype(jnp.float32)
        moving = total.astype(LOW)
        if later and step == 1:
            moving = collect([moving], later)[0]
    return total


def ctx_sum_direct(terms):
    size = lax.axis_size("ctx")
    if size > LINE:
        return ctx_sum(terms)
    total = terms[0].astype(jnp.float32)
    for step in range(1, size):
        part = lax.ppermute(terms[step], "ctx", [(i, (i - step) % size) for i in range(size)])
        total = total + part.astype(jnp.float32)
    return total


def back_slots(part):
    size = lax.axis_size("ctx")
    if size > LINE:
        whole = lax.all_gather(part, "ctx", axis=0)
        return [whole[i] for i in range(size)]
    slots = [part]
    for step in range(1, size):
        slots.append(lax.ppermute(part, "ctx", [(i, i + step) for i in range(size - step)]))
    return slots


def back_sum(terms):
    size = lax.axis_size("ctx")
    if size > LINE:
        total = lax.psum_scatter(jnp.stack(terms), "ctx", scatter_dimension=0, tiled=False)
        return total.astype(jnp.float32), total
    parts = [terms[0]] + [
        lax.ppermute(terms[step], "ctx", [(i, i - step) for i in range(step, size)])
        for step in range(1, size)
    ]
    return sum(part.astype(jnp.float32) for part in parts), parts[1]


def group_tokens(part):
    across = flip(part, 2)
    return (part, flip(collect([part, across]), 1), across)


def chip_sum(keep, send):
    beside = flip(send, 1)
    far = keep[1].astype(jnp.float32) + beside[1].astype(jnp.float32)
    near = keep[0].astype(jnp.float32) + beside[0].astype(jnp.float32)
    return near, far.astype(LOW)


def pair_sum(near, far):
    return near + flip(far, 2).astype(jnp.float32)


def group_sum(keep, send):
    return pair_sum(*chip_sum(keep, send))


def gather_all(where, slots, share, later=(), pieces=1):
    own = collect(slots, later)
    across = flip(own, 2)
    both = flip(collect([own, across]), 1)
    return arrange(where, [own, both, across], share, pieces), across


def scatter_hidden(terms):
    size, parts, count, share, width = terms.shape
    own = lax.psum_scatter(terms.reshape(-1, width), "ctx", scatter_dimension=0, tiled=True)
    own = own.reshape(parts, count, share, width)
    return own, [own[0]] + [flip(own[bit], bit) for bit in range(1, parts)]


def body(
    inputs,
    cotangent,
    doc_bounds,
    attn_gain,
    w_query,
    w_key,
    w_value,
    w_output,
    query_gain,
    key_gain,
    ffn_gain,
    w_gate,
    w_up,
    w_down,
):
    parts = lax.axis_size("fsdp")
    size = lax.axis_size("ctx")
    tensor = lax.axis_size("tp")
    me = lax.axis_index("ctx")
    share = w_query.shape[0]
    model = share * parts * size
    width = HQ // tensor * HEAD
    kv_width = HK // tensor * HEAD
    small = query_gain.shape[0]
    shards = parts * size
    steps = jnp.arange(size, dtype=jnp.int32)
    slots_at = lax.rem(me - steps + size, size) if size <= LINE else steps
    where = jnp.concatenate(
        [slots_at, jnp.stack([me, lax.axis_index("fsdp")]).astype(jnp.int32)]
    )
    bounds = doc_bounds[0]

    split = split_columns(where, [w_gate, w_up, w_down.T])
    gains = jnp.concatenate([attn_gain, ffn_gain, query_gain, key_gain])
    pad = 16
    gain_rows = jnp.zeros((pad, 2 * kv_width), LOW).at[0, : gains.shape[0]].set(gains)
    kv_block = jnp.concatenate([jnp.concatenate([w_key, w_value], axis=1), gain_rows], axis=0)
    traded = [
        [part[0]] + [flip(part[bit], bit) for bit in range(1, parts)] for part in split
    ]
    kv_slots = ctx_slots(kv_block)
    head_slots = ctx_slots(jnp.concatenate([w_query, w_output.T], axis=1))
    (full_kv, gain_rows), kv_across = gather_all(where, kv_slots, share)
    (full_query, full_output), output_across = gather_all(
        where, head_slots, share, [kv_across], 2
    )
    weights = []
    for chunk in traded:
        block = collect(chunk, [kv_slots[-1], head_slots[2]])
        weights.append(
            lax.all_gather(
                block.reshape(-1, block.shape[-1]), "ctx", axis=0, tiled=True
            ).reshape(size, *block.shape)
        )
    pulled_all = group_tokens(collect([cotangent[0]], [output_across])[0])
    all_gains = gain_rows[:, 0].astype(jnp.float32)
    gain_attn = all_gains[:, :share].reshape(model)
    gain_ffn = all_gains[:, share : 2 * share].reshape(model)
    gain_query = jnp.tile(all_gains[:, 2 * share : 2 * share + small].reshape(HEAD), 2)[None]
    gain_key = jnp.tile(
        all_gains[:, 2 * share + small : 2 * share + 2 * small].reshape(HEAD), 2
    )[None]

    pulled = cotangent[0]

    tokens = inputs[0].astype(jnp.float32)
    rows = tokens.shape[0]
    cosine, sine = tables(me * rows, rows, bounds)
    first_inv = inverse_rms(tokens)
    normed = (tokens * first_inv * gain_attn).astype(LOW)
    keys_values = jnp.dot(normed, full_kv, preferred_element_type=jnp.float32)
    own_kv = prepare_keys(keys_values, gain_key, cosine, sine)
    kv = back_slots(own_kv)
    queries = jnp.dot(normed, full_query, preferred_element_type=jnp.float32)
    query_rot, mixed_low, mixed = attend(where, bounds, queries, kv, gain_query, cosine, sine)
    branch_part = contract_cols(mixed_low, full_output).astype(LOW)
    branch = branch_part.astype(jnp.float32) + swap(branch_part).astype(jnp.float32)
    hidden = tokens + branch
    second_inv = inverse_rms(hidden)
    hidden_normed = (hidden * second_inv * gain_ffn).astype(LOW)

    hidden_all = group_tokens(hidden_normed)
    keep, send, keep_out, send_out, terms = ffn(where, hidden_all, pulled_all, weights[0])
    near, far = chip_sum(keep, send)
    normed_part = pair_sum(near, far).astype(LOW)
    hidden_sum, traded_back = scatter_hidden(terms)
    grad_gate, grad_up, grad_down = join_columns(where, [traded_back])
    grad_down = grad_down.T
    grad_normed_ffn = normed_part.astype(jnp.float32) + swap(normed_part).astype(jnp.float32)

    ffn_gain_part = jnp.sum(grad_normed_ffn * hidden * second_inv, axis=0) * 0.5
    grad_hidden = pulled.astype(jnp.float32) + norm_back(
        hidden, second_inv, gain_ffn, grad_normed_ffn
    )
    grad_hidden_low = grad_hidden.astype(LOW)
    grad_mixed = jnp.dot(
        grad_hidden_low, full_output, preferred_element_type=jnp.float32
    ).astype(LOW)
    grad_query_low, *key_terms, query_gain_pair = attend_back(
        where, bounds, queries, query_rot, grad_mixed, mixed, kv, gain_query, cosine, sine,
        [terms],
    )
    near, far = chip_sum(
        *head_grads(where, [normed, grad_hidden_low], [grad_query_low, mixed_low])
    )
    heads_terms = pair_sum(near, far).astype(LOW)
    moved = collect(key_terms[1:], [far])
    own_terms, _ = back_sum([key_terms[0]] + [moved[i] for i in range(size - 1)])
    feed_part = group_sum(keep_out, collect([send_out], [grad_hidden_low])[0]).astype(LOW)
    feed = feed_part.astype(jnp.float32) + swap(feed_part).astype(jnp.float32)
    result = (hidden + feed).astype(LOW)[None]
    grad_kv_low, key_gain_pair = keys_back(
        keys_values,
        own_terms,
        gain_key,
        cosine,
        sine,
    )
    normed_low, attn_gain_part = normed_back(
        grad_query_low, grad_kv_low, full_query, full_kv, inputs[0], first_inv
    )
    near, far = chip_sum(
        *head_grads(
            where,
            [normed],
            [grad_kv_low],
            [attn_gain_part, ffn_gain_part[None], query_gain_pair, key_gain_pair],
            small,
        )
    )
    kv_sum = pair_sum(near, far).astype(LOW)
    own_kv = ctx_sum_direct(collect([kv_sum], [hidden_sum])[0])
    heads_sum = ctx_sum(heads_terms, [hidden_sum])
    grad_query = heads_sum[:, :width]
    grad_output = heads_sum[:, width:].T
    grad_key = own_kv[:share, :kv_width]
    grad_value = own_kv[:share, kv_width:]
    normed_low = collect([normed_low], [far])[0]
    grad_normed = normed_low.astype(jnp.float32) + swap(normed_low).astype(jnp.float32)
    own_gains = own_kv[share].astype(LOW)
    grad_gains = own_gains.astype(jnp.float32) + swap(own_gains).astype(jnp.float32)
    grad_inputs = grad_hidden + norm_back(tokens, first_inv, gain_attn, grad_normed)
    return (
        result,
        grad_inputs[None],
        grad_gains[:share],
        grad_query,
        grad_key,
        grad_value,
        grad_output,
        grad_gains[256 : 256 + small],
        grad_gains[384 : 384 + small],
        grad_gains[128 : 128 + share],
        grad_gate,
        grad_up,
        grad_down,
    )


def solution(mesh):
    vector = P(("fsdp", "ctx"))
    columns = P(("fsdp", "ctx"), "tp")
    tall = P("tp", ("fsdp", "ctx"))
    act = P("fsdp", "ctx", None)
    return jax.shard_map(
        body,
        mesh=mesh,
        in_specs=(
            act,
            act,
            P("fsdp", None),
            vector,
            columns,
            columns,
            columns,
            tall,
            vector,
            vector,
            vector,
            columns,
            columns,
            tall,
        ),
        out_specs=(
            act,
            act,
            vector,
            columns,
            columns,
            columns,
            tall,
            vector,
            vector,
            vector,
            columns,
            columns,
            tall,
        ),
        check_vma=False,
    )
```

```python
import functools
import math

import jax
import jax.numpy as jnp
from jax import lax
from jax.experimental import pallas as pl
from jax.experimental.pallas import tpu as pltpu
from jax.sharding import PartitionSpec as P

HQ = 24
HK = 8
HEAD = 64
GROUP = HQ // HK


EPS = 1e-05
THETA = 1000000.0
LINE = 4
LOG2E = math.log2(math.e)
LOW = jnp.bfloat16
VMEM = pl.BlockSpec(memory_space=pltpu.VMEM)
SMEM = pl.BlockSpec(memory_space=pltpu.SMEM)
ANY = pl.BlockSpec(memory_space=pl.ANY)
PARAMS = pltpu.CompilerParams(vmem_limit_bytes=52 * 1024 * 1024)


def inverse_rms(values):
    return lax.rsqrt(jnp.mean(values * values, axis=-1, keepdims=True) + EPS)


def norm_back(values, inverse, gain, grads):
    scaled = grads * gain
    return inverse * scaled - values * (inverse * inverse * inverse) * jnp.mean(
        scaled * values, axis=-1, keepdims=True
    )


def contract_rows(left, right):
    return lax.dot_general(
        left, right, (((0,), (0,)), ((), ())), preferred_element_type=jnp.float32
    )


def contract_cols(left, right):
    return lax.dot_general(
        left, right, (((1,), (1,)), ((), ())), preferred_element_type=jnp.float32
    )


def tables(first, rows, bounds):
    index = first + jnp.arange(rows, dtype=jnp.int32)
    begin = jnp.where(index >= bounds[1], bounds[1], jnp.where(index >= bounds[0], bounds[0], 0))
    freq = THETA ** (-(jnp.arange(HEAD // 2, dtype=jnp.float32) * 2.0 / HEAD))
    angle = (index - begin).astype(jnp.float32)[:, None] * freq[None, :]
    cosine = jnp.cos(angle)
    sine = jnp.sin(angle)
    return (
        jnp.concatenate([cosine, cosine, cosine, cosine], axis=1),
        jnp.concatenate([-sine, sine, -sine, sine], axis=1),
    )


def shaped(shape, dtype=LOW):
    return jax.ShapeDtypeStruct(shape, dtype)


def cost(micros):
    return pl.CostEstimate(
        flops=int(micros * 900000000.0), bytes_accessed=int(micros * 1000000.0), transcendentals=0
    )


def pair_inverse(x):
    lane=lax.broadcasted_iota(jnp.int32,x.shape,1)
    left=lane<HEAD
    sq=x*x
    a=jnp.sum(jnp.where(left,sq,0.0),axis=-1,keepdims=True)
    b=jnp.sum(jnp.where(left,0.0,sq),axis=-1,keepdims=True)
    return lax.rsqrt(jnp.where(left,a,b)*(1.0/HEAD)+EPS)

def pair_mean(x):
    lane=lax.broadcasted_iota(jnp.int32,x.shape,1)
    left=lane<HEAD
    a=jnp.sum(jnp.where(left,x,0.0),axis=-1,keepdims=True)
    b=jnp.sum(jnp.where(left,0.0,x),axis=-1,keepdims=True)
    return jnp.where(left,a,b)*(1.0/HEAD)

def partner(x):
    lane=lax.broadcasted_iota(jnp.int32,x.shape,1)
    front=lax.rem(lane,HEAD)<HEAD//2
    return jnp.where(front,pltpu.roll(x,2*HEAD-HEAD//2,1),pltpu.roll(x,HEAD//2,1))

def kprep_kernel(kv_ref,gain_ref,cos_ref,sin_ref,out_ref):
    width=kv_ref.shape[1]//2
    for i in range(width//128):
        x=kv_ref[:,128*i:128*(i+1)]
        xn=x*pair_inverse(x)*gain_ref[...]
        out_ref[:,128*i:128*(i+1)]=(xn*cos_ref[...]+partner(xn)*sin_ref[...]).astype(jnp.bfloat16)
    out_ref[:,width:]=kv_ref[:,width:].astype(jnp.bfloat16)

def bias_of(first_key,first_row,bounds_ref,keys,rows):
    key=first_key+lax.broadcasted_iota(jnp.int32,(keys,rows),0)
    row=first_row+lax.broadcasted_iota(jnp.int32,(keys,rows),1)
    b0=bounds_ref[0]; b1=bounds_ref[1]
    begin=jnp.where(row>=b1,b1,jnp.where(row>=b0,b0,0))
    return jnp.where((key<=row)&(key>=begin),0.0,-1e30)

def fwd_kernel(slots, where_ref, bounds_ref, q_ref, *refs):
    kv_refs = refs[:slots]
    gain_ref, cos_ref, sin_ref, qr_ref, ob_ref, oT_ref, qs, ks, vs, bias = refs[slots:]
    rows, width = kv_refs[0].shape
    width //= 2
    heads = q_ref.shape[1] // HEAD
    kvh = width // HEAD
    me = where_ref[slots]
    for i in range(heads // 2):
        at = slice(2 * HEAD * i, 2 * HEAD * (i + 1))
        x = q_ref[:, at]
        xn = x * pair_inverse(x) * gain_ref[...]
        qr_ref[:, at] = (xn * cos_ref[...] + partner(xn) * sin_ref[...]).astype(LOW)
    for h in range(heads):
        qs[h // GROUP, (h % GROUP) * rows : (h % GROUP + 1) * rows] = qr_ref[
            :, HEAD * h : HEAD * (h + 1)
        ]
    for j in range(slots):
        for k in range(kvh):
            ks[j * kvh + k] = kv_refs[j][:, HEAD * k : HEAD * (k + 1)]
            vT = kv_refs[j][:, width + HEAD * k : width + HEAD * (k + 1)].astype(jnp.float32).T
            vs[j * kvh + k] = jnp.concatenate([vT, jnp.ones_like(vT)], axis=0).astype(LOW)
    oT_ref[...] = jnp.zeros_like(oT_ref)

    def step(j, carry):
        c = where_ref[j]

        @pl.when((c <= me) & (c >= 0))
        def _():
            mask = bias_of(c * rows, me * rows, bounds_ref, rows, rows)
            for g in range(GROUP):
                bias[:, g * rows : (g + 1) * rows] = mask
            for k in range(kvh):
                s = contract_cols(ks[j * kvh + k], qs[k])
                p = jnp.exp2(s * (0.125 * LOG2E) + bias[...]).astype(LOW)
                oT_ref[k] += jnp.dot(vs[j * kvh + k], p, preferred_element_type=jnp.float32)

        return carry

    lax.fori_loop(0, slots, step, 0)
    for k in range(kvh):
        oT = oT_ref[k, :HEAD, :] * (1.0 / oT_ref[k, HEAD : HEAD + 1, :])
        oT_ref[k, :HEAD, :] = oT
        for g in range(GROUP):
            h = k * GROUP + g
            ob_ref[:, HEAD * h : HEAD * (h + 1)] = oT[:, g * rows : (g + 1) * rows].T.astype(LOW)


def bwd_kernel(slots, where_ref, bounds_ref, q_ref, qr_ref, dob_ref, oT_ref, *refs):
    kv_refs = refs[:slots]
    gain_ref, cos_ref, sin_ref, _, dqb_ref = refs[slots : slots + 5]
    dkv_refs = refs[slots + 5 : 2 * slots + 5]
    gg_ref, qs, ds_, ks, vs, kTs, dks, dvs, logl, delta, dqT, bias = refs[2 * slots + 5 :]
    rows, width = kv_refs[0].shape
    width //= 2
    heads = q_ref.shape[1] // HEAD
    kvh = width // HEAD
    me = where_ref[slots]
    for h in range(heads):
        k, g = h // GROUP, h % GROUP
        at = slice(g * rows, (g + 1) * rows)
        qs[k, at] = qr_ref[:, HEAD * h : HEAD * (h + 1)]
        d = dob_ref[:, HEAD * h : HEAD * (h + 1)]
        ds_[k, at] = d
        dT = d.astype(jnp.float32).T
        delta[k, :, at] = jnp.broadcast_to(
            jnp.sum(dT * oT_ref[k, :HEAD, at], axis=0, keepdims=True), (8, rows)
        )
    for k in range(kvh):
        logl[k] = jnp.broadcast_to(jnp.log2(oT_ref[k, HEAD : HEAD + 1, :]), logl.shape[1:])
    for j in range(slots):
        for k in range(kvh):
            t = j * kvh + k
            kb = kv_refs[j][:, HEAD * k : HEAD * (k + 1)]
            ks[t] = kb
            vs[t] = kv_refs[j][:, width + HEAD * k : width + HEAD * (k + 1)]
            kTs[t] = kb.astype(jnp.float32).T.astype(LOW)
    dqT[...] = jnp.zeros_like(dqT)

    def step(j, carry):
        c = where_ref[j]
        seen = (c <= me) & (c >= 0)

        @pl.when(seen)
        def _():
            mask = bias_of(c * rows, me * rows, bounds_ref, rows, rows)
            for g in range(GROUP):
                bias[:, g * rows : (g + 1) * rows] = mask
            for k in range(kvh):
                t = j * kvh + k
                s = contract_cols(ks[t], qs[k])
                dp = contract_cols(vs[t], ds_[k])
                p = jnp.exp2(s * (0.125 * LOG2E) + (bias[...] - logl[k, 0:1]))
                ds = (p * (dp - delta[k, 0:1])).astype(LOW)
                dvs[t] = jnp.dot(p.astype(LOW), ds_[k], preferred_element_type=jnp.float32).astype(LOW)
                dk = jnp.dot(ds, qs[k], preferred_element_type=jnp.float32)
                dks[t] = (dk * 0.125).astype(LOW)
                dqT[k] += jnp.dot(kTs[t], ds, preferred_element_type=jnp.float32)

        @pl.when(jnp.logical_not(seen))
        def _():
            for k in range(kvh):
                dks[j * kvh + k] = jnp.zeros((rows, HEAD), LOW)
                dvs[j * kvh + k] = jnp.zeros((rows, HEAD), LOW)

        return carry

    lax.fori_loop(0, slots, step, 0)
    for j in range(slots):
        for k in range(kvh):
            t = j * kvh + k
            dkv_refs[j][:, HEAD * k : HEAD * (k + 1)] = dks[t]
            dkv_refs[j][:, width + HEAD * k : width + HEAD * (k + 1)] = dvs[t]
    gg = jnp.zeros((1, 2 * HEAD), jnp.float32)
    for i in range(heads // 2):
        at = slice(2 * HEAD * i, 2 * HEAD * (i + 1))
        pair = []
        for h in (2 * i, 2 * i + 1):
            k, g = h // GROUP, h % GROUP
            pair.append(dqT[k, :, g * rows : (g + 1) * rows].T * 0.125)
        d = jnp.concatenate(pair, axis=1)
        x = q_ref[:, at]
        inv = pair_inverse(x)
        dn = d * cos_ref[...] - partner(d) * sin_ref[...]
        gg += jnp.sum(dn * x * inv, axis=0, keepdims=True)
        sc = dn * gain_ref[...]
        dqb_ref[:, at] = (inv * sc - x * (inv * inv * inv) * pair_mean(sc * x)).astype(LOW)
    gg_ref[...] = gg


def kback_kernel(kv_ref, d_ref, gain_ref, cos_ref, sin_ref, *refs):
    out_ref, gg_ref = refs[-2:]
    width = kv_ref.shape[1] // 2
    gg = jnp.zeros((1, 2 * HEAD), jnp.float32)
    for i in range(width // (2 * HEAD)):
        at = slice(2 * HEAD * i, 2 * HEAD * (i + 1))
        x = kv_ref[:, at]
        d = d_ref[:, at]
        inv = pair_inverse(x)
        dn = d * cos_ref[...] - partner(d) * sin_ref[...]
        gg += jnp.sum(dn * x * inv, axis=0, keepdims=True)
        sc = dn * gain_ref[...]
        out_ref[:, at] = (inv * sc - x * (inv * inv * inv) * pair_mean(sc * x)).astype(LOW)
    out_ref[:, width:] = d_ref[:, width:].astype(LOW)
    gg_ref[...] = gg


def prepare_keys(kv, gain, cosine, sine):
    return pl.pallas_call(
        kprep_kernel,
        out_shape=shaped(kv.shape),
        in_specs=[VMEM] * 4,
        out_specs=VMEM,
        compiler_params=PARAMS,
        name="keys",
        cost_estimate=cost(1),
    )(kv, gain, cosine, sine)


def attend(where, bounds, q, kv, gain, cosine, sine):
    slots = len(kv)
    rows, width = kv[0].shape
    heads = width // 2 // HEAD
    return pl.pallas_call(
        functools.partial(fwd_kernel, slots),
        out_shape=(
            shaped(q.shape),
            shaped(q.shape),
            shaped((heads, 2 * HEAD, GROUP * rows), jnp.float32),
        ),
        in_specs=[SMEM, SMEM] + [VMEM] * (4 + slots),
        out_specs=(VMEM,) * 3,
        scratch_shapes=[
            pltpu.VMEM((heads, GROUP * rows, HEAD), LOW),
            pltpu.VMEM((slots * heads, rows, HEAD), LOW),
            pltpu.VMEM((slots * heads, 2 * HEAD, rows), LOW),
            pltpu.VMEM((rows, GROUP * rows), jnp.float32),
        ],
        compiler_params=PARAMS,
        name="attend",
        cost_estimate=cost(14),
    )(where, bounds, q, *kv, gain, cosine, sine)


def attend_back(where, bounds, q, qr, dob, mixed, kv, gain, cosine, sine, later):
    slots = len(kv)
    rows, width = kv[0].shape
    heads = width // 2 // HEAD
    return pl.pallas_call(
        functools.partial(bwd_kernel, slots),
        out_shape=(shaped(q.shape),)
        + (shaped(kv[0].shape),) * slots
        + (shaped((1, 2 * HEAD), jnp.float32),),
        in_specs=[SMEM, SMEM] + [VMEM] * (7 + slots) + [ANY],
        out_specs=(VMEM,) * (2 + slots),
        scratch_shapes=[
            pltpu.VMEM((heads, GROUP * rows, HEAD), LOW),
            pltpu.VMEM((heads, GROUP * rows, HEAD), LOW),
            pltpu.VMEM((slots * heads, rows, HEAD), LOW),
            pltpu.VMEM((slots * heads, rows, HEAD), LOW),
            pltpu.VMEM((slots * heads, HEAD, rows), LOW),
            pltpu.VMEM((slots * heads, rows, HEAD), LOW),
            pltpu.VMEM((slots * heads, rows, HEAD), LOW),
            pltpu.VMEM((heads, 8, GROUP * rows), jnp.float32),
            pltpu.VMEM((heads, 8, GROUP * rows), jnp.float32),
            pltpu.VMEM((heads, HEAD, GROUP * rows), jnp.float32),
            pltpu.VMEM((rows, GROUP * rows), jnp.float32),
        ],
        compiler_params=PARAMS,
        name="attend_back",
        cost_estimate=cost(17),
    )(where, bounds, q, qr, dob, mixed, *kv, gain, cosine, sine, *later)


def keys_back(kv, grads, gain, cosine, sine, later=()):
    return pl.pallas_call(
        kback_kernel,
        out_shape=(shaped(kv.shape), shaped((1, 2 * HEAD), jnp.float32)),
        in_specs=[VMEM] * 5 + [ANY] * len(later),
        out_specs=(VMEM,) * 2,
        compiler_params=PARAMS,
        name="keys_back",
        cost_estimate=cost(1),
    )(kv, grads, gain, cosine, sine, *later)


def normed_back(grad_query, grad_kv, query, kv, tokens, inverse):
    def kernel(dq, dkv, wq, wkv, x, inv, out, gain):
        terms = contract_cols(dq[...], wq[...]) + contract_cols(dkv[...], wkv[...])
        out[...] = terms.astype(LOW)
        gain[...] = jnp.sum(
            terms * (x[...].astype(jnp.float32) * inv[...]), axis=0, keepdims=True
        )

    rows, model = tokens.shape
    return pl.pallas_call(
        kernel,
        out_shape=(shaped((rows, model)), shaped((1, model), jnp.float32)),
        in_specs=[VMEM] * 6,
        out_specs=(VMEM,) * 2,
        compiler_params=PARAMS,
        name="normed_back",
        cost_estimate=cost(4),
    )(grad_query, grad_kv, query, kv, tokens, inverse)


def begin(copies):
    for copy in copies:
        copy.start()


def finish(copies):
    for copy in copies:
        copy.wait()


def collect(parts, later=()):
    count = len(parts)

    def kernel(*refs):
        out, sems = refs[-2:]
        copies = [pltpu.make_async_copy(refs[i], out.at[i], sems.at[i]) for i in range(count)]
        begin(copies)
        finish(copies)

    return pl.pallas_call(
        kernel,
        out_shape=shaped((count,) + parts[0].shape, parts[0].dtype),
        in_specs=[ANY] * (count + len(later)),
        out_specs=VMEM,
        scratch_shapes=[pltpu.SemaphoreType.DMA((count,))],
        compiler_params=PARAMS,
        name="collect",
        cost_estimate=cost(1),
    )(*parts, *later)


def chunks_of(width):
    return ((0, width),)


def split_columns(where, weights):
    count = len(weights)
    share, width = weights[0].shape
    parts = 4
    width //= parts
    chunks = chunks_of(width)

    def kernel(where_ref, *refs):
        me = where_ref[where.shape[0] - 1]
        ins, outs = refs[:count], refs[count:]
        for column in range(parts):
            for bit in range(parts):

                @pl.when(column ^ bit == me)
                def _():
                    for j, (begin, end) in enumerate(chunks):
                        at = slice(column * width + begin, column * width + end)
                        for i in range(count):
                            outs[j * parts + bit][i] = ins[i][:, at]

    outs = pl.pallas_call(
        kernel,
        out_shape=tuple(
            shaped((count, share, end - begin)) for begin, end in chunks for _ in range(parts)
        ),
        in_specs=[SMEM] + [VMEM] * count,
        out_specs=(VMEM,) * (parts * len(chunks)),
        compiler_params=PARAMS,
        name="split_columns",
        cost_estimate=cost(3),
    )(where, *weights)
    return [outs[j * parts : (j + 1) * parts] for j in range(len(chunks))]


def join_columns(where, slots):
    parts = len(slots[0])
    count, share, _ = slots[0][0].shape
    width = sum(chunk[0].shape[-1] for chunk in slots)
    chunks = chunks_of(width)

    def kernel(where_ref, *refs):
        me = where_ref[where.shape[0] - 1]
        ins, outs = refs[: parts * len(chunks)], refs[parts * len(chunks) :]
        for column in range(parts):
            for bit in range(parts):

                @pl.when(column ^ bit == me)
                def _():
                    for j, (begin, end) in enumerate(chunks):
                        at = slice(column * width + begin, column * width + end)
                        for i in range(count):
                            outs[i][:, at] = ins[j * parts + bit][i].astype(jnp.float32)

    return pl.pallas_call(
        kernel,
        out_shape=(shaped((share, width * parts), jnp.float32),) * count,
        in_specs=[SMEM] + [VMEM] * (parts * len(chunks)),
        out_specs=(VMEM,) * count,
        compiler_params=PARAMS,
        name="join_columns",
        cost_estimate=cost(4),
    )(where, *[part for chunk in slots for part in chunk])


def arrange(where, slots, share, pieces):
    own, both, across = slots
    size, rows, width = own.shape
    parts = 4
    more = rows - share
    piece = width // pieces

    def kernel(where_ref, *refs):
        me = where_ref[size + 1]
        own, both, across = refs[:3]
        outs, sems = refs[3:-1], refs[-1]
        ins = [own, both.at[0], across, both.at[1]]
        copies = []
        for bit in range(parts):
            for step in range(size):
                index = (me ^ bit) * size + where_ref[step]
                row = pl.multiple_of(index * share, share)
                for i in range(pieces):
                    copies.append(
                        pltpu.make_async_copy(
                            ins[bit].at[step, pl.ds(0, share), pl.ds(i * piece, piece)],
                            outs[i].at[pl.ds(row, share)],
                            sems.at[i, bit, step],
                        )
                    )
                if more:
                    copies.append(
                        pltpu.make_async_copy(
                            ins[bit].at[step, pl.ds(share, more)],
                            outs[pieces].at[index],
                            sems.at[pieces, bit, step],
                        )
                    )
        begin(copies)
        finish(copies)

    shapes = [shaped((parts * size * share, piece))] * pieces
    if more:
        shapes.append(shaped((parts * size, more, width)))
    return pl.pallas_call(
        kernel,
        out_shape=tuple(shapes),
        in_specs=[SMEM] + [ANY] * 3,
        out_specs=(VMEM,) * len(shapes),
        scratch_shapes=[pltpu.SemaphoreType.DMA((pieces + 1, parts, size))],
        compiler_params=PARAMS,
        name="arrange",
        cost_estimate=cost(2),
    )(where, *slots)


def token_copies(refs, whole, sems):
    rows = refs[0].shape[0]
    return [
        pltpu.make_async_copy(ref, whole.at[pl.ds(i * rows, rows)], sems.at[i])
        for i, ref in enumerate(refs)
    ]


def weight_copies(where_ref, ref, m, whole, sems):
    size, parts, _, share, _ = ref.shape
    me = where_ref[size + 1]
    copies = []
    for c in range(size):
        for bit in range(parts):
            row = pl.multiple_of(((me ^ bit) * size + c) * share, share)
            copies.append(
                pltpu.make_async_copy(
                    ref.at[c, bit, m], whole.at[pl.ds(row, share)], sems.at[c * parts + bit]
                )
            )
    return copies


def ffn(where, tokens, pulled, weights):
    rows, model = tokens[0].shape
    size, parts, count, share, width = weights.shape
    total = rows * parts
    tall = model // parts

    def kernel(where_ref, *refs):
        weights_ref = refs[8]
        sums, grads = refs[9:13], refs[13]
        left, w_gate, w_up, w_down, right, back, stage = refs[14:21]
        sem_h, sem_c, sem_g, sem_u, sem_d, sem_s, sem_o = refs[21:]
        me = where_ref[size + 1]
        gates = weight_copies(where_ref, weights_ref, 0, w_gate, sem_g)
        reads = token_copies(refs[:4], left.at[0], sem_h)
        ups = weight_copies(where_ref, weights_ref, 1, w_up, sem_u)
        pulls = token_copies(refs[4:8], left.at[1], sem_c)
        downs = weight_copies(where_ref, weights_ref, 2, w_down, sem_d)
        for copies in (gates, reads, ups, pulls, downs):
            begin(copies)

        def sum_copies(i):
            return [
                pltpu.make_async_copy(
                    back.at[j, pl.ds((2 * i + odd) * rows, rows)],
                    sums[2 * j + odd].at[i],
                    sem_s.at[j, 2 * i + odd],
                )
                for j in (0, 1)
                for odd in (0, 1)
            ]

        def token_part(i, carry):
            at = pl.ds(pl.multiple_of(i * 2 * rows, 2 * rows), 2 * rows)

            @pl.when(i == 0)
            def _():
                finish(gates)
                finish(reads)

            g = jnp.dot(left[0, at], w_gate[...], preferred_element_type=jnp.float32)

            @pl.when(i == 0)
            def _():
                finish(ups)

            u = jnp.dot(left[0, at], w_up[...], preferred_element_type=jnp.float32)
            sigma = jax.nn.sigmoid(g)
            active = g * sigma
            right[2, at] = (active * u).astype(LOW)

            @pl.when(i == 0)
            def _():
                finish(pulls)
                finish(downs)

            d = jnp.dot(left[1, at], w_down[...], preferred_element_type=jnp.float32)
            right[0, at] = (d * u * sigma * (1.0 + g * (1.0 - sigma))).astype(LOW)
            right[1, at] = (d * active).astype(LOW)
            back[0, at] = (
                contract_cols(right[0, at], w_gate[...]) + contract_cols(right[1, at], w_up[...])
            ).astype(LOW)
            back[1, at] = contract_cols(right[2, at], w_down[...]).astype(LOW)
            begin(sum_copies(i))
            return carry

        lax.fori_loop(0, parts // 2, token_part, 0)

        def write(i, c):
            return pltpu.make_async_copy(
                stage.at[i, pl.ds(c * share, share)],
                grads.at[c, me ^ lax.rem(i, parts), i // parts],
                sem_o.at[i, c],
            )

        def block(i, carry):
            m, half = i // 2, lax.rem(i, 2)
            column = pl.multiple_of(half * 2 * tall, 2 * tall)
            both = contract_rows(left[m // 2, :, pl.ds(column, 2 * tall)], right[m]).astype(LOW)
            for j in range(2):
                stage[2 * i + j] = both[j * tall : (j + 1) * tall]
                for c in range(size):
                    write(2 * i + j, c).start()
            return carry

        lax.fori_loop(0, count * parts // 2, block, 0)

        def drain(i, carry):
            for c in range(size):
                write(i, c).wait()
            return carry

        lax.fori_loop(0, count * parts, drain, 0)

        def drain_sums(i, carry):
            finish(sum_copies(i))
            return carry

        lax.fori_loop(0, parts // 2, drain_sums, 0)

    return pl.pallas_call(
        kernel,
        out_shape=(shaped((2, rows, model)),) * 4 + (shaped((size, parts, count, share, width)),),
        in_specs=[SMEM] + [ANY] * 9,
        out_specs=(ANY,) * 5,
        scratch_shapes=[pltpu.VMEM((2, total, model), LOW)]
        + [pltpu.VMEM((model, width), LOW)] * 3
        + [
            pltpu.VMEM((3, total, width), LOW),
            pltpu.VMEM((2, total, model), LOW),
            pltpu.VMEM((count * parts, tall, width), LOW),
        ]
        + [pltpu.SemaphoreType.DMA((4,))] * 2
        + [pltpu.SemaphoreType.DMA((size * parts,))] * 3
        + [pltpu.SemaphoreType.DMA((2, parts)), pltpu.SemaphoreType.DMA((count * parts, size))],
        compiler_params=PARAMS,
        name="ffn",
        cost_estimate=cost(37),
    )(where, *tokens, *pulled, weights)


def head_grads(where, lefts, rights, gains=None, small=0, later=()):
    count = len(lefts)
    model = lefts[0].shape[1]
    each = rights[0].shape[1]
    width = each * count
    size = where.shape[0] - 2
    parts = 4
    tall = model // parts
    share = tall // size
    pad = 16 if gains else 0
    gains = gains or []

    def kernel(where_ref, *refs):
        left_refs, right_refs, refs = refs[:count], refs[count : 2 * count], refs[2 * count :]
        *gain_refs, keep, send, stage, sems = refs[: len(gains)] + refs[len(gains) + len(later) :]
        me = where_ref[size + 1]
        here = where_ref[size]

        def block(part, carry):
            column = pl.multiple_of(part * tall, tall)
            for m in range(count):
                grads = contract_rows(
                    left_refs[m][:, pl.ds(column, tall)], right_refs[m][...]
                ).astype(LOW)
                for c in range(size):
                    stage[part * size + c, :share, m * each : (m + 1) * each] = grads[
                        c * share : (c + 1) * share
                    ]
            return carry

        lax.fori_loop(0, parts, block, 0)
        if pad:
            pairs = [gain[:, :HEAD] + gain[:, HEAD:] for gain in gain_refs[2:4]]
            for i in range(parts * size):
                pieces = [gain[:, i * share : (i + 1) * share] for gain in gain_refs[:2]]
                pieces += [pair[:, i * small : (i + 1) * small] for pair in pairs]
                row = jnp.concatenate(
                    [
                        jnp.concatenate(
                            [piece, jnp.zeros((1, 128 - piece.shape[1]), jnp.float32)], axis=1
                        )
                        for piece in pieces
                    ],
                    axis=1,
                )
                stage[i, share:] = jnp.broadcast_to(row, (pad, width)).astype(LOW)

        def each_copy(do):
            for part in range(parts):
                bit = me ^ part
                for odd, out in ((0, keep), (1, send)):

                    @pl.when(lax.rem(bit, 2) == odd)
                    def _():
                        for c in range(size):
                            step = lax.rem(here - c + size, size) if size <= LINE else c
                            i = part * size + c
                            do(
                                pltpu.make_async_copy(
                                    stage.at[i], out.at[bit // 2, step], sems.at[i]
                                )
                            )

        each_copy(lambda copy: copy.start())
        each_copy(lambda copy: copy.wait())

    return pl.pallas_call(
        kernel,
        out_shape=(shaped((2, size, share + pad, width)),) * 2,
        in_specs=[SMEM] + [VMEM] * (2 * count + len(gains)) + [ANY] * len(later),
        out_specs=(ANY,) * 2,
        scratch_shapes=[
            pltpu.VMEM((parts * size, share + pad, width), LOW),
            pltpu.SemaphoreType.DMA((parts * size,)),
        ],
        compiler_params=PARAMS,
        name="head_grads",
        cost_estimate=cost(3),
    )(where, *lefts, *rights, *gains, *later)


def flip(part, bit):
    size = lax.axis_size("fsdp")
    return lax.ppermute(part, "fsdp", [(i, i ^ bit) for i in range(size)])


def swap(part):
    return lax.ppermute(part, "tp", [(0, 1), (1, 0)])


def turn(part):
    size = lax.axis_size("ctx")
    return lax.ppermute(part, "ctx", [(i, (i + 1) % size) for i in range(size)])


def ctx_slots(part):
    size = lax.axis_size("ctx")
    if size > LINE:
        whole = lax.all_gather(part, "ctx", axis=0)
        return [whole[i] for i in range(size)]
    slots = [part]
    for _ in range(1, size):
        slots.append(turn(slots[-1]))
    return slots


def ctx_sum(terms, later=()):
    size = lax.axis_size("ctx")
    if size > LINE:
        return lax.psum_scatter(terms, "ctx", scatter_dimension=0, tiled=False).astype(jnp.float32)
    moving = terms[1]
    for step in range(1, size):
        total = turn(moving).astype(jnp.float32) + terms[(step + 1) % size].astype(jnp.float32)
        moving = total.astype(LOW)
        if later and step == 1:
            moving = collect([moving], later)[0]
    return total


def ctx_sum_direct(terms):
    size = lax.axis_size("ctx")
    if size > LINE:
        return ctx_sum(terms)
    total = terms[0].astype(jnp.float32)
    for step in range(1, size):
        part = lax.ppermute(terms[step], "ctx", [(i, (i - step) % size) for i in range(size)])
        total = total + part.astype(jnp.float32)
    return total


def back_slots(part):
    size = lax.axis_size("ctx")
    if size > LINE:
        whole = lax.all_gather(part, "ctx", axis=0)
        return [whole[i] for i in range(size)]
    slots = [part]
    for step in range(1, size):
        slots.append(lax.ppermute(part, "ctx", [(i, i + step) for i in range(size - step)]))
    return slots


def back_sum(terms):
    size = lax.axis_size("ctx")
    if size > LINE:
        total = lax.psum_scatter(jnp.stack(terms), "ctx", scatter_dimension=0, tiled=False)
        return total.astype(jnp.float32), total
    parts = [terms[0]] + [
        lax.ppermute(terms[step], "ctx", [(i, i - step) for i in range(step, size)])
        for step in range(1, size)
    ]
    return sum(part.astype(jnp.float32) for part in parts), parts[1]


def group_tokens(part):
    across = flip(part, 2)
    return (part, flip(part, 1), across, flip(across, 1))


def chip_sum(keep, send):
    beside = flip(send, 1)
    far = keep[1].astype(jnp.float32) + beside[1].astype(jnp.float32)
    near = keep[0].astype(jnp.float32) + beside[0].astype(jnp.float32)
    return near, far.astype(LOW)


def pair_sum(near, far):
    return near + flip(far, 2).astype(jnp.float32)


def group_sum(keep, send):
    return pair_sum(*chip_sum(keep, send))


def gather_all(where, slots, share, later=(), pieces=1):
    own = collect(slots, later)
    across = flip(own, 2)
    both = flip(collect([own, across]), 1)
    return arrange(where, [own, both, across], share, pieces), across


def scatter_hidden(terms):
    size, parts, count, share, width = terms.shape
    own = lax.psum_scatter(terms.reshape(-1, width), "ctx", scatter_dimension=0, tiled=True)
    own = own.reshape(parts, count, share, width)
    return own, [own[0]] + [flip(own[bit], bit) for bit in range(1, parts)]


def body(
    inputs,
    cotangent,
    doc_bounds,
    attn_gain,
    w_query,
    w_key,
    w_value,
    w_output,
    query_gain,
    key_gain,
    ffn_gain,
    w_gate,
    w_up,
    w_down,
):
    parts = lax.axis_size("fsdp")
    size = lax.axis_size("ctx")
    tensor = lax.axis_size("tp")
    me = lax.axis_index("ctx")
    share = w_query.shape[0]
    model = share * parts * size
    width = HQ // tensor * HEAD
    kv_width = HK // tensor * HEAD
    small = query_gain.shape[0]
    shards = parts * size
    steps = jnp.arange(size, dtype=jnp.int32)
    slots_at = lax.rem(me - steps + size, size) if size <= LINE else steps
    where = jnp.concatenate(
        [slots_at, jnp.stack([me, lax.axis_index("fsdp")]).astype(jnp.int32)]
    )
    bounds = doc_bounds[0]

    split = split_columns(where, [w_gate, w_up, w_down.T])
    gains = jnp.concatenate([attn_gain, ffn_gain, query_gain, key_gain])
    pad = 16
    gain_rows = jnp.zeros((pad, 2 * kv_width), LOW).at[0, : gains.shape[0]].set(gains)
    kv_block = jnp.concatenate([jnp.concatenate([w_key, w_value], axis=1), gain_rows], axis=0)
    traded = [
        [part[0]] + [flip(part[bit], bit) for bit in range(1, parts)] for part in split
    ]
    kv_slots = ctx_slots(kv_block)
    head_slots = ctx_slots(jnp.concatenate([w_query, w_output.T], axis=1))
    (full_kv, gain_rows), kv_across = gather_all(where, kv_slots, share)
    (full_query, full_output), output_across = gather_all(
        where, head_slots, share, [kv_across], 2
    )
    weights = []
    for chunk in traded:
        block = collect(chunk, [kv_slots[-1], head_slots[2]])
        weights.append(
            lax.all_gather(
                block.reshape(-1, block.shape[-1]), "ctx", axis=0, tiled=True
            ).reshape(size, *block.shape)
        )
    pulled_all = group_tokens(collect([cotangent[0]], [output_across])[0])
    all_gains = gain_rows[:, 0].astype(jnp.float32)
    gain_attn = all_gains[:, :share].reshape(model)
    gain_ffn = all_gains[:, share : 2 * share].reshape(model)
    gain_query = jnp.tile(all_gains[:, 2 * share : 2 * share + small].reshape(HEAD), 2)[None]
    gain_key = jnp.tile(
        all_gains[:, 2 * share + small : 2 * share + 2 * small].reshape(HEAD), 2
    )[None]

    pulled = cotangent[0]

    tokens = inputs[0].astype(jnp.float32)
    rows = tokens.shape[0]
    cosine, sine = tables(me * rows, rows, bounds)
    first_inv = inverse_rms(tokens)
    normed = (tokens * first_inv * gain_attn).astype(LOW)
    keys_values = jnp.dot(normed, full_kv, preferred_element_type=jnp.float32)
    own_kv = prepare_keys(keys_values, gain_key, cosine, sine)
    kv = back_slots(own_kv)
    queries = jnp.dot(normed, full_query, preferred_element_type=jnp.float32)
    query_rot, mixed_low, mixed = attend(where, bounds, queries, kv, gain_query, cosine, sine)
    branch_part = contract_cols(mixed_low, full_output).astype(LOW)
    branch = branch_part.astype(jnp.float32) + swap(branch_part).astype(jnp.float32)
    hidden = tokens + branch
    second_inv = inverse_rms(hidden)
    hidden_normed = (hidden * second_inv * gain_ffn).astype(LOW)

    hidden_all = group_tokens(hidden_normed)
    keep, send, keep_out, send_out, terms = ffn(where, hidden_all, pulled_all, weights[0])
    near, far = chip_sum(keep, send)
    normed_part = pair_sum(near, far).astype(LOW)
    hidden_sum, traded_back = scatter_hidden(terms)
    grad_gate, grad_up, grad_down = join_columns(where, [traded_back])
    grad_down = grad_down.T
    grad_normed_ffn = normed_part.astype(jnp.float32) + swap(normed_part).astype(jnp.float32)

    ffn_gain_part = jnp.sum(grad_normed_ffn * hidden * second_inv, axis=0) * 0.5
    grad_hidden = pulled.astype(jnp.float32) + norm_back(
        hidden, second_inv, gain_ffn, grad_normed_ffn
    )
    grad_hidden_low = grad_hidden.astype(LOW)
    grad_mixed = jnp.dot(
        grad_hidden_low, full_output, preferred_element_type=jnp.float32
    ).astype(LOW)
    grad_query_low, *key_terms, query_gain_pair = attend_back(
        where, bounds, queries, query_rot, grad_mixed, mixed, kv, gain_query, cosine, sine,
        [terms],
    )
    near, far = chip_sum(
        *head_grads(where, [normed, grad_hidden_low], [grad_query_low, mixed_low])
    )
    heads_terms = pair_sum(near, far).astype(LOW)
    moved = collect(key_terms[1:], [far])
    own_terms, _ = back_sum([key_terms[0]] + [moved[i] for i in range(size - 1)])
    feed_part = group_sum(keep_out, collect([send_out], [grad_hidden_low])[0]).astype(LOW)
    feed = feed_part.astype(jnp.float32) + swap(feed_part).astype(jnp.float32)
    result = (hidden + feed).astype(LOW)[None]
    grad_kv_low, key_gain_pair = keys_back(
        keys_values,
        own_terms,
        gain_key,
        cosine,
        sine,
    )
    normed_low, attn_gain_part = normed_back(
        grad_query_low, grad_kv_low, full_query, full_kv, inputs[0], first_inv
    )
    near, far = chip_sum(
        *head_grads(
            where,
            [normed],
            [grad_kv_low],
            [attn_gain_part, ffn_gain_part[None], query_gain_pair, key_gain_pair],
            small,
        )
    )
    kv_sum = pair_sum(near, far).astype(LOW)
    own_kv = ctx_sum_direct(collect([kv_sum], [hidden_sum])[0])
    heads_sum = ctx_sum(heads_terms, [hidden_sum])
    grad_query = heads_sum[:, :width]
    grad_output = heads_sum[:, width:].T
    grad_key = own_kv[:share, :kv_width]
    grad_value = own_kv[:share, kv_width:]
    normed_low = collect([normed_low], [far])[0]
    grad_normed = normed_low.astype(jnp.float32) + swap(normed_low).astype(jnp.float32)
    own_gains = own_kv[share].astype(LOW)
    grad_gains = own_gains.astype(jnp.float32) + swap(own_gains).astype(jnp.float32)
    grad_inputs = grad_hidden + norm_back(tokens, first_inv, gain_attn, grad_normed)
    return (
        result,
        grad_inputs[None],
        grad_gains[:share],
        grad_query,
        grad_key,
        grad_value,
        grad_output,
        grad_gains[256 : 256 + small],
        grad_gains[384 : 384 + small],
        grad_gains[128 : 128 + share],
        grad_gate,
        grad_up,
        grad_down,
    )


def solution(mesh):
    vector = P(("fsdp", "ctx"))
    columns = P(("fsdp", "ctx"), "tp")
    tall = P("tp", ("fsdp", "ctx"))
    act = P("fsdp", "ctx", None)
    return jax.shard_map(
        body,
        mesh=mesh,
        in_specs=(
            act,
            act,
            P("fsdp", None),
            vector,
            columns,
            columns,
            columns,
            tall,
            vector,
            vector,
            vector,
            columns,
            columns,
            tall,
        ),
        out_specs=(
            act,
            act,
            vector,
            columns,
            columns,
            columns,
            tall,
            vector,
            vector,
            vector,
            columns,
            columns,
            tall,
        ),
        check_vma=False,
    )
```

```python
import functools
import math

import jax
import jax.numpy as jnp
from jax import lax
from jax.experimental import pallas as pl
from jax.experimental.pallas import tpu as pltpu
from jax.sharding import PartitionSpec as P

HQ = 24
HK = 8
HEAD = 64
GROUP = HQ // HK


EPS = 1e-05
THETA = 1000000.0
LINE = 4
LOG2E = math.log2(math.e)
LOW = jnp.bfloat16
VMEM = pl.BlockSpec(memory_space=pltpu.VMEM)
SMEM = pl.BlockSpec(memory_space=pltpu.SMEM)
ANY = pl.BlockSpec(memory_space=pl.ANY)
PARAMS = pltpu.CompilerParams(vmem_limit_bytes=52 * 1024 * 1024)


def inverse_rms(values):
    return lax.rsqrt(jnp.mean(values * values, axis=-1, keepdims=True) + EPS)


def norm_back(values, inverse, gain, grads):
    scaled = grads * gain
    return inverse * scaled - values * (inverse * inverse * inverse) * jnp.mean(
        scaled * values, axis=-1, keepdims=True
    )


def contract_rows(left, right):
    return lax.dot_general(
        left, right, (((0,), (0,)), ((), ())), preferred_element_type=jnp.float32
    )


def contract_cols(left, right):
    return lax.dot_general(
        left, right, (((1,), (1,)), ((), ())), preferred_element_type=jnp.float32
    )


def tables(first, rows, bounds):
    index = first + jnp.arange(rows, dtype=jnp.int32)
    begin = jnp.where(index >= bounds[1], bounds[1], jnp.where(index >= bounds[0], bounds[0], 0))
    freq = THETA ** (-(jnp.arange(HEAD // 2, dtype=jnp.float32) * 2.0 / HEAD))
    angle = (index - begin).astype(jnp.float32)[:, None] * freq[None, :]
    cosine = jnp.cos(angle)
    sine = jnp.sin(angle)
    return (
        jnp.concatenate([cosine, cosine, cosine, cosine], axis=1),
        jnp.concatenate([-sine, sine, -sine, sine], axis=1),
    )


def shaped(shape, dtype=LOW):
    return jax.ShapeDtypeStruct(shape, dtype)


def cost(micros):
    return pl.CostEstimate(
        flops=int(micros * 900000000.0), bytes_accessed=int(micros * 1000000.0), transcendentals=0
    )


def pair_inverse(x):
    lane=lax.broadcasted_iota(jnp.int32,x.shape,1)
    left=lane<HEAD
    sq=x*x
    a=jnp.sum(jnp.where(left,sq,0.0),axis=-1,keepdims=True)
    b=jnp.sum(jnp.where(left,0.0,sq),axis=-1,keepdims=True)
    return lax.rsqrt(jnp.where(left,a,b)*(1.0/HEAD)+EPS)

def pair_mean(x):
    lane=lax.broadcasted_iota(jnp.int32,x.shape,1)
    left=lane<HEAD
    a=jnp.sum(jnp.where(left,x,0.0),axis=-1,keepdims=True)
    b=jnp.sum(jnp.where(left,0.0,x),axis=-1,keepdims=True)
    return jnp.where(left,a,b)*(1.0/HEAD)

def partner(x):
    lane=lax.broadcasted_iota(jnp.int32,x.shape,1)
    front=lax.rem(lane,HEAD)<HEAD//2
    return jnp.where(front,pltpu.roll(x,2*HEAD-HEAD//2,1),pltpu.roll(x,HEAD//2,1))

def kprep_kernel(kv_ref,gain_ref,cos_ref,sin_ref,out_ref):
    width=kv_ref.shape[1]//2
    for i in range(width//128):
        x=kv_ref[:,128*i:128*(i+1)]
        xn=x*pair_inverse(x)*gain_ref[...]
        out_ref[:,128*i:128*(i+1)]=(xn*cos_ref[...]+partner(xn)*sin_ref[...]).astype(jnp.bfloat16)
    out_ref[:,width:]=kv_ref[:,width:].astype(jnp.bfloat16)

def bias_of(first_key,first_row,bounds_ref,keys,rows):
    key=first_key+lax.broadcasted_iota(jnp.int32,(keys,rows),0)
    row=first_row+lax.broadcasted_iota(jnp.int32,(keys,rows),1)
    b0=bounds_ref[0]; b1=bounds_ref[1]
    begin=jnp.where(row>=b1,b1,jnp.where(row>=b0,b0,0))
    return jnp.where((key<=row)&(key>=begin),0.0,-1e30)

def fwd_kernel(slots, where_ref, bounds_ref, q_ref, *refs):
    kv_refs = refs[:slots]
    gain_ref, cos_ref, sin_ref, qr_ref, ob_ref, oT_ref, qs, ks, vs, bias = refs[slots:]
    rows, width = kv_refs[0].shape
    width //= 2
    heads = q_ref.shape[1] // HEAD
    kvh = width // HEAD
    me = where_ref[slots]
    for i in range(heads // 2):
        at = slice(2 * HEAD * i, 2 * HEAD * (i + 1))
        x = q_ref[:, at]
        xn = x * pair_inverse(x) * gain_ref[...]
        qr_ref[:, at] = (xn * cos_ref[...] + partner(xn) * sin_ref[...]).astype(LOW)
    for h in range(heads):
        qs[h // GROUP, (h % GROUP) * rows : (h % GROUP + 1) * rows] = qr_ref[
            :, HEAD * h : HEAD * (h + 1)
        ]
    for j in range(slots):
        for k in range(kvh):
            ks[j * kvh + k] = kv_refs[j][:, HEAD * k : HEAD * (k + 1)]
            vT = kv_refs[j][:, width + HEAD * k : width + HEAD * (k + 1)].astype(jnp.float32).T
            vs[j * kvh + k] = jnp.concatenate([vT, jnp.ones_like(vT)], axis=0).astype(LOW)
    oT_ref[...] = jnp.zeros_like(oT_ref)

    def step(j, carry):
        c = where_ref[j]

        @pl.when((c <= me) & (c >= 0))
        def _():
            mask = bias_of(c * rows, me * rows, bounds_ref, rows, rows)
            for g in range(GROUP):
                bias[:, g * rows : (g + 1) * rows] = mask
            for k in range(kvh):
                s = contract_cols(ks[j * kvh + k], qs[k])
                p = jnp.exp2(s * (0.125 * LOG2E) + bias[...]).astype(LOW)
                oT_ref[k] += jnp.dot(vs[j * kvh + k], p, preferred_element_type=jnp.float32)

        return carry

    lax.fori_loop(0, slots, step, 0)
    for k in range(kvh):
        oT = oT_ref[k, :HEAD, :] * (1.0 / oT_ref[k, HEAD : HEAD + 1, :])
        oT_ref[k, :HEAD, :] = oT
        for g in range(GROUP):
            h = k * GROUP + g
            ob_ref[:, HEAD * h : HEAD * (h + 1)] = oT[:, g * rows : (g + 1) * rows].T.astype(LOW)


def bwd_kernel(slots, where_ref, bounds_ref, q_ref, qr_ref, dob_ref, oT_ref, *refs):
    kv_refs = refs[:slots]
    gain_ref, cos_ref, sin_ref, _, dqb_ref = refs[slots : slots + 5]
    dkv_refs = refs[slots + 5 : 2 * slots + 5]
    gg_ref, qs, ds_, ks, vs, kTs, dks, dvs, logl, delta, dqT, bias = refs[2 * slots + 5 :]
    rows, width = kv_refs[0].shape
    width //= 2
    heads = q_ref.shape[1] // HEAD
    kvh = width // HEAD
    me = where_ref[slots]
    for h in range(heads):
        k, g = h // GROUP, h % GROUP
        at = slice(g * rows, (g + 1) * rows)
        qs[k, at] = qr_ref[:, HEAD * h : HEAD * (h + 1)]
        d = dob_ref[:, HEAD * h : HEAD * (h + 1)]
        ds_[k, at] = d
        dT = d.astype(jnp.float32).T
        delta[k, :, at] = jnp.broadcast_to(
            jnp.sum(dT * oT_ref[k, :HEAD, at], axis=0, keepdims=True), (8, rows)
        )
    for k in range(kvh):
        logl[k] = jnp.broadcast_to(jnp.log2(oT_ref[k, HEAD : HEAD + 1, :]), logl.shape[1:])
    for j in range(slots):
        for k in range(kvh):
            t = j * kvh + k
            kb = kv_refs[j][:, HEAD * k : HEAD * (k + 1)]
            ks[t] = kb
            vs[t] = kv_refs[j][:, width + HEAD * k : width + HEAD * (k + 1)]
            kTs[t] = kb.astype(jnp.float32).T.astype(LOW)
    dqT[...] = jnp.zeros_like(dqT)

    def step(j, carry):
        c = where_ref[j]
        seen = (c <= me) & (c >= 0)

        @pl.when(seen)
        def _():
            mask = bias_of(c * rows, me * rows, bounds_ref, rows, rows)
            for g in range(GROUP):
                bias[:, g * rows : (g + 1) * rows] = mask
            for k in range(kvh):
                t = j * kvh + k
                s = contract_cols(ks[t], qs[k])
                dp = contract_cols(vs[t], ds_[k])
                p = jnp.exp2(s * (0.125 * LOG2E) + (bias[...] - logl[k, 0:1]))
                ds = (p * (dp - delta[k, 0:1])).astype(LOW)
                dvs[t] = jnp.dot(p.astype(LOW), ds_[k], preferred_element_type=jnp.float32).astype(LOW)
                dk = jnp.dot(ds, qs[k], preferred_element_type=jnp.float32)
                dks[t] = (dk * 0.125).astype(LOW)
                dqT[k] += jnp.dot(kTs[t], ds, preferred_element_type=jnp.float32)

        @pl.when(jnp.logical_not(seen))
        def _():
            for k in range(kvh):
                dks[j * kvh + k] = jnp.zeros((rows, HEAD), LOW)
                dvs[j * kvh + k] = jnp.zeros((rows, HEAD), LOW)

        return carry

    lax.fori_loop(0, slots, step, 0)
    for j in range(slots):
        for k in range(kvh):
            t = j * kvh + k
            dkv_refs[j][:, HEAD * k : HEAD * (k + 1)] = dks[t]
            dkv_refs[j][:, width + HEAD * k : width + HEAD * (k + 1)] = dvs[t]
    gg = jnp.zeros((1, 2 * HEAD), jnp.float32)
    for i in range(heads // 2):
        at = slice(2 * HEAD * i, 2 * HEAD * (i + 1))
        pair = []
        for h in (2 * i, 2 * i + 1):
            k, g = h // GROUP, h % GROUP
            pair.append(dqT[k, :, g * rows : (g + 1) * rows].T * 0.125)
        d = jnp.concatenate(pair, axis=1)
        x = q_ref[:, at]
        inv = pair_inverse(x)
        dn = d * cos_ref[...] - partner(d) * sin_ref[...]
        gg += jnp.sum(dn * x * inv, axis=0, keepdims=True)
        sc = dn * gain_ref[...]
        dqb_ref[:, at] = (inv * sc - x * (inv * inv * inv) * pair_mean(sc * x)).astype(LOW)
    gg_ref[...] = gg


def kback_kernel(kv_ref, d_ref, gain_ref, cos_ref, sin_ref, *refs):
    out_ref, gg_ref = refs[-2:]
    width = kv_ref.shape[1] // 2
    gg = jnp.zeros((1, 2 * HEAD), jnp.float32)
    for i in range(width // (2 * HEAD)):
        at = slice(2 * HEAD * i, 2 * HEAD * (i + 1))
        x = kv_ref[:, at]
        d = d_ref[:, at]
        inv = pair_inverse(x)
        dn = d * cos_ref[...] - partner(d) * sin_ref[...]
        gg += jnp.sum(dn * x * inv, axis=0, keepdims=True)
        sc = dn * gain_ref[...]
        out_ref[:, at] = (inv * sc - x * (inv * inv * inv) * pair_mean(sc * x)).astype(LOW)
    out_ref[:, width:] = d_ref[:, width:].astype(LOW)
    gg_ref[...] = gg


def prepare_keys(kv, gain, cosine, sine):
    return pl.pallas_call(
        kprep_kernel,
        out_shape=shaped(kv.shape),
        in_specs=[VMEM] * 4,
        out_specs=VMEM,
        compiler_params=PARAMS,
        name="keys",
        cost_estimate=cost(1),
    )(kv, gain, cosine, sine)


def attend(where, bounds, q, kv, gain, cosine, sine):
    slots = len(kv)
    rows, width = kv[0].shape
    heads = width // 2 // HEAD
    return pl.pallas_call(
        functools.partial(fwd_kernel, slots),
        out_shape=(
            shaped(q.shape),
            shaped(q.shape),
            shaped((heads, 2 * HEAD, GROUP * rows), jnp.float32),
        ),
        in_specs=[SMEM, SMEM] + [VMEM] * (4 + slots),
        out_specs=(VMEM,) * 3,
        scratch_shapes=[
            pltpu.VMEM((heads, GROUP * rows, HEAD), LOW),
            pltpu.VMEM((slots * heads, rows, HEAD), LOW),
            pltpu.VMEM((slots * heads, 2 * HEAD, rows), LOW),
            pltpu.VMEM((rows, GROUP * rows), jnp.float32),
        ],
        compiler_params=PARAMS,
        name="attend",
        cost_estimate=cost(14),
    )(where, bounds, q, *kv, gain, cosine, sine)


def attend_back(where, bounds, q, qr, dob, mixed, kv, gain, cosine, sine, later):
    slots = len(kv)
    rows, width = kv[0].shape
    heads = width // 2 // HEAD
    return pl.pallas_call(
        functools.partial(bwd_kernel, slots),
        out_shape=(shaped(q.shape),)
        + (shaped(kv[0].shape),) * slots
        + (shaped((1, 2 * HEAD), jnp.float32),),
        in_specs=[SMEM, SMEM] + [VMEM] * (7 + slots) + [ANY],
        out_specs=(VMEM,) * (2 + slots),
        scratch_shapes=[
            pltpu.VMEM((heads, GROUP * rows, HEAD), LOW),
            pltpu.VMEM((heads, GROUP * rows, HEAD), LOW),
            pltpu.VMEM((slots * heads, rows, HEAD), LOW),
            pltpu.VMEM((slots * heads, rows, HEAD), LOW),
            pltpu.VMEM((slots * heads, HEAD, rows), LOW),
            pltpu.VMEM((slots * heads, rows, HEAD), LOW),
            pltpu.VMEM((slots * heads, rows, HEAD), LOW),
            pltpu.VMEM((heads, 8, GROUP * rows), jnp.float32),
            pltpu.VMEM((heads, 8, GROUP * rows), jnp.float32),
            pltpu.VMEM((heads, HEAD, GROUP * rows), jnp.float32),
            pltpu.VMEM((rows, GROUP * rows), jnp.float32),
        ],
        compiler_params=PARAMS,
        name="attend_back",
        cost_estimate=cost(17),
    )(where, bounds, q, qr, dob, mixed, *kv, gain, cosine, sine, *later)


def keys_back(kv, grads, gain, cosine, sine, later=()):
    return pl.pallas_call(
        kback_kernel,
        out_shape=(shaped(kv.shape), shaped((1, 2 * HEAD), jnp.float32)),
        in_specs=[VMEM] * 5 + [ANY] * len(later),
        out_specs=(VMEM,) * 2,
        compiler_params=PARAMS,
        name="keys_back",
        cost_estimate=cost(1),
    )(kv, grads, gain, cosine, sine, *later)


def normed_back(grad_query, grad_kv, query, kv, tokens, inverse):
    def kernel(dq, dkv, wq, wkv, x, inv, out, gain):
        terms = contract_cols(dq[...], wq[...]) + contract_cols(dkv[...], wkv[...])
        out[...] = terms.astype(LOW)
        gain[...] = jnp.sum(
            terms * (x[...].astype(jnp.float32) * inv[...]), axis=0, keepdims=True
        )

    rows, model = tokens.shape
    return pl.pallas_call(
        kernel,
        out_shape=(shaped((rows, model)), shaped((1, model), jnp.float32)),
        in_specs=[VMEM] * 6,
        out_specs=(VMEM,) * 2,
        compiler_params=PARAMS,
        name="normed_back",
        cost_estimate=cost(4),
    )(grad_query, grad_kv, query, kv, tokens, inverse)


def begin(copies):
    for copy in copies:
        copy.start()


def finish(copies):
    for copy in copies:
        copy.wait()


def collect(parts, later=()):
    count = len(parts)

    def kernel(*refs):
        out, sems = refs[-2:]
        copies = [pltpu.make_async_copy(refs[i], out.at[i], sems.at[i]) for i in range(count)]
        begin(copies)
        finish(copies)

    return pl.pallas_call(
        kernel,
        out_shape=shaped((count,) + parts[0].shape, parts[0].dtype),
        in_specs=[ANY] * (count + len(later)),
        out_specs=VMEM,
        scratch_shapes=[pltpu.SemaphoreType.DMA((count,))],
        compiler_params=PARAMS,
        name="collect",
        cost_estimate=cost(1),
    )(*parts, *later)


def chunks_of(width):
    return ((0, width),)


def split_columns(where, weights):
    count = len(weights)
    share, width = weights[0].shape
    parts = 4
    width //= parts
    chunks = chunks_of(width)

    def kernel(where_ref, *refs):
        me = where_ref[where.shape[0] - 1]
        ins, outs = refs[:count], refs[count:]
        for column in range(parts):
            for bit in range(parts):

                @pl.when(column ^ bit == me)
                def _():
                    for j, (begin, end) in enumerate(chunks):
                        at = slice(column * width + begin, column * width + end)
                        for i in range(count):
                            outs[j * parts + bit][i] = ins[i][:, at]

    outs = pl.pallas_call(
        kernel,
        out_shape=tuple(
            shaped((count, share, end - begin)) for begin, end in chunks for _ in range(parts)
        ),
        in_specs=[SMEM] + [VMEM] * count,
        out_specs=(VMEM,) * (parts * len(chunks)),
        compiler_params=PARAMS,
        name="split_columns",
        cost_estimate=cost(3),
    )(where, *weights)
    return [outs[j * parts : (j + 1) * parts] for j in range(len(chunks))]


def join_columns(where, slots):
    parts = len(slots[0])
    count, share, _ = slots[0][0].shape
    width = sum(chunk[0].shape[-1] for chunk in slots)
    chunks = chunks_of(width)

    def kernel(where_ref, *refs):
        me = where_ref[where.shape[0] - 1]
        ins, outs = refs[: parts * len(chunks)], refs[parts * len(chunks) :]
        for column in range(parts):
            for bit in range(parts):

                @pl.when(column ^ bit == me)
                def _():
                    for j, (begin, end) in enumerate(chunks):
                        at = slice(column * width + begin, column * width + end)
                        for i in range(count):
                            outs[i][:, at] = ins[j * parts + bit][i].astype(jnp.float32)

    return pl.pallas_call(
        kernel,
        out_shape=(shaped((share, width * parts), jnp.float32),) * count,
        in_specs=[SMEM] + [VMEM] * (parts * len(chunks)),
        out_specs=(VMEM,) * count,
        compiler_params=PARAMS,
        name="join_columns",
        cost_estimate=cost(4),
    )(where, *[part for chunk in slots for part in chunk])


def arrange(where, slots, share, pieces):
    own, both, across = slots
    size, rows, width = own.shape
    parts = 4
    more = rows - share
    piece = width // pieces

    def kernel(where_ref, *refs):
        me = where_ref[size + 1]
        own, both, across = refs[:3]
        outs, sems = refs[3:-1], refs[-1]
        ins = [own, both.at[0], across, both.at[1]]
        copies = []
        for bit in range(parts):
            for step in range(size):
                index = (me ^ bit) * size + where_ref[step]
                row = pl.multiple_of(index * share, share)
                for i in range(pieces):
                    copies.append(
                        pltpu.make_async_copy(
                            ins[bit].at[step, pl.ds(0, share), pl.ds(i * piece, piece)],
                            outs[i].at[pl.ds(row, share)],
                            sems.at[i, bit, step],
                        )
                    )
                if more:
                    copies.append(
                        pltpu.make_async_copy(
                            ins[bit].at[step, pl.ds(share, more)],
                            outs[pieces].at[index],
                            sems.at[pieces, bit, step],
                        )
                    )
        begin(copies)
        finish(copies)

    shapes = [shaped((parts * size * share, piece))] * pieces
    if more:
        shapes.append(shaped((parts * size, more, width)))
    return pl.pallas_call(
        kernel,
        out_shape=tuple(shapes),
        in_specs=[SMEM] + [ANY] * 3,
        out_specs=(VMEM,) * len(shapes),
        scratch_shapes=[pltpu.SemaphoreType.DMA((pieces + 1, parts, size))],
        compiler_params=PARAMS,
        name="arrange",
        cost_estimate=cost(2),
    )(where, *slots)


def token_copies(refs, whole, sems):
    rows = refs[0].shape[0]
    return [
        pltpu.make_async_copy(ref, whole.at[pl.ds(i * rows, rows)], sems.at[i])
        for i, ref in enumerate(refs)
    ]


def weight_copies(where_ref, ref, m, whole, sems):
    size, parts, _, share, _ = ref.shape
    me = where_ref[size + 1]
    copies = []
    for c in range(size):
        for bit in range(parts):
            row = pl.multiple_of(((me ^ bit) * size + c) * share, share)
            copies.append(
                pltpu.make_async_copy(
                    ref.at[c, bit, m], whole.at[pl.ds(row, share)], sems.at[c * parts + bit]
                )
            )
    return copies


def ffn(where, tokens, pulled, weights):
    rows, model = tokens[0].shape
    size, parts, count, share, width = weights.shape
    total = rows * parts
    tall = model // parts

    def kernel(where_ref, *refs):
        weights_ref = refs[8]
        sums, grads = refs[9:13], refs[13]
        left, w_gate, w_up, w_down, right, back, stage = refs[14:21]
        sem_h, sem_c, sem_g, sem_u, sem_d, sem_s, sem_o = refs[21:]
        me = where_ref[size + 1]
        gates = weight_copies(where_ref, weights_ref, 0, w_gate, sem_g)
        reads = token_copies(refs[:4], left.at[0], sem_h)
        ups = weight_copies(where_ref, weights_ref, 1, w_up, sem_u)
        pulls = token_copies(refs[4:8], left.at[1], sem_c)
        downs = weight_copies(where_ref, weights_ref, 2, w_down, sem_d)
        for copies in (gates, reads, ups, pulls, downs):
            begin(copies)

        def sum_copies(i):
            return [
                pltpu.make_async_copy(
                    back.at[j, pl.ds((2 * i + odd) * rows, rows)],
                    sums[2 * j + odd].at[i],
                    sem_s.at[j, 2 * i + odd],
                )
                for j in (0, 1)
                for odd in (0, 1)
            ]

        def token_part(i, carry):
            at = pl.ds(pl.multiple_of(i * 2 * rows, 2 * rows), 2 * rows)

            @pl.when(i == 0)
            def _():
                finish(gates)
                finish(reads)

            g = jnp.dot(left[0, at], w_gate[...], preferred_element_type=jnp.float32)

            @pl.when(i == 0)
            def _():
                finish(ups)

            u = jnp.dot(left[0, at], w_up[...], preferred_element_type=jnp.float32)
            sigma = jax.nn.sigmoid(g)
            active = g * sigma
            right[2, at] = (active * u).astype(LOW)

            @pl.when(i == 0)
            def _():
                finish(pulls)
                finish(downs)

            d = jnp.dot(left[1, at], w_down[...], preferred_element_type=jnp.float32)
            right[0, at] = (d * u * sigma * (1.0 + g * (1.0 - sigma))).astype(LOW)
            right[1, at] = (d * active).astype(LOW)
            back[0, at] = (
                contract_cols(right[0, at], w_gate[...]) + contract_cols(right[1, at], w_up[...])
            ).astype(LOW)
            back[1, at] = contract_cols(right[2, at], w_down[...]).astype(LOW)
            begin(sum_copies(i))
            return carry

        lax.fori_loop(0, parts // 2, token_part, 0)

        def write(i, c):
            return pltpu.make_async_copy(
                stage.at[i, pl.ds(c * share, share)],
                grads.at[c, me ^ lax.rem(i, parts), i // parts],
                sem_o.at[i, c],
            )

        def block(i, carry):
            m, half = i // 2, lax.rem(i, 2)
            column = pl.multiple_of(half * 2 * tall, 2 * tall)
            both = contract_rows(left[m // 2, :, pl.ds(column, 2 * tall)], right[m]).astype(LOW)
            for j in range(2):
                stage[2 * i + j] = both[j * tall : (j + 1) * tall]
                for c in range(size):
                    write(2 * i + j, c).start()
            return carry

        lax.fori_loop(0, count * parts // 2, block, 0)

        def drain(i, carry):
            for c in range(size):
                write(i, c).wait()
            return carry

        lax.fori_loop(0, count * parts, drain, 0)

        def drain_sums(i, carry):
            finish(sum_copies(i))
            return carry

        lax.fori_loop(0, parts // 2, drain_sums, 0)

    return pl.pallas_call(
        kernel,
        out_shape=(shaped((2, rows, model)),) * 4 + (shaped((size, parts, count, share, width)),),
        in_specs=[SMEM] + [ANY] * 9,
        out_specs=(ANY,) * 5,
        scratch_shapes=[pltpu.VMEM((2, total, model), LOW)]
        + [pltpu.VMEM((model, width), LOW)] * 3
        + [
            pltpu.VMEM((3, total, width), LOW),
            pltpu.VMEM((2, total, model), LOW),
            pltpu.VMEM((count * parts, tall, width), LOW),
        ]
        + [pltpu.SemaphoreType.DMA((4,))] * 2
        + [pltpu.SemaphoreType.DMA((size * parts,))] * 3
        + [pltpu.SemaphoreType.DMA((2, parts)), pltpu.SemaphoreType.DMA((count * parts, size))],
        compiler_params=PARAMS,
        name="ffn",
        cost_estimate=cost(37),
    )(where, *tokens, *pulled, weights)


def head_grads(where, lefts, rights, gains=None, small=0, later=()):
    count = len(lefts)
    model = lefts[0].shape[1]
    each = rights[0].shape[1]
    width = each * count
    size = where.shape[0] - 2
    parts = 4
    tall = model // parts
    share = tall // size
    pad = 16 if gains else 0
    gains = gains or []

    def kernel(where_ref, *refs):
        left_refs, right_refs, refs = refs[:count], refs[count : 2 * count], refs[2 * count :]
        *gain_refs, keep, send, stage, sems = refs[: len(gains)] + refs[len(gains) + len(later) :]
        me = where_ref[size + 1]
        here = where_ref[size]

        def block(part, carry):
            column = pl.multiple_of(part * tall, tall)
            for m in range(count):
                grads = contract_rows(
                    left_refs[m][:, pl.ds(column, tall)], right_refs[m][...]
                ).astype(LOW)
                for c in range(size):
                    stage[part * size + c, :share, m * each : (m + 1) * each] = grads[
                        c * share : (c + 1) * share
                    ]
            return carry

        lax.fori_loop(0, parts, block, 0)
        if pad:
            pairs = [gain[:, :HEAD] + gain[:, HEAD:] for gain in gain_refs[2:4]]
            for i in range(parts * size):
                pieces = [gain[:, i * share : (i + 1) * share] for gain in gain_refs[:2]]
                pieces += [pair[:, i * small : (i + 1) * small] for pair in pairs]
                row = jnp.concatenate(
                    [
                        jnp.concatenate(
                            [piece, jnp.zeros((1, 128 - piece.shape[1]), jnp.float32)], axis=1
                        )
                        for piece in pieces
                    ],
                    axis=1,
                )
                stage[i, share:] = jnp.broadcast_to(row, (pad, width)).astype(LOW)

        def each_copy(do):
            for part in range(parts):
                bit = me ^ part
                for odd, out in ((0, keep), (1, send)):

                    @pl.when(lax.rem(bit, 2) == odd)
                    def _():
                        for c in range(size):
                            step = lax.rem(here - c + size, size) if size <= LINE else c
                            i = part * size + c
                            do(
                                pltpu.make_async_copy(
                                    stage.at[i], out.at[bit // 2, step], sems.at[i]
                                )
                            )

        each_copy(lambda copy: copy.start())
        each_copy(lambda copy: copy.wait())

    return pl.pallas_call(
        kernel,
        out_shape=(shaped((2, size, share + pad, width)),) * 2,
        in_specs=[SMEM] + [VMEM] * (2 * count + len(gains)) + [ANY] * len(later),
        out_specs=(ANY,) * 2,
        scratch_shapes=[
            pltpu.VMEM((parts * size, share + pad, width), LOW),
            pltpu.SemaphoreType.DMA((parts * size,)),
        ],
        compiler_params=PARAMS,
        name="head_grads",
        cost_estimate=cost(3),
    )(where, *lefts, *rights, *gains, *later)


def flip(part, bit):
    size = lax.axis_size("fsdp")
    return lax.ppermute(part, "fsdp", [(i, i ^ bit) for i in range(size)])


def swap(part):
    return lax.ppermute(part, "tp", [(0, 1), (1, 0)])


def turn(part):
    size = lax.axis_size("ctx")
    return lax.ppermute(part, "ctx", [(i, (i + 1) % size) for i in range(size)])


def ctx_slots(part):
    size = lax.axis_size("ctx")
    if size > LINE:
        whole = lax.all_gather(part, "ctx", axis=0)
        return [whole[i] for i in range(size)]
    slots = [part]
    for _ in range(1, size):
        slots.append(turn(slots[-1]))
    return slots


def ctx_sum(terms, later=()):
    size = lax.axis_size("ctx")
    if size > LINE:
        return lax.psum_scatter(terms, "ctx", scatter_dimension=0, tiled=False).astype(jnp.float32)
    moving = terms[1]
    for step in range(1, size):
        total = turn(moving).astype(jnp.float32) + terms[(step + 1) % size].astype(jnp.float32)
        moving = total.astype(LOW)
        if later and step == 1:
            moving = collect([moving], later)[0]
    return total


def back_slots(part):
    size = lax.axis_size("ctx")
    if size > LINE:
        whole = lax.all_gather(part, "ctx", axis=0)
        return [whole[i] for i in range(size)]
    slots = [part]
    for step in range(1, size):
        slots.append(lax.ppermute(part, "ctx", [(i, i + step) for i in range(size - step)]))
    return slots


def back_sum(terms):
    size = lax.axis_size("ctx")
    if size > LINE:
        total = lax.psum_scatter(jnp.stack(terms), "ctx", scatter_dimension=0, tiled=False)
        return total.astype(jnp.float32), total
    parts = [terms[0]] + [
        lax.ppermute(terms[step], "ctx", [(i, i - step) for i in range(step, size)])
        for step in range(1, size)
    ]
    return sum(part.astype(jnp.float32) for part in parts), parts[1]


def group_tokens(part):
    across = flip(part, 2)
    return (part, flip(part, 1), across, flip(across, 1))


def chip_sum(keep, send):
    beside = flip(send, 1)
    far = keep[1].astype(jnp.float32) + beside[1].astype(jnp.float32)
    near = keep[0].astype(jnp.float32) + beside[0].astype(jnp.float32)
    return near, far.astype(LOW)


def pair_sum(near, far):
    return near + flip(far, 2).astype(jnp.float32)


def group_sum(keep, send):
    return pair_sum(*chip_sum(keep, send))


def gather_all(where, slots, share, later=(), pieces=1):
    own = collect(slots, later)
    across = flip(own, 2)
    both = flip(collect([own, across]), 1)
    return arrange(where, [own, both, across], share, pieces), across


def scatter_hidden(terms):
    size, parts, count, share, width = terms.shape
    own = lax.psum_scatter(terms.reshape(-1, width), "ctx", scatter_dimension=0, tiled=True)
    own = own.reshape(parts, count, share, width)
    return own, [own[0]] + [flip(own[bit], bit) for bit in range(1, parts)]


def body(
    inputs,
    cotangent,
    doc_bounds,
    attn_gain,
    w_query,
    w_key,
    w_value,
    w_output,
    query_gain,
    key_gain,
    ffn_gain,
    w_gate,
    w_up,
    w_down,
):
    parts = lax.axis_size("fsdp")
    size = lax.axis_size("ctx")
    tensor = lax.axis_size("tp")
    me = lax.axis_index("ctx")
    share = w_query.shape[0]
    model = share * parts * size
    width = HQ // tensor * HEAD
    kv_width = HK // tensor * HEAD
    small = query_gain.shape[0]
    shards = parts * size
    steps = jnp.arange(size, dtype=jnp.int32)
    slots_at = lax.rem(me - steps + size, size) if size <= LINE else steps
    where = jnp.concatenate(
        [slots_at, jnp.stack([me, lax.axis_index("fsdp")]).astype(jnp.int32)]
    )
    bounds = doc_bounds[0]

    split = split_columns(where, [w_gate, w_up, w_down.T])
    gains = jnp.concatenate([attn_gain, ffn_gain, query_gain, key_gain])
    pad = 16
    gain_rows = jnp.zeros((pad, 2 * kv_width), LOW).at[0, : gains.shape[0]].set(gains)
    kv_block = jnp.concatenate([jnp.concatenate([w_key, w_value], axis=1), gain_rows], axis=0)
    traded = [
        [part[0]] + [flip(part[bit], bit) for bit in range(1, parts)] for part in split
    ]
    kv_slots = ctx_slots(kv_block)
    head_slots = ctx_slots(jnp.concatenate([w_query, w_output.T], axis=1))
    (full_kv, gain_rows), kv_across = gather_all(where, kv_slots, share)
    (full_query, full_output), output_across = gather_all(
        where, head_slots, share, [kv_across], 2
    )
    weights = []
    for chunk in traded:
        block = collect(chunk, [kv_slots[-1], head_slots[2]])
        weights.append(
            lax.all_gather(
                block.reshape(-1, block.shape[-1]), "ctx", axis=0, tiled=True
            ).reshape(size, *block.shape)
        )
    pulled_all = group_tokens(collect([cotangent[0]], [output_across])[0])
    all_gains = gain_rows[:, 0].astype(jnp.float32)
    gain_attn = all_gains[:, :share].reshape(model)
    gain_ffn = all_gains[:, share : 2 * share].reshape(model)
    gain_query = jnp.tile(all_gains[:, 2 * share : 2 * share + small].reshape(HEAD), 2)[None]
    gain_key = jnp.tile(
        all_gains[:, 2 * share + small : 2 * share + 2 * small].reshape(HEAD), 2
    )[None]

    pulled = cotangent[0]

    tokens = inputs[0].astype(jnp.float32)
    rows = tokens.shape[0]
    cosine, sine = tables(me * rows, rows, bounds)
    first_inv = inverse_rms(tokens)
    normed = (tokens * first_inv * gain_attn).astype(LOW)
    keys_values = jnp.dot(normed, full_kv, preferred_element_type=jnp.float32)
    own_kv = prepare_keys(keys_values, gain_key, cosine, sine)
    kv = back_slots(own_kv)
    queries = jnp.dot(normed, full_query, preferred_element_type=jnp.float32)
    query_rot, mixed_low, mixed = attend(where, bounds, queries, kv, gain_query, cosine, sine)
    branch_part = contract_cols(mixed_low, full_output).astype(LOW)
    branch = branch_part.astype(jnp.float32) + swap(branch_part).astype(jnp.float32)
    hidden = tokens + branch
    second_inv = inverse_rms(hidden)
    hidden_normed = (hidden * second_inv * gain_ffn).astype(LOW)

    hidden_all = group_tokens(hidden_normed)
    keep, send, keep_out, send_out, terms = ffn(where, hidden_all, pulled_all, weights[0])
    near, far = chip_sum(keep, send)
    normed_part = pair_sum(near, far).astype(LOW)
    hidden_sum, traded_back = scatter_hidden(terms)
    grad_gate, grad_up, grad_down = join_columns(where, [traded_back])
    grad_down = grad_down.T
    grad_normed_ffn = normed_part.astype(jnp.float32) + swap(normed_part).astype(jnp.float32)

    ffn_gain_part = jnp.sum(grad_normed_ffn * hidden * second_inv, axis=0) * 0.5
    grad_hidden = pulled.astype(jnp.float32) + norm_back(
        hidden, second_inv, gain_ffn, grad_normed_ffn
    )
    grad_hidden_low = grad_hidden.astype(LOW)
    grad_mixed = jnp.dot(
        grad_hidden_low, full_output, preferred_element_type=jnp.float32
    ).astype(LOW)
    grad_query_low, *key_terms, query_gain_pair = attend_back(
        where, bounds, queries, query_rot, grad_mixed, mixed, kv, gain_query, cosine, sine,
        [terms],
    )
    near, far = chip_sum(
        *head_grads(where, [normed, grad_hidden_low], [grad_query_low, mixed_low])
    )
    heads_terms = pair_sum(near, far).astype(LOW)
    moved = collect(key_terms[1:], [far])
    own_terms, _ = back_sum([key_terms[0]] + [moved[i] for i in range(size - 1)])
    feed_part = group_sum(keep_out, collect([send_out], [grad_hidden_low])[0]).astype(LOW)
    feed = feed_part.astype(jnp.float32) + swap(feed_part).astype(jnp.float32)
    result = (hidden + feed).astype(LOW)[None]
    grad_kv_low, key_gain_pair = keys_back(
        keys_values,
        own_terms,
        gain_key,
        cosine,
        sine,
    )
    normed_low, attn_gain_part = normed_back(
        grad_query_low, grad_kv_low, full_query, full_kv, inputs[0], first_inv
    )
    near, far = chip_sum(
        *head_grads(
            where,
            [normed],
            [grad_kv_low],
            [attn_gain_part, ffn_gain_part[None], query_gain_pair, key_gain_pair],
            small,
        )
    )
    kv_sum = pair_sum(near, far).astype(LOW)
    own_kv = ctx_sum(collect([kv_sum], [hidden_sum])[0])
    heads_sum = ctx_sum(heads_terms, [hidden_sum])
    grad_query = heads_sum[:, :width]
    grad_output = heads_sum[:, width:].T
    grad_key = own_kv[:share, :kv_width]
    grad_value = own_kv[:share, kv_width:]
    normed_low = collect([normed_low], [far])[0]
    grad_normed = normed_low.astype(jnp.float32) + swap(normed_low).astype(jnp.float32)
    own_gains = own_kv[share].astype(LOW)
    grad_gains = own_gains.astype(jnp.float32) + swap(own_gains).astype(jnp.float32)
    grad_inputs = grad_hidden + norm_back(tokens, first_inv, gain_attn, grad_normed)
    return (
        result,
        grad_inputs[None],
        grad_gains[:share],
        grad_query,
        grad_key,
        grad_value,
        grad_output,
        grad_gains[256 : 256 + small],
        grad_gains[384 : 384 + small],
        grad_gains[128 : 128 + share],
        grad_gate,
        grad_up,
        grad_down,
    )


def solution(mesh):
    vector = P(("fsdp", "ctx"))
    columns = P(("fsdp", "ctx"), "tp")
    tall = P("tp", ("fsdp", "ctx"))
    act = P("fsdp", "ctx", None)
    return jax.shard_map(
        body,
        mesh=mesh,
        in_specs=(
            act,
            act,
            P("fsdp", None),
            vector,
            columns,
            columns,
            columns,
            tall,
            vector,
            vector,
            vector,
            columns,
            columns,
            tall,
        ),
        out_specs=(
            act,
            act,
            vector,
            columns,
            columns,
            columns,
            tall,
            vector,
            vector,
            vector,
            columns,
            columns,
            tall,
        ),
        check_vma=False,
    )
```
